256 devices in a mesh: ens: 8 (over z), space: 32 (over x, y, core).
Axes of the slice: x: 4, y: 4, z: 8, core: 2. Of those that a mesh axis runs over, the one named last changes fastest.
Arguments:
- initial_state: float32 [3, 256, 128, 1024], P(None, 'space', 'ens'), may hold values from -6 to 6
- depth_field: float32 [256, 1024], P('space'), may hold values from 0.5 to 1.5
- obs_index: int32 [256, 64], P('space', 'ens'), may hold values from 0 to 127
- obs_value: float32 [256, 64], P('space', 'ens'), may hold values from -6 to 6
- obs_var: float32 [256, 64], P('space', 'ens'), may hold values from 0.5 to 4
- cotangent: float32 [3, 256, 128, 1024], P(None, 'space', 'ens'), may hold values from -6 to 6
Outputs:
- state_grad: float32 [3, 256, 128, 1024], P(None, 'space', 'ens')
- depth_grad: float32 [256, 1024], P('space')
The draws below stay inside these ranges and needn't reach their ends.
Inputs may be any that keep to these rules, and one draw needn't show every extreme that they name: `obs_index`: observation j of a row lies in the block of columns j // 8; several observations may share a column.
All inputs are finite; a program needn't handle non-finite values.
Results may differ from the reference program's by a relative error of at most 0.00011.
Values sent between devices are 32-bit elements; how exact they have to be, the bound alone decides.
No kernel may reach another device: no remote copies, remote signals or barrier semaphores. Data moves between devices by JAX's collectives and lax.ppermute only.
A program may use at most 128 MiB of HBM per device.

```python
import math
import jax
import jax.numpy as jnp
from jax import lax

ENS = 128
NX = 1024
STEPS = 2
OBS_BLK = 8
NY = 256
COLS_BLK = 128
OBS = 64
N_ENS = 8


def touch_ends(drawn, rng, low, largest):
    longest = drawn.shape.index(max(drawn.shape))
    spots = []
    for shift in (0, 1):
        where = [jax.random.randint(jax.random.fold_in(rng, axis), (), 0, length) for axis, length in enumerate(drawn.shape)]
        where[longest] = (where[longest] + shift) % drawn.shape[longest]
        spots.append(tuple(where))
    return drawn.at[spots[0]].set(low).at[spots[1]].set(largest)


def block_levels(own_key, shape, shards, low, high):
    factor_of = 1.0
    for dim, parts in shards:
        steps = jax.random.uniform(jax.random.fold_in(jax.random.fold_in(own_key, 6), dim), (parts,), jnp.float32, low / len(shards), high / len(shards))
        factor_of = factor_of * jnp.repeat(jnp.exp(steps), shape[dim] // parts).reshape((-1,) + (1,) * (len(shape) - 1 - dim))
    return factor_of


def gaussian(stream_key, shape, spread, most, pieces=(), kind=jnp.bfloat16):
    gain = block_levels(stream_key, shape, pieces, -0.22, 0.18) if pieces else 1.0
    result = jax.random.normal(stream_key, shape, jnp.float32) * spread * gain
    return jnp.minimum(jnp.maximum(result, -most), most).astype(kind)


def setup_inputs(seed: int = 0) -> dict:
    splits = jax.random.split(jax.random.key(seed), 7)
    return {
        "initial_state": gaussian(splits[0], (3, NY, ENS, NX), 1.0, 6.0, ((1, 32), (2, 8)), jnp.float32),
        "depth_field": jnp.clip(0.5 + 1.0 * jax.random.uniform(splits[1], (NY, NX), jnp.float32) ** block_levels(splits[1], (NY, NX), ((0, 32),), -0.2, 0.2), 0.5, 1.5),
        "obs_index": touch_ends(jax.random.randint(splits[2], (NY, OBS), 0, COLS_BLK), jax.random.fold_in(splits[2], 1), 0, COLS_BLK - 1).astype(jnp.int32),
        "obs_value": gaussian(splits[3], (NY, OBS), 1.0, 6.0, ((0, 32), (1, 8)), jnp.float32),
        "obs_var": jnp.clip(jnp.exp(math.log(4.0) - 2.0794415 * jax.random.uniform(splits[4], (NY, OBS), jnp.float32) ** block_levels(splits[4], (NY, OBS), ((0, 32), (1, 8)), -0.2, 0.2)), 0.5, 4.0),
        "cotangent": gaussian(splits[5], (3, NY, ENS, NX), 1.0, 6.0, ((1, 32), (2, 8)), jnp.float32),
    }


WAVE_COEF = 0.3
SPIN_COEF = 0.1

def diff_cols(field):
    return jnp.roll(field, -1, axis=2) - jnp.roll(field, 1, axis=2)

def diff_rows(field):
    padded = jnp.pad(field, ((1, 1), (0, 0), (0, 0)))
    return padded[2:] - padded[:-2]

def advance(surface_height, eastward_velocity, northward_velocity, depth_rows):
    new_east = eastward_velocity - WAVE_COEF * diff_cols(surface_height) + SPIN_COEF * northward_velocity
    new_north = northward_velocity - WAVE_COEF * diff_rows(surface_height) - SPIN_COEF * eastward_velocity
    new_height = surface_height - WAVE_COEF * (diff_cols(depth_rows * new_east) + diff_rows(depth_rows * new_north))
    return (new_height, new_east, new_north)

def transform(gram_sum, proj_sum):
    ensemble_members = gram_sum.shape[0]
    identity = jnp.eye(ensemble_members, dtype=gram_sum.dtype)
    lower_factor = jnp.linalg.cholesky(identity + gram_sum)
    halfway = lax.linalg.triangular_solve(lower_factor, proj_sum[:, None], left_side=True, lower=True)
    mean_weights = lax.linalg.triangular_solve(lower_factor, halfway, left_side=True, lower=True, transpose_a=True)
    inverse_lower = lax.linalg.triangular_solve(lower_factor, identity, left_side=True, lower=True)
    return mean_weights / math.sqrt(ensemble_members - 1) + inverse_lower.T

def reference(initial_state, depth_field, obs_index, obs_value, obs_var, cotangent):
    upper_bound = lax.Precision.HIGHEST
    offsets = jnp.arange(OBS, dtype=jnp.int32) // OBS_BLK * (NX // N_ENS)
    columns = (obs_index + offsets[None, :]).astype(jnp.int32)
    picker = jnp.broadcast_to(columns[:, None, :], (NY, ENS, OBS))

    def forward(state, depth):
        depth_rows = depth[:, None, :]
        surface_height, eastward_velocity, northward_velocity = (state[0], state[1], state[2])
        for section_num in range(STEPS):
            surface_height, eastward_velocity, northward_velocity = advance(surface_height, eastward_velocity, northward_velocity, depth_rows)
        predicted_state = jnp.stack([surface_height, eastward_velocity, northward_velocity])
        ensemble_average = lax.optimization_barrier(jnp.mean(predicted_state, axis=2, keepdims=True))
        member_deviation = predicted_state - ensemble_average
        measured_values = jnp.take_along_axis(surface_height, picker, axis=2)
        obs_mean = lax.optimization_barrier(jnp.mean(measured_values, axis=1))
        obs_scale = 1.0 / jnp.sqrt(obs_var * (ENS - 1))
        scaled = (measured_values - obs_mean[:, None, :]) * obs_scale[:, None, :]
        innovation = (obs_value - obs_mean) / jnp.sqrt(obs_var)
        gram = jnp.einsum('rko,rmo->km', scaled, scaled, precision=upper_bound)
        proj = jnp.einsum('rko,ro->k', scaled, innovation, precision=upper_bound)
        weights = transform(gram, proj)
        return ensemble_average + jnp.einsum('frkc,km->frmc', member_deviation, weights, precision=upper_bound)
    unused, pullback = jax.vjp(forward, initial_state, depth_field)
    state_grad, depth_grad = pullback(cotangent)
    return (state_grad, depth_grad)
```

```python
import math

import jax
import jax.numpy as jnp
from jax import lax
from jax.sharding import PartitionSpec as P

WAVE_COEF = 0.3
SPIN_COEF = 0.1
HALO = 4
HIGHEST = lax.Precision.HIGHEST


def gathered(block, axis):
    count = lax.axis_size(axis)
    copies = jnp.broadcast_to(block[None], (count,) + block.shape)
    return lax.all_to_all(copies, axis, 0, 0, tiled=False)


def summed(block, axis):
    count = lax.axis_size(axis)
    distance = 1
    while distance < count:
        block = block + lax.ppermute(block, axis, [(i, i ^ distance) for i in range(count)])
        distance *= 2
    return block


def from_above(rows_sent):
    count = lax.axis_size("space")
    return lax.ppermute(rows_sent, "space", [(i, i + 1) for i in range(count - 1)])


def from_below(rows_sent):
    count = lax.axis_size("space")
    return lax.ppermute(rows_sent, "space", [(i + 1, i) for i in range(count - 1)])


def cols(field):
    return jnp.roll(field, -1, axis=-1) - jnp.roll(field, 1, axis=-1)


def rows(field):
    pad = [(1, 1)] + [(0, 0)] * (field.ndim - 1)
    padded = jnp.pad(field, pad)
    return padded[2:] - padded[:-2]


def per_device(initial_state, depth_field, obs_index, obs_value, obs_var, cotangent):
    groups = lax.axis_size("ens")
    ens_place = lax.axis_index("ens")
    space_place = lax.axis_index("space")
    own_rows, own_members, width = initial_state.shape[1:]
    members = own_members * groups
    block_cols = width // groups
    tall = own_rows + 2 * HALO
    inner = slice(HALO, HALO + own_rows)
    band = own_rows * lax.axis_size("space")

    all_cot = lax.all_gather(cotangent, "ens")

    def edge(first, take):
        parts = [
            initial_state[f, take(n)].reshape(n * own_members, width)
            for f, n in ((0, HALO), (1, HALO - 1), (2, HALO - 1))
        ]
        return jnp.concatenate(parts + [depth_field[take(HALO)]])

    tail = edge(0, lambda n: slice(own_rows - n, own_rows))
    head = edge(0, lambda n: slice(0, n))
    above, below = from_above(tail), from_below(head)
    packed = jnp.stack([obs_index.astype(jnp.float32), obs_value, obs_var])
    obs_all = gathered(packed, "ens")
    obs_all = obs_all.transpose(1, 2, 0, 3).reshape(3, own_rows, -1)

    def split(edge_rows):
        at = 0
        out = []
        for n in (HALO, HALO - 1, HALO - 1):
            out.append(edge_rows[at : at + n * own_members].reshape(n, own_members, width))
            at += n * own_members
        return out, edge_rows[at:]

    up, depth_up = split(above)
    down, depth_down = split(below)
    padded = []
    for f in range(3):
        n = up[f].shape[0]
        blank = [(HALO - n, 0), (0, 0), (0, 0)]
        blank_low = [(0, HALO - n), (0, 0), (0, 0)]
        padded.append(
            jnp.concatenate(
                [jnp.pad(up[f], blank), initial_state[f], jnp.pad(down[f], blank_low)]
            )
        )
    depth = jnp.concatenate([depth_up, depth_field, depth_down])[:, None, :]
    row_number = space_place * own_rows - HALO + jnp.arange(tall)
    inside = ((row_number >= 0) & (row_number < band)).astype(jnp.float32)[:, None, None]

    height, east, north = padded
    record = []
    for _ in range(2):
        new_east = east - WAVE_COEF * cols(height) + SPIN_COEF * north
        new_north = north - WAVE_COEF * rows(height) - SPIN_COEF * east
        height = (
            height - WAVE_COEF * (cols(depth * new_east) + rows(depth * new_north))
        ) * inside
        east, north = new_east, new_north
        record.append((east[inner], north[inner]))
    forecast = [height[inner], east[inner], north[inner]]

    index, value, var = obs_all[0], obs_all[1], obs_all[2]
    observations = index.shape[1]

    def selector(index_rows):
        n = index_rows.shape[0]
        offset = (jnp.arange(observations) // (observations // groups)) * block_cols
        place = index_rows.astype(jnp.int32) + offset[None]
        return (
            place[:, :, None] == lax.broadcasted_iota(jnp.int32, (n, observations, width), 2)
        ).astype(jnp.float32)

    observed = jnp.einsum("rmc,roc->rmo", forecast[0], selector(index), precision=HIGHEST)
    observed = gathered(observed, "ens")
    observed = observed.transpose(1, 0, 2, 3).reshape(own_rows, members, observations)
    obs_mean = jnp.mean(observed, axis=1)
    inv_sd = 1.0 / jnp.sqrt(var)
    obs_scale = 1.0 / jnp.sqrt(var * (members - 1))
    scaled = (observed - obs_mean[:, None, :]) * obs_scale[:, None, :]
    innovation = (value - obs_mean) * inv_sd
    extra = jnp.stack([innovation, obs_scale, inv_sd, index], axis=1)
    obs_pack = jnp.concatenate([scaled, extra], axis=1)
    obs_tall = jnp.concatenate(
        [from_above(obs_pack[own_rows - HALO :]), obs_pack, from_below(obs_pack[:HALO])]
    )
    flat = jnp.concatenate([scaled, innovation[:, None, :]], axis=1)
    gram_proj = summed(jnp.einsum("rko,rmo->km", flat, scaled, precision=HIGHEST), "space")
    gram, proj = gram_proj[:members], gram_proj[members]

    identity = jnp.eye(members, dtype=jnp.float32)
    lower = jnp.linalg.cholesky(identity + gram)
    inverse = lax.linalg.triangular_solve(lower, identity, left_side=True, lower=True)
    root = math.sqrt(members - 1)
    mean_weights = jnp.dot(
        inverse.T, jnp.dot(inverse, proj, precision=HIGHEST), precision=HIGHEST
    )
    weights = mean_weights[:, None] / root + inverse.T
    mixing = weights - jnp.mean(weights, axis=0, keepdims=True) + 1.0 / members
    first = ens_place * own_members
    own_mixing = lax.dynamic_slice_in_dim(mixing, first, own_members, 0)

    cot = all_cot.transpose(1, 2, 0, 3, 4).reshape(3, own_rows, members, width)
    own_forecast = jnp.stack(forecast)
    own_cross = jnp.einsum("frkc,frmc->km", own_forecast, cot, precision=HIGHEST)
    adjoint = jnp.einsum("km,frmc->frkc", own_mixing, cot, precision=HIGHEST)
    cross = jnp.sum(gathered(own_cross, "space"), axis=0)
    cross = gathered(cross, "ens").reshape(members, members)
    cross = cross - jnp.mean(cross, axis=0, keepdims=True)

    adjoint_up = from_above(adjoint[:, own_rows - HALO :])
    adjoint_down = from_below(adjoint[:, :HALO])
    adjoint_tall = jnp.concatenate([adjoint_up, adjoint, adjoint_down], axis=1)

    mean_grad = jnp.sum(cross, axis=1) / root
    proj_grad = jnp.dot(
        inverse.T, jnp.dot(inverse, mean_grad, precision=HIGHEST), precision=HIGHEST
    )
    product = jnp.dot(cross.T, inverse.T, precision=HIGHEST)
    strict = jnp.tril(product, -1)
    mirrored = strict + strict.T + identity * product
    inner_grad = jnp.dot(
        inverse.T, jnp.dot(mirrored, inverse, precision=HIGHEST), precision=HIGHEST
    )
    outer = proj_grad[:, None] * mean_weights[None, :]
    gram_grad = -(inner_grad + outer + outer.T)
    both = jnp.concatenate([gram_grad, proj_grad[:, None]], axis=1)
    both = both - jnp.mean(both, axis=0, keepdims=True)
    own_both = lax.dynamic_slice_in_dim(both, first, own_members, 0)

    obs_grad = jnp.einsum(
        "km,rmo->rko", own_both, obs_tall[:, : members + 1], precision=HIGHEST
    )
    innov_grad = jnp.einsum("m,rmo->ro", proj_grad, obs_tall[:, :members], precision=HIGHEST)
    obs_grad = (
        obs_grad * obs_tall[:, members + 1][:, None, :]
        - (innov_grad * obs_tall[:, members + 2] / members)[:, None, :]
    )
    seen = jnp.einsum(
        "rko,roc->rkc", obs_grad, selector(obs_tall[:, members + 3]), precision=HIGHEST
    )
    height, east, north = adjoint_tall[0] + seen, adjoint_tall[1], adjoint_tall[2]
    depth_grad = 0.0
    for step in (1, 0):
        new_east, new_north = record[step]
        across = WAVE_COEF * cols(height)
        along = WAVE_COEF * rows(height)
        depth_grad = depth_grad + jnp.sum(
            new_east * across[inner] + new_north * along[inner], axis=1
        )
        east_total = east + depth * across
        north_total = north + depth * along
        height = (height + WAVE_COEF * (cols(east_total) + rows(north_total))) * inside
        east = east_total - SPIN_COEF * north_total
        north = north_total + SPIN_COEF * east_total
    state_grad = jnp.stack([height[inner], east[inner], north[inner]])
    depth_grad = jnp.sum(gathered(depth_grad, "ens"), axis=0)
    return (state_grad, depth_grad)


def solution(mesh):
    in_specs = (
        P(None, "space", "ens", None),
        P("space", None),
        P("space", "ens"),
        P("space", "ens"),
        P("space", "ens"),
        P(None, "space", "ens", None),
    )
    out_specs = (P(None, "space", "ens", None), P("space", None))
    return jax.shard_map(
        per_device, mesh=mesh, in_specs=in_specs, out_specs=out_specs, check_vma=False
    )
```

```python
import functools
import math

import jax
import jax.numpy as jnp
from jax import lax
from jax.experimental import pallas as pl
from jax.experimental.pallas import tpu as pltpu
from jax.sharding import PartitionSpec as P

WAVE_COEF = 0.3
SPIN_COEF = 0.1
HALO = 4
HIGHEST = lax.Precision.HIGHEST


def gathered(block, axis):
    count = lax.axis_size(axis)
    copies = jnp.broadcast_to(block[None], (count,) + block.shape)
    return lax.all_to_all(copies, axis, 0, 0, tiled=False)


def summed(block, axis):
    count = lax.axis_size(axis)
    distance = 1
    while distance < count:
        block = block + lax.ppermute(block, axis, [(i, i ^ distance) for i in range(count)])
        distance *= 2
    return block


def from_above(rows_sent):
    count = lax.axis_size("space")
    return lax.ppermute(rows_sent, "space", [(i, i + 1) for i in range(count - 1)])


def from_below(rows_sent):
    count = lax.axis_size("space")
    return lax.ppermute(rows_sent, "space", [(i + 1, i) for i in range(count - 1)])


def cols(field):
    return jnp.roll(field, -1, axis=-1) - jnp.roll(field, 1, axis=-1)


def rows(field):
    pad = [(1, 1)] + [(0, 0)] * (field.ndim - 1)
    padded = jnp.pad(field, pad)
    return padded[2:] - padded[:-2]


def owner_of(owners_ref, place, size, count):
    owner = jnp.zeros_like(place)
    for i in range(count):
        owner = jnp.where(place // size == i, owners_ref[i], owner)
    return owner


def cross_kernel(own_members, halves, owners_ref, state_ref, *refs):
    blocks, out_ref = refs[:-1], refs[-1]
    height = blocks[0].shape[1]
    total = jnp.zeros(out_ref.shape, jnp.float32)
    row = lax.broadcasted_iota(jnp.int32, (height, height), 0) // own_members
    col = lax.broadcasted_iota(jnp.int32, (height, height), 1) // own_members
    same = row == col
    member = lax.broadcasted_iota(jnp.int32, (height, out_ref.shape[1]), 0) % own_members
    place = lax.broadcasted_iota(jnp.int32, (height, out_ref.shape[1]), 1)
    for i, (half, block) in enumerate(zip(halves, blocks)):
        products = jnp.zeros((height, height), jnp.float32)
        for f in range(block.shape[0]):
            products += lax.dot_general(
                state_ref[f, half * height : (half + 1) * height],
                block[f],
                (((1,), (1,)), ((), ())),
                precision=HIGHEST,
                preferred_element_type=jnp.float32,
            )
        products = jnp.where(same, products, 0.0)
        products = products.reshape(height // own_members, own_members, height).sum(0)
        put = (place == member + owners_ref[i] * own_members).astype(jnp.float32)
        total += jnp.dot(products, put, precision=HIGHEST, preferred_element_type=jnp.float32)
    out_ref[...] = total


def cross_of(owners, halves, state, blocks):
    members, own_members = state.shape[1], 16
    size = sum(b.size for b in blocks) * 4 + state.size * 4
    return pl.pallas_call(
        functools.partial(cross_kernel, own_members, halves),
        out_shape=jax.ShapeDtypeStruct((own_members, members), jnp.float32),
        in_specs=[pl.BlockSpec(memory_space=pltpu.SMEM)]
        + [pl.BlockSpec(memory_space=pltpu.VMEM)] * (1 + len(blocks)),
        out_specs=pl.BlockSpec(memory_space=pltpu.VMEM),
        compiler_params=pltpu.CompilerParams(vmem_limit_bytes=48 * 2**20),
        cost_estimate=pl.CostEstimate(flops=size * 400, bytes_accessed=size, transcendentals=0),
        name="cross",
    )(owners, state, *blocks)


def mix_kernel(own_members, halves, started, owners_ref, mixing_ref, *refs):
    if started:
        begun_ref, refs = refs[0], refs[1:]
    blocks, out_ref = refs[:-1], refs[-1]
    height = blocks[0].shape[1]
    members = mixing_ref.shape[1]
    tiled = jnp.concatenate([mixing_ref[...]] * (height // own_members), axis=0)
    for half in range(2):
        mine = [i for i, h in enumerate(halves) if h == half]
        depth = len(mine) * height
        place = lax.broadcasted_iota(jnp.int32, (members, depth), 0)
        item = lax.broadcasted_iota(jnp.int32, (members, depth), 1)
        owner = jnp.zeros_like(item)
        for n, i in enumerate(mine):
            owner = jnp.where(item // height == n, owners_ref[i], owner)
        put = (place == owner * own_members + item % own_members).astype(jnp.float32)
        spread = jnp.dot(tiled, put, precision=HIGHEST, preferred_element_type=jnp.float32)
        row = lax.broadcasted_iota(jnp.int32, (height, depth), 0) // own_members
        col = lax.broadcasted_iota(jnp.int32, (height, depth), 1) % height // own_members
        spread = jnp.where(row == col, spread, 0.0)
        for f in range(out_ref.shape[0]):
            stacked = jnp.concatenate([blocks[i][f] for i in mine], axis=0)
            part = jnp.dot(
                spread, stacked, precision=HIGHEST, preferred_element_type=jnp.float32
            )
            at = slice(half * height, (half + 1) * height)
            if started:
                part = part + begun_ref[f, at]
            out_ref[f, at] = part


def mix_of(owners, halves, mixing, blocks, begun=None):
    own_members, members = mixing.shape
    shape = (blocks[0].shape[0], members, blocks[0].shape[2])
    started = begun is not None
    size = sum(b.size for b in blocks) * 4 + 2 * 4 * math.prod(shape)
    return pl.pallas_call(
        functools.partial(mix_kernel, own_members, halves, started),
        out_shape=jax.ShapeDtypeStruct(shape, jnp.float32),
        in_specs=[pl.BlockSpec(memory_space=pltpu.SMEM)]
        + [pl.BlockSpec(memory_space=pltpu.VMEM)] * (1 + started + len(blocks)),
        out_specs=pl.BlockSpec(memory_space=pltpu.VMEM),
        compiler_params=pltpu.CompilerParams(vmem_limit_bytes=48 * 2**20),
        cost_estimate=pl.CostEstimate(flops=size * 400, bytes_accessed=size, transcendentals=0),
        name="mix",
    )(owners, mixing, *([begun] if started else []), *blocks)


def per_device(initial_state, depth_field, obs_index, obs_value, obs_var, cotangent):
    groups = lax.axis_size("ens")
    ens_place = lax.axis_index("ens")
    space_place = lax.axis_index("space")
    own_rows, own_members, width = initial_state.shape[1:]
    members = own_members * groups
    block_cols = width // groups
    tall = own_rows + 2 * HALO
    inner = slice(HALO, HALO + own_rows)
    band = own_rows * lax.axis_size("space")

    fields = cotangent.shape[0]
    middle = own_rows // 2
    ring_up = [(i, (i + 1) % groups) for i in range(groups)]
    ring_down = [(i, (i - 1) % groups) for i in range(groups)]
    rising = [
        cotangent[:, h * middle : (h + 1) * middle].reshape(fields, middle * own_members, width)
        for h in range(2)
    ]
    falling = list(rising)
    ring = {0: list(rising)}
    for step in range(1, groups // 2):
        for h in range(2):
            rising[h] = lax.ppermute(rising[h], "ens", ring_up)
            falling[1 - h] = lax.ppermute(falling[1 - h], "ens", ring_down)
        ring[-step], ring[step] = list(rising), list(falling)
    ring[groups // 2] = [
        lax.ppermute(rising[0], "ens", ring_up),
        lax.ppermute(falling[1], "ens", ring_down),
    ]

    def edge(first, take):
        parts = [
            initial_state[f, take(n)].reshape(n * own_members, width)
            for f, n in ((0, HALO), (1, HALO - 1), (2, HALO - 1))
        ]
        return jnp.concatenate(parts + [depth_field[take(HALO)]])

    tail = edge(0, lambda n: slice(own_rows - n, own_rows))
    head = edge(0, lambda n: slice(0, n))
    above, below = from_above(tail), from_below(head)
    packed = jnp.stack([obs_index.astype(jnp.float32), obs_value, obs_var])
    obs_all = gathered(packed, "ens")
    obs_all = obs_all.transpose(1, 2, 0, 3).reshape(3, own_rows, -1)

    def split(edge_rows):
        at = 0
        out = []
        for n in (HALO, HALO - 1, HALO - 1):
            out.append(edge_rows[at : at + n * own_members].reshape(n, own_members, width))
            at += n * own_members
        return out, edge_rows[at:]

    up, depth_up = split(above)
    down, depth_down = split(below)
    padded = []
    for f in range(3):
        n = up[f].shape[0]
        blank = [(HALO - n, 0), (0, 0), (0, 0)]
        blank_low = [(0, HALO - n), (0, 0), (0, 0)]
        padded.append(
            jnp.concatenate(
                [jnp.pad(up[f], blank), initial_state[f], jnp.pad(down[f], blank_low)]
            )
        )
    depth = jnp.concatenate([depth_up, depth_field, depth_down])[:, None, :]
    row_number = space_place * own_rows - HALO + jnp.arange(tall)
    inside = ((row_number >= 0) & (row_number < band)).astype(jnp.float32)[:, None, None]

    height, east, north = padded
    record = []
    for _ in range(2):
        new_east = east - WAVE_COEF * cols(height) + SPIN_COEF * north
        new_north = north - WAVE_COEF * rows(height) - SPIN_COEF * east
        height = (
            height - WAVE_COEF * (cols(depth * new_east) + rows(depth * new_north))
        ) * inside
        east, north = new_east, new_north
        record.append((east[inner], north[inner]))
    forecast = [height[inner], east[inner], north[inner]]

    index, value, var = obs_all[0], obs_all[1], obs_all[2]
    observations = index.shape[1]

    def selector(index_rows):
        n = index_rows.shape[0]
        offset = (jnp.arange(observations) // (observations // groups)) * block_cols
        place = index_rows.astype(jnp.int32) + offset[None]
        return (
            place[:, :, None] == lax.broadcasted_iota(jnp.int32, (n, observations, width), 2)
        ).astype(jnp.float32)

    observed = jnp.einsum("rmc,roc->rmo", forecast[0], selector(index), precision=HIGHEST)
    observed = gathered(observed, "ens")
    observed = observed.transpose(1, 0, 2, 3).reshape(own_rows, members, observations)
    obs_mean = jnp.mean(observed, axis=1)
    inv_sd = 1.0 / jnp.sqrt(var)
    obs_scale = 1.0 / jnp.sqrt(var * (members - 1))
    scaled = (observed - obs_mean[:, None, :]) * obs_scale[:, None, :]
    innovation = (value - obs_mean) * inv_sd
    extra = jnp.stack([innovation, obs_scale, inv_sd, index], axis=1)
    obs_pack = jnp.concatenate([scaled, extra], axis=1)
    obs_tall = jnp.concatenate(
        [from_above(obs_pack[own_rows - HALO :]), obs_pack, from_below(obs_pack[:HALO])]
    )
    flat = jnp.concatenate([scaled, innovation[:, None, :]], axis=1)
    gram_proj = summed(jnp.einsum("rko,rmo->km", flat, scaled, precision=HIGHEST), "space")
    gram, proj = gram_proj[:members], gram_proj[members]

    identity = jnp.eye(members, dtype=jnp.float32)
    lower = jnp.linalg.cholesky(identity + gram)
    inverse = lax.linalg.triangular_solve(lower, identity, left_side=True, lower=True)
    root = math.sqrt(members - 1)
    mean_weights = jnp.dot(
        inverse.T, jnp.dot(inverse, proj, precision=HIGHEST), precision=HIGHEST
    )
    weights = mean_weights[:, None] / root + inverse.T
    mixing = weights - jnp.mean(weights, axis=0, keepdims=True) + 1.0 / members
    first = ens_place * own_members
    own_mixing = lax.dynamic_slice_in_dim(mixing, first, own_members, 0)

    own_forecast = jnp.stack(forecast).reshape(fields, own_rows * own_members, width)

    def blocks_at(distances):
        owners = jnp.stack([(ens_place + d) % groups for d in distances for _ in range(2)])
        halves = tuple(h for _ in distances for h in range(2))
        return owners.astype(jnp.int32), halves, [ring[d][h] for d in distances for h in range(2)]

    early, late, last = (0, -1, 1, -2, 2), (-3, 3), (4,)
    own_cross = 0.0
    for distances in (early, late, last):
        owners, halves, blocks = blocks_at(distances)
        own_cross = own_cross + cross_of(owners, halves, own_forecast, blocks)
    owners, halves, blocks = blocks_at(early + late)
    adjoint = mix_of(owners, halves, own_mixing, blocks)
    owners, halves, blocks = blocks_at(last)
    adjoint = mix_of(owners, halves, own_mixing, blocks, adjoint)
    adjoint = adjoint.reshape(fields, own_rows, own_members, width)
    cross = jnp.sum(gathered(own_cross, "space"), axis=0)
    cross = gathered(cross, "ens").reshape(members, members)
    cross = cross - jnp.mean(cross, axis=0, keepdims=True)

    adjoint_up = from_above(adjoint[:, own_rows - HALO :])
    adjoint_down = from_below(adjoint[:, :HALO])
    adjoint_tall = jnp.concatenate([adjoint_up, adjoint, adjoint_down], axis=1)

    mean_grad = jnp.sum(cross, axis=1) / root
    proj_grad = jnp.dot(
        inverse.T, jnp.dot(inverse, mean_grad, precision=HIGHEST), precision=HIGHEST
    )
    product = jnp.dot(cross.T, inverse.T, precision=HIGHEST)
    strict = jnp.tril(product, -1)
    mirrored = strict + strict.T + identity * product
    inner_grad = jnp.dot(
        inverse.T, jnp.dot(mirrored, inverse, precision=HIGHEST), precision=HIGHEST
    )
    outer = proj_grad[:, None] * mean_weights[None, :]
    gram_grad = -(inner_grad + outer + outer.T)
    both = jnp.concatenate([gram_grad, proj_grad[:, None]], axis=1)
    both = both - jnp.mean(both, axis=0, keepdims=True)
    own_both = lax.dynamic_slice_in_dim(both, first, own_members, 0)

    obs_grad = jnp.einsum(
        "km,rmo->rko", own_both, obs_tall[:, : members + 1], precision=HIGHEST
    )
    innov_grad = jnp.einsum("m,rmo->ro", proj_grad, obs_tall[:, :members], precision=HIGHEST)
    obs_grad = (
        obs_grad * obs_tall[:, members + 1][:, None, :]
        - (innov_grad * obs_tall[:, members + 2] / members)[:, None, :]
    )
    seen = jnp.einsum(
        "rko,roc->rkc", obs_grad, selector(obs_tall[:, members + 3]), precision=HIGHEST
    )
    height, east, north = adjoint_tall[0] + seen, adjoint_tall[1], adjoint_tall[2]
    depth_grad = 0.0
    for step in (1, 0):
        new_east, new_north = record[step]
        across = WAVE_COEF * cols(height)
        along = WAVE_COEF * rows(height)
        depth_grad = depth_grad + jnp.sum(
            new_east * across[inner] + new_north * along[inner], axis=1
        )
        east_total = east + depth * across
        north_total = north + depth * along
        height = (height + WAVE_COEF * (cols(east_total) + rows(north_total))) * inside
        east = east_total - SPIN_COEF * north_total
        north = north_total + SPIN_COEF * east_total
    state_grad = jnp.stack([height[inner], east[inner], north[inner]])
    depth_grad = jnp.sum(gathered(depth_grad, "ens"), axis=0)
    return (state_grad, depth_grad)


def solution(mesh):
    in_specs = (
        P(None, "space", "ens", None),
        P("space", None),
        P("space", "ens"),
        P("space", "ens"),
        P("space", "ens"),
        P(None, "space", "ens", None),
    )
    out_specs = (P(None, "space", "ens", None), P("space", None))
    return jax.shard_map(
        per_device, mesh=mesh, in_specs=in_specs, out_specs=out_specs, check_vma=False
    )
```

```python
import functools
import math

import jax
import jax.numpy as jnp
from jax import lax
from jax.experimental import pallas as pl
from jax.experimental.pallas import tpu as pltpu
from jax.sharding import PartitionSpec as P

WAVE_COEF = 0.3
SPIN_COEF = 0.1
HALO = 4
HIGHEST = lax.Precision.HIGHEST
STATE_EDGE = ((0, 4), (1, 3), (2, 3))
ADJOINT_EDGE = ((0, 4), (2, 3), (1, 2))
VMEM = pl.BlockSpec(memory_space=pltpu.VMEM)
SMEM = pl.BlockSpec(memory_space=pltpu.SMEM)


def kernel_call(body, outs, ins, scratch=(), flops=0, name=None):
    moved = sum(math.prod(o) for o in outs) * 4 + sum(i.size for i in ins) * 4
    result = pl.pallas_call(
        body,
        out_shape=[jax.ShapeDtypeStruct(o, jnp.float32) for o in outs],
        in_specs=[SMEM if i.ndim == 1 else VMEM for i in ins],
        out_specs=[VMEM] * len(outs),
        scratch_shapes=[pltpu.VMEM(s, jnp.float32) for s in scratch],
        compiler_params=pltpu.CompilerParams(vmem_limit_bytes=40 * 2**20),
        cost_estimate=pl.CostEstimate(flops=flops, bytes_accessed=moved, transcendentals=0),
        name=name,
    )(*ins)
    return result


def exchanged(blocks):
    return lax.all_to_all(blocks, "ens", 0, 0, tiled=False)


def gathered(block, axis):
    count = lax.axis_size(axis)
    copies = jnp.broadcast_to(block[None], (count,) + block.shape)
    return lax.all_to_all(copies, axis, 0, 0, tiled=False)


def summed(block, axis):
    count = lax.axis_size(axis)
    distance = 1
    while distance < count:
        block = block + lax.ppermute(block, axis, [(i, i ^ distance) for i in range(count)])
        distance *= 2
    return block


def from_above(rows_sent):
    count = lax.axis_size("space")
    return lax.ppermute(rows_sent, "space", [(i, i + 1) for i in range(count - 1)])


def from_below(rows_sent):
    count = lax.axis_size("space")
    return lax.ppermute(rows_sent, "space", [(i + 1, i) for i in range(count - 1)])


def cols(field):
    width = field.shape[1]
    return pltpu.roll(field, width - 1, 1) - pltpu.roll(field, 1, 1)


def dot(a, b, dims=((1,), (0,))):
    return lax.dot_general(
        a, b, (dims, ((), ())), precision=HIGHEST, preferred_element_type=jnp.float32
    )


def spread_kernel(in_ref, out_ref):
    out_ref[0] = in_ref[...]


def by_columns(field_rows, groups):
    n, width = field_rows.shape
    part = width // groups
    return pl.pallas_call(
        spread_kernel,
        grid=(groups,),
        out_shape=jax.ShapeDtypeStruct((groups, n, part), jnp.float32),
        in_specs=[pl.BlockSpec((n, part), lambda j: (0, j))],
        out_specs=pl.BlockSpec((1, n, part), lambda j: (j, 0, 0)),
        name="spread",
    )(field_rows)


def padded_rows(edges, size, own_row, above, below):
    start = {}
    at = 0
    for f, n in edges:
        start[f] = (at, n)
        at += n * size

    def row(f, p, own_rows):
        first, n = start[f]
        if p < HALO:
            return above(first + (p - (HALO - n)) * size)
        if p < HALO + own_rows:
            return own_row(f, p - HALO)
        return below(first + (p - HALO - own_rows) * size)

    return row, at


def forward_kernel(
    inside_ref, state_ref, depth_ref, above_ref, below_ref,
    spread_ref, height_ref, east1_ref, north1_ref, east2_ref, north2_ref,
    e1, n1, h1, n2, depth,
):
    own, size, width = height_ref.shape
    groups = spread_ref.shape[0]
    part = width // groups
    low, high = HALO, HALO + own
    row, at = padded_rows(
        STATE_EDGE,
        size,
        lambda f, r: state_ref[f, r],
        lambda i: above_ref[i : i + size],
        lambda i: below_ref[i : i + size],
    )
    row = functools.partial(row, own_rows=own)
    depth[:HALO] = above_ref[at : at + HALO]
    depth[low:high] = depth_ref[...]
    depth[high:] = below_ref[at : at + HALO]

    def d(p):
        return depth[p : p + 1]

    for p in range(low - 3, high + 3):
        n1[p] = row(2, p) - WAVE_COEF * (row(0, p + 1) - row(0, p - 1)) - SPIN_COEF * row(1, p)
    for p in range(low - 2, high + 2):
        new_east = row(1, p) - WAVE_COEF * cols(row(0, p)) + SPIN_COEF * row(2, p)
        e1[p] = new_east
        flow = cols(d(p) * new_east) + (d(p + 1) * n1[p + 1] - d(p - 1) * n1[p - 1])
        h1[p] = (row(0, p) - WAVE_COEF * flow) * inside_ref[p]
    for p in range(low - 1, high + 1):
        n2[p] = n1[p] - WAVE_COEF * (h1[p + 1] - h1[p - 1]) - SPIN_COEF * e1[p]
    for p in range(low, high):
        r = p - low
        new_east = e1[p] - WAVE_COEF * cols(h1[p]) + SPIN_COEF * n1[p]
        flow = cols(d(p) * new_east) + (d(p + 1) * n2[p + 1] - d(p - 1) * n2[p - 1])
        new_height = h1[p] - WAVE_COEF * flow
        new_north = n2[p]
        height_ref[r] = new_height
        east1_ref[r] = e1[p]
        north1_ref[r] = n1[p]
        east2_ref[r] = new_east
        north2_ref[r] = new_north
        for f, field in enumerate((new_height, new_east, new_north)):
            for j in range(groups):
                spread_ref[j, f * own + r] = field[:, j * part : (j + 1) * part]


def backward_kernel(
    inside_ref, back_ref, above_ref, below_ref, seen_ref, depth_ref,
    east1_ref, north1_ref, east2_ref, north2_ref,
    depth_grad_ref, state_grad_ref,
    h2, h1, e1, n1, nt,
):
    own, size, width = east1_ref.shape
    groups = back_ref.shape[0]
    low, high = HALO, HALO + own
    wide = lambda ref, at: jnp.concatenate([ref[j, at] for j in range(groups)], axis=1)
    row, _ = padded_rows(
        ADJOINT_EDGE,
        size,
        lambda f, r: wide(back_ref, f * own + r),
        lambda i: wide(above_ref, slice(i, i + size)),
        lambda i: wide(below_ref, slice(i, i + size)),
    )
    row = functools.partial(row, own_rows=own)

    def d(p):
        return depth_ref[p : p + 1]

    for p in range(0, high + HALO):
        h2[p] = row(0, p) + seen_ref[p]
    for p in range(low - 3, high + 3):
        along = WAVE_COEF * (h2[p + 1] - h2[p - 1])
        nt[p] = row(2, p) + d(p) * along
    for p in range(low - 2, high + 2):
        across = WAVE_COEF * cols(h2[p])
        total = row(1, p) + d(p) * across
        h1[p] = (h2[p] + WAVE_COEF * (cols(total) + (nt[p + 1] - nt[p - 1]))) * inside_ref[p]
        if low - 1 <= p < high + 1:
            n1[p] = nt[p] + SPIN_COEF * total
        if low <= p < high:
            r = p - low
            e1[p] = total - SPIN_COEF * nt[p]
            along = WAVE_COEF * (h2[p + 1] - h2[p - 1])
            depth_grad_ref[r : r + 1] = jnp.sum(
                east2_ref[r] * across + north2_ref[r] * along, axis=0, keepdims=True
            )
    for p in range(low - 1, high + 1):
        along = WAVE_COEF * (h1[p + 1] - h1[p - 1])
        nt[p] = n1[p] + d(p) * along
    for p in range(low, high):
        r = p - low
        across = WAVE_COEF * cols(h1[p])
        along = WAVE_COEF * (h1[p + 1] - h1[p - 1])
        total = e1[p] + d(p) * across
        depth_grad_ref[r : r + 1] += jnp.sum(
            east1_ref[r] * across + north1_ref[r] * along, axis=0, keepdims=True
        )
        state_grad_ref[0, r] = h1[p] + WAVE_COEF * (cols(total) + (nt[p + 1] - nt[p - 1]))
        state_grad_ref[1, r] = total - SPIN_COEF * nt[p]
        state_grad_ref[2, r] = nt[p] + SPIN_COEF * total


def gram_kernel(observed_ref, params_ref, scaled_ref, extra_ref, gram_ref):
    groups, pairs, size, lanes = observed_ref.shape
    members = groups * size
    gram = jnp.zeros((members, members), jnp.float32)
    proj = jnp.zeros((8, members), jnp.float32)
    for q in range(pairs):
        seen = observed_ref[:, q].reshape(members, lanes)
        mean = jnp.mean(seen, axis=0, keepdims=True)
        value, var = params_ref[1, q : q + 1], params_ref[2, q : q + 1]
        inv_sd = 1.0 / jnp.sqrt(var)
        obs_scale = 1.0 / jnp.sqrt(var * (members - 1))
        scaled = (seen - mean) * obs_scale
        innovation = (value - mean) * inv_sd
        scaled_ref[q] = scaled
        extra_ref[q] = jnp.concatenate(
            [innovation, obs_scale, inv_sd, params_ref[0, q : q + 1]]
            + [jnp.zeros((4, lanes), jnp.float32)],
            axis=0,
        )
        gram += dot(scaled, scaled, ((1,), (1,)))
        lead = jnp.concatenate([innovation, jnp.zeros((7, lanes), jnp.float32)], axis=0)
        proj += dot(lead, scaled, ((1,), (1,)))
    gram_ref[:members] = gram
    gram_ref[members:] = proj


def factor_kernel(gram_ref, inverse_ref, mixing_ref, mean_ref):
    members = inverse_ref.shape[0]
    step = 8
    blocks = members // step
    lane = lax.broadcasted_iota(jnp.int32, (step, members), 1)
    sub = lax.broadcasted_iota(jnp.int32, (step, members), 0)
    left, right = [], []
    for i in range(blocks):
        eye = (lane == sub + i * step).astype(jnp.float32)
        left.append(gram_ref[i * step : (i + 1) * step] + eye)
        right.append(eye)
    for k in range(members):
        i0, s = divmod(k, step)
        top_left, top_right = left[i0][s : s + 1], right[i0][s : s + 1]
        pivot = top_left[:, k : k + 1]
        inverse_ref[k : k + 1] = top_right * (1.0 / jnp.sqrt(pivot))
        if k == members - 1:
            break
        turned = 1.0 / pivot
        scaled_left, scaled_right = top_left * turned, top_right * turned
        for i in range(i0, blocks):
            factor = left[i][:, k : k + 1]
            if i == i0:
                factor = jnp.where(sub[:, :1] > s, factor, 0.0)
            left[i] = left[i] - factor * scaled_left
            right[i] = right[i] - factor * scaled_right
    inverse = inverse_ref[...]
    proj = gram_ref[members:]
    mean = dot(dot(proj, inverse, ((1,), (1,))), inverse)
    mean_ref[...] = mean
    root = math.sqrt(members - 1)
    turned = inverse + mean[:1] / root
    turned = turned - jnp.mean(turned, axis=1, keepdims=True) + 1.0 / members
    mixing_ref[...] = turned.T


def cross_kernel(state_ref, cot_ref, out_ref):
    groups, sites, size, part = state_ref.shape
    members = groups * size
    total = jnp.zeros((members, members), jnp.float32)
    for at in range(0, sites, 2):
        pick = lambda ref: jnp.concatenate(
            [ref[:, at + i].reshape(members, part) for i in range(2)], axis=1
        )
        total += dot(pick(state_ref), pick(cot_ref), ((1,), (1,)))
    out_ref[...] = total


def mix_kernel(mixing_ref, cot_ref, out_ref):
    groups, sites, size, part = cot_ref.shape
    members = groups * size
    mixing = mixing_ref[...]
    for at in range(0, sites, 2):
        both = jnp.concatenate(
            [cot_ref[:, at + i].reshape(members, part) for i in range(2)], axis=1
        )
        mixed = dot(mixing, both)
        for i in range(2):
            out_ref[:, at + i] = mixed[:, i * part : (i + 1) * part].reshape(groups, size, part)


def per_device(initial_state, depth_field, obs_index, obs_value, obs_var, cotangent):
    groups = lax.axis_size("ens")
    ens_place = lax.axis_index("ens")
    space_place = lax.axis_index("space")
    fields, own_rows, own_members, width = initial_state.shape
    members = own_members * groups
    block_cols = width // groups
    tall = own_rows + 2 * HALO
    band = own_rows * lax.axis_size("space")
    sites = fields * own_rows
    half = own_rows // 2

    def edge(take):
        parts = [initial_state[f, take(n)].reshape(-1, width) for f, n in STATE_EDGE]
        return jnp.concatenate(parts + [depth_field[take(HALO)]])

    tail = edge(lambda n: slice(own_rows - n, own_rows))
    head = edge(lambda n: slice(0, n))
    above, below = from_above(tail), from_below(head)
    cot_in, _, _ = lax.optimization_barrier((cotangent, tail, head))
    cot_out = by_columns(cot_in.reshape(-1, width), groups)
    cot = exchanged(cot_out).reshape(groups, sites, own_members, block_cols)

    packed = jnp.stack([obs_index.astype(jnp.float32), obs_value, obs_var])
    params = gathered(packed, "ens").transpose(1, 2, 0, 3).reshape(3, own_rows, -1)
    observations = params.shape[2]

    row_number = space_place * own_rows - HALO + jnp.arange(tall)
    inside = ((row_number >= 0) & (row_number < band)).astype(jnp.float32)
    shape = (own_rows, own_members, width)
    padded = (tall, own_members, width)
    spread, height, east1, north1, east2, north2 = kernel_call(
        forward_kernel,
        [(groups, sites, own_members, block_cols)] + [shape] * 5,
        [inside, initial_state, depth_field, above, below],
        [padded] * 4 + [(tall, width)],
        flops=10**8,
        name="forward",
    )

    def selector(index_rows):
        n = index_rows.shape[0]
        offset = (jnp.arange(observations) // (observations // groups)) * block_cols
        place = index_rows.astype(jnp.int32) + offset[None]
        return (
            place[:, :, None] == lax.broadcasted_iota(jnp.int32, (n, observations, width), 2)
        ).astype(jnp.float32)

    def paired(a):
        return jnp.concatenate([a[..., :half, :, :], a[..., half:, :, :]], axis=-1)

    def unpaired(a):
        return jnp.concatenate([a[..., :observations], a[..., observations:]], axis=0)

    observed = jnp.einsum("rmc,roc->rmo", height, selector(params[0]), precision=HIGHEST)
    observed = gathered(paired(observed), "ens")
    spread, _ = lax.optimization_barrier((spread, observed))
    forecast = exchanged(spread)
    params_paired = jnp.concatenate([params[:, :half], params[:, half:]], axis=-1)
    scaled, extra, gram = kernel_call(
        gram_kernel,
        [(half, members, 2 * observations), (half, 8, 2 * observations), (members + 8, members)],
        [observed, params_paired],
        flops=4 * 2 * 6 * members**3,
        name="gram",
    )
    gram = summed(gram, "space")
    inverse, mixing, mean_weights = kernel_call(
        factor_kernel,
        [(members, members), (members, members), (8, members)],
        [gram],
        flops=10**9,
        name="factor",
    )
    mean_weights = mean_weights[0]
    scaled, extra, _ = lax.optimization_barrier((scaled, extra, gram))
    obs_pack = unpaired(jnp.concatenate([scaled, extra], axis=1))
    obs_tall = jnp.concatenate(
        [from_above(obs_pack[own_rows - HALO :]), obs_pack, from_below(obs_pack[:HALO])]
    )

    (own_cross,) = kernel_call(
        cross_kernel, [(members, members)], [forecast, cot], flops=10**10, name="cross"
    )
    (mixed,) = kernel_call(
        mix_kernel, [cot.shape], [mixing, cot], flops=10**10, name="mix"
    )
    back = exchanged(mixed)

    cross = jnp.sum(exchanged(own_cross.reshape(groups, own_members, members)), axis=0)
    cross = jnp.sum(gathered(cross, "space"), axis=0)
    cross = gathered(cross, "ens").reshape(members, members)
    cross = cross - jnp.mean(cross, axis=0, keepdims=True)
    identity = jnp.eye(members, dtype=jnp.float32)
    mean_grad = jnp.sum(cross, axis=1) / math.sqrt(members - 1)
    proj_grad = jnp.dot(
        inverse.T, jnp.dot(inverse, mean_grad, precision=HIGHEST), precision=HIGHEST
    )
    product = jnp.dot(cross.T, inverse.T, precision=HIGHEST)
    strict = jnp.tril(product, -1)
    mirrored = strict + strict.T + identity * product
    inner_grad = jnp.dot(
        inverse.T, jnp.dot(mirrored, inverse, precision=HIGHEST), precision=HIGHEST
    )
    outer = proj_grad[:, None] * mean_weights[None, :]
    gram_grad = -(inner_grad + outer + outer.T)
    both = jnp.concatenate([gram_grad, proj_grad[:, None]], axis=1)
    both = both - jnp.mean(both, axis=0, keepdims=True)
    own_both = lax.dynamic_slice_in_dim(both, ens_place * own_members, own_members, 0)

    obs_grad = jnp.einsum(
        "km,rmo->rko", own_both, obs_tall[:, : members + 1], precision=HIGHEST
    )
    innov_grad = jnp.einsum("m,rmo->ro", proj_grad, obs_tall[:, :members], precision=HIGHEST)
    obs_grad = (
        obs_grad * obs_tall[:, members + 1][:, None, :]
        - (innov_grad * obs_tall[:, members + 2] / members)[:, None, :]
    )
    seen = jnp.einsum(
        "rko,roc->rkc", obs_grad, selector(obs_tall[:, members + 3]), precision=HIGHEST
    )

    by_field = back.reshape(groups, fields, own_rows, own_members, block_cols)

    def adjoint_edge(take):
        parts = [
            by_field[:, f, take(n)].reshape(groups, -1, block_cols) for f, n in ADJOINT_EDGE
        ]
        return jnp.concatenate(parts, axis=1)

    adjoint_above = from_above(adjoint_edge(lambda n: slice(own_rows - n, own_rows)))
    adjoint_below = from_below(adjoint_edge(lambda n: slice(0, n)))
    depth_tall = jnp.concatenate([above[-HALO:], depth_field, below[-HALO:]])
    depth_grad, state_grad = kernel_call(
        backward_kernel,
        [(own_rows, width), (fields,) + shape],
        [
            inside, back, adjoint_above, adjoint_below, seen, depth_tall,
            east1, north1, east2, north2,
        ],
        [padded] * 5,
        flops=10**8,
        name="backward",
    )
    depth_grad = jnp.sum(gathered(depth_grad, "ens"), axis=0)
    return (state_grad, depth_grad)


def solution(mesh):
    in_specs = (
        P(None, "space", "ens", None),
        P("space", None),
        P("space", "ens"),
        P("space", "ens"),
        P("space", "ens"),
        P(None, "space", "ens", None),
    )
    out_specs = (P(None, "space", "ens", None), P("space", None))
    return jax.shard_map(
        per_device, mesh=mesh, in_specs=in_specs, out_specs=out_specs, check_vma=False
    )
```

```python
import functools
import math

import jax
import jax.numpy as jnp
from jax import lax
from jax.experimental import pallas as pl
from jax.experimental.pallas import tpu as pltpu
from jax.sharding import PartitionSpec as P

WAVE_COEF = 0.3
SPIN_COEF = 0.1
HALO = 4
HIGHEST = lax.Precision.HIGHEST
STATE_EDGE = ((0, 4), (1, 3), (2, 3))
ADJOINT_EDGE = ((0, 4), (2, 3), (1, 2))
VMEM = pl.BlockSpec(memory_space=pltpu.VMEM)
HBM = pl.BlockSpec(memory_space=pltpu.HBM)
SMEM = pl.BlockSpec(memory_space=pltpu.SMEM)


def kernel_call(body, outs, ins, scratch=(), copies=0, far_outs=(), far_ins=(), flops=0, name=None):
    moved = sum(math.prod(o) for o in outs) * 4 + sum(i.size for i in ins) * 4
    near = lambda i, a: SMEM if a.ndim == 1 else HBM if i in far_ins else VMEM
    made = lambda i, o: (pltpu.HBM if i in far_outs else jax.ShapeDtypeStruct)(o, jnp.float32)
    ins = [
        pltpu.with_memory_space_constraint(a, pltpu.HBM) if i in far_ins else a
        for i, a in enumerate(ins)
    ]
    return pl.pallas_call(
        body,
        out_shape=[made(i, o) for i, o in enumerate(outs)],
        in_specs=[near(i, a) for i, a in enumerate(ins)],
        out_specs=[HBM if i in far_outs else VMEM for i in range(len(outs))],
        scratch_shapes=[pltpu.VMEM(s, jnp.float32) for s in scratch]
        + ([pltpu.SemaphoreType.DMA((copies,))] if copies else []),
        compiler_params=pltpu.CompilerParams(vmem_limit_bytes=20 * 2**20),
        cost_estimate=pl.CostEstimate(flops=flops, bytes_accessed=moved, transcendentals=0),
        name=name,
    )(*ins)


def exchanged(blocks):
    return lax.all_to_all(blocks, "ens", 0, 0, tiled=False)


def gathered(block, axis):
    count = lax.axis_size(axis)
    copies = jnp.broadcast_to(block[None], (count,) + block.shape)
    return lax.all_to_all(copies, axis, 0, 0, tiled=False)


def turned(block, distance):
    count = lax.axis_size("ens")
    return lax.ppermute(block, "ens", [(i, (i + distance) % count) for i in range(count)])


def summed(block, axis):
    count = lax.axis_size(axis)
    distance = 1
    while distance < count:
        block = block + lax.ppermute(block, axis, [(i, i ^ distance) for i in range(count)])
        distance *= 2
    return block


def from_above(rows_sent):
    count = lax.axis_size("space")
    return lax.ppermute(rows_sent, "space", [(i, i + 1) for i in range(count - 1)])


def from_below(rows_sent):
    count = lax.axis_size("space")
    return lax.ppermute(rows_sent, "space", [(i + 1, i) for i in range(count - 1)])


def cols(field):
    width = field.shape[1]
    return pltpu.roll(field, width - 1, 1) - pltpu.roll(field, 1, 1)


def dot(a, b, dims=((1,), (0,))):
    return lax.dot_general(
        a, b, (dims, ((), ())), precision=HIGHEST, preferred_element_type=jnp.float32
    )


def prepare_kernel(
    state_ref, depth_ref, cot_ref, tail_ref, head_ref, out_ref, tail, head, cot, spread, sems
):
    own = state_ref.shape[1]
    groups, sites, part = spread.shape
    copies = []

    def send(source, target):
        copies.append(pltpu.make_async_copy(source, target, sems.at[len(copies)]))
        copies[-1].start()

    fields = len(STATE_EDGE)
    piece = sites // fields
    at = 0
    for f, n in STATE_EDGE:
        send(state_ref.at[f, pl.ds(own - n, n)], tail.at[pl.ds(at, n)])
        send(state_ref.at[f, pl.ds(0, n)], head.at[pl.ds(at, n)])
        at += n
    for edge in (tail, head):
        send(depth_ref, edge.at[at, pl.ds(0, own)])
    for f in range(fields):
        send(cot_ref.at[pl.ds(f * piece, piece)], cot.at[pl.ds(f * piece, piece)])
    for copy in copies[: 2 * fields + 2]:
        copy.wait()
    tail[at, own:] = tail[at, :own]
    head[at, own:] = head[at, :own]
    send(tail, tail_ref)
    send(head, head_ref)
    for f in range(fields):
        copies[2 * fields + 2 + f].wait()
        for j in range(groups):
            spread[j, f * piece : (f + 1) * piece] = cot[
                f * piece : (f + 1) * piece, j * part : (j + 1) * part
            ]
        send(spread.at[:, pl.ds(f * piece, piece)], out_ref.at[:, pl.ds(f * piece, piece)])
    for copy in copies[3 * fields + 2 :]:
        copy.wait()


def padded_rows(edges, size, own_row, above, below):
    start = {}
    at = 0
    for f, n in edges:
        start[f] = (at, n)
        at += n * size

    def row(f, p, own_rows):
        first, n = start[f]
        if p < HALO:
            return above(first + (p - (HALO - n)) * size)
        if p < HALO + own_rows:
            return own_row(f, p - HALO)
        return below(first + (p - HALO - own_rows) * size)

    return row, at


def forward_kernel(
    inside_ref, state_ref, depth_ref, above_ref, below_ref, index_ref,
    out_ref, observed_ref, east1_ref, north1_ref, east2_ref, north2_ref,
    e1, n1, h1, n2, h2, e2, depth, spread, sems,
):
    own, size, width = east1_ref.shape
    groups = spread.shape[0]
    part = width // groups
    low, high = HALO, HALO + own
    row, at = padded_rows(
        STATE_EDGE,
        1,
        lambda f, r: state_ref[f, r],
        lambda i: above_ref[i],
        lambda i: below_ref[i],
    )
    row = functools.partial(row, own_rows=own)
    depth[:HALO] = above_ref[at, own - HALO : own]
    depth[low:high] = depth_ref[...]
    depth[high:] = below_ref[at, :HALO]

    def d(p):
        return depth[p : p + 1]

    for p in range(low - 3, high + 3):
        n1[p] = row(2, p) - WAVE_COEF * (row(0, p + 1) - row(0, p - 1)) - SPIN_COEF * row(1, p)
    for p in range(low - 2, high + 2):
        new_east = row(1, p) - WAVE_COEF * cols(row(0, p)) + SPIN_COEF * row(2, p)
        e1[p] = new_east
        flow = cols(d(p) * new_east) + (d(p + 1) * n1[p + 1] - d(p - 1) * n1[p - 1])
        h1[p] = (row(0, p) - WAVE_COEF * flow) * inside_ref[p]
    copies = []

    def send(source, target):
        copies.append(pltpu.make_async_copy(source, target, sems.at[len(copies)]))
        copies[-1].start()

    send(e1.at[pl.ds(low, own)], east1_ref)
    send(n1.at[pl.ds(low, own)], north1_ref)
    for p in range(low - 1, high + 1):
        n2[p] = n1[p] - WAVE_COEF * (h1[p + 1] - h1[p - 1]) - SPIN_COEF * e1[p]
    for p in range(low, high):
        r = p - low
        new_east = e1[p] - WAVE_COEF * cols(h1[p]) + SPIN_COEF * n1[p]
        flow = cols(d(p) * new_east) + (d(p + 1) * n2[p + 1] - d(p - 1) * n2[p - 1])
        new_height = h1[p] - WAVE_COEF * flow
        new_north = n2[p]
        h2[r] = new_height
        e2[r] = new_east
        for f, field in enumerate((new_height, new_east, new_north)):
            for j in range(groups):
                spread[j, f * own + r] = field[:, j * part : (j + 1) * part]
    send(spread, out_ref)
    send(e2, east2_ref)
    send(n2.at[pl.ds(low, own)], north2_ref)
    pairs, lanes = index_ref.shape
    many = 2 * groups * size
    sub = lax.broadcasted_iota(jnp.int32, (part, lanes), 0)
    source = lax.broadcasted_iota(jnp.int32, (many, lanes), 0) // size
    target = lax.broadcasted_iota(jnp.int32, (many, lanes), 1) // (lanes // 2 // groups)
    for q in range(pairs):
        index = index_ref[q : q + 1].astype(jnp.int32)
        hit = (sub == index).astype(jnp.float32)
        stacked = jnp.concatenate(
            [h2[q + h * pairs, :, j * part : (j + 1) * part] for h in range(2) for j in range(groups)],
            axis=0,
        )
        seen = jnp.where(source == target, dot(stacked, hit), 0.0)
        observed_ref[q] = seen.reshape(2 * groups, size, lanes).sum(0)
    for copy in copies:
        copy.wait()


def backward_kernel(
    inside_ref, back_ref, above_ref, below_ref, seen_ref, depth_ref,
    east1_ref, north1_ref, east2_ref, north2_ref,
    depth_grad_ref, state_grad_ref,
    h2, h1, e1, n1, nt,
):
    own, size, width = east1_ref.shape
    groups = back_ref.shape[0]
    low, high = HALO, HALO + own
    wide = lambda ref, at: jnp.concatenate([ref[j, at] for j in range(groups)], axis=1)
    row, _ = padded_rows(
        ADJOINT_EDGE,
        size,
        lambda f, r: wide(back_ref, f * own + r),
        lambda i: wide(above_ref, slice(i, i + size)),
        lambda i: wide(below_ref, slice(i, i + size)),
    )
    row = functools.partial(row, own_rows=own)

    def d(p):
        return depth_ref[p : p + 1]

    for p in range(0, high + HALO):
        h2[p] = row(0, p) + seen_ref[p]
    for p in range(low - 3, high + 3):
        along = WAVE_COEF * (h2[p + 1] - h2[p - 1])
        nt[p] = row(2, p) + d(p) * along
    for p in range(low - 2, high + 2):
        across = WAVE_COEF * cols(h2[p])
        total = row(1, p) + d(p) * across
        h1[p] = (h2[p] + WAVE_COEF * (cols(total) + (nt[p + 1] - nt[p - 1]))) * inside_ref[p]
        if low - 1 <= p < high + 1:
            n1[p] = nt[p] + SPIN_COEF * total
        if low <= p < high:
            r = p - low
            e1[p] = total - SPIN_COEF * nt[p]
            along = WAVE_COEF * (h2[p + 1] - h2[p - 1])
            depth_grad_ref[r : r + 1] = jnp.sum(
                east2_ref[r] * across + north2_ref[r] * along, axis=0, keepdims=True
            )
    for p in range(low - 1, high + 1):
        along = WAVE_COEF * (h1[p + 1] - h1[p - 1])
        nt[p] = n1[p] + d(p) * along
    for p in range(low, high):
        r = p - low
        across = WAVE_COEF * cols(h1[p])
        along = WAVE_COEF * (h1[p + 1] - h1[p - 1])
        total = e1[p] + d(p) * across
        depth_grad_ref[r : r + 1] += jnp.sum(
            east1_ref[r] * across + north1_ref[r] * along, axis=0, keepdims=True
        )
        state_grad_ref[0, r] = h1[p] + WAVE_COEF * (cols(total) + (nt[p + 1] - nt[p - 1]))
        state_grad_ref[1, r] = total - SPIN_COEF * nt[p]
        state_grad_ref[2, r] = nt[p] + SPIN_COEF * total


def gram_kernel(place_ref, params_ref, *refs):
    *observed_refs, scaled_ref, extra_ref, gram_ref, observed_ref, sems = refs
    groups, pairs, size, lanes = observed_ref.shape
    copies = []
    for d, ref in enumerate(observed_refs):
        there = observed_ref.at[lax.rem(place_ref[0] + groups - d, groups)]
        copies.append(pltpu.make_async_copy(ref, there, sems.at[d]))
        copies[-1].start()
    for copy in copies:
        copy.wait()
    members = groups * size
    gram = jnp.zeros((members, members), jnp.float32)
    proj = jnp.zeros((8, members), jnp.float32)
    for q in range(pairs):
        seen = observed_ref[:, q].reshape(members, lanes)
        mean = jnp.mean(seen, axis=0, keepdims=True)
        value, var = params_ref[1, q : q + 1], params_ref[2, q : q + 1]
        inv_sd = 1.0 / jnp.sqrt(var)
        obs_scale = 1.0 / jnp.sqrt(var * (members - 1))
        scaled = (seen - mean) * obs_scale
        innovation = (value - mean) * inv_sd
        scaled_ref[q] = scaled
        extra_ref[q] = jnp.concatenate(
            [innovation, obs_scale, inv_sd, params_ref[0, q : q + 1]]
            + [jnp.zeros((4, lanes), jnp.float32)],
            axis=0,
        )
        gram += dot(scaled, scaled, ((1,), (1,)))
        lead = jnp.concatenate([innovation, jnp.zeros((7, lanes), jnp.float32)], axis=0)
        proj += dot(lead, scaled, ((1,), (1,)))
    gram_ref[:members] = gram
    gram_ref[members:] = proj


def factor_kernel(gram_ref, inverse_ref, mixing_ref, mean_ref):
    members = inverse_ref.shape[0]
    step = 8
    blocks = members // step
    lane = lax.broadcasted_iota(jnp.int32, (step, members), 1)
    sub = lax.broadcasted_iota(jnp.int32, (step, members), 0)
    left, right = [], []
    for i in range(blocks):
        eye = (lane == sub + i * step).astype(jnp.float32)
        left.append(gram_ref[i * step : (i + 1) * step] + eye)
        right.append(eye)
    for k in range(members):
        i0, s = divmod(k, step)
        top_left, top_right = left[i0][s : s + 1], right[i0][s : s + 1]
        pivot = top_left[:, k : k + 1]
        inverse_ref[k : k + 1] = top_right * (1.0 / jnp.sqrt(pivot))
        if k == members - 1:
            break
        turned = 1.0 / pivot
        scaled_left, scaled_right = top_left * turned, top_right * turned
        for i in range(i0, blocks):
            factor = left[i][:, k : k + 1]
            if i == i0:
                factor = jnp.where(sub[:, :1] > s, factor, 0.0)
            left[i] = left[i] - factor * scaled_left
            right[i] = right[i] - factor * scaled_right
    inverse = inverse_ref[...]
    proj = gram_ref[members:]
    mean = dot(dot(proj, inverse, ((1,), (1,))), inverse)
    mean_ref[...] = mean
    root = math.sqrt(members - 1)
    turned = inverse + mean[:1] / root
    turned = turned - jnp.mean(turned, axis=1, keepdims=True) + 1.0 / members
    mixing_ref[...] = turned.T


def pullback_kernel(place_ref, cross_ref, inverse_ref, mean_ref, *refs):
    *parts, grad, column = refs
    members = inverse_ref.shape[0]
    groups = len(parts)
    size = members // groups
    inverse = inverse_ref[...]
    cross = cross_ref[...]
    cross = cross - jnp.mean(cross, axis=0, keepdims=True)
    first = lax.broadcasted_iota(jnp.int32, (8, members), 0) == 0
    ones = jnp.where(first, 1.0, 0.0)
    mean_grad = dot(ones, cross, ((1,), (1,))) / math.sqrt(members - 1)
    proj_grad = dot(dot(mean_grad, inverse, ((1,), (1,))), inverse)
    product = dot(inverse, cross)
    row = lax.broadcasted_iota(jnp.int32, (members, members), 0)
    col = lax.broadcasted_iota(jnp.int32, (members, members), 1)
    upper = jnp.where(row < col, product, 0.0)
    mirrored = jnp.where(row == col, product, 0.0) + upper + upper.T
    inner_grad = dot(inverse.T, dot(mirrored, inverse))
    every = jnp.broadcast_to(proj_grad[:1], (members, members)).T
    outer = every * mean_ref[:1]
    gram_grad = -(inner_grad + outer + outer.T)
    grad[...] = gram_grad - jnp.mean(gram_grad, axis=0, keepdims=True)
    column[...] = every - jnp.mean(every, axis=0, keepdims=True)
    for d, part in enumerate(parts):
        there = lax.rem(place_ref[0] + d, groups)
        rows_there = pl.ds(pl.multiple_of(there * size, size), size)
        part[:size] = grad[rows_there]
        part[size : 2 * size] = column[rows_there]
        part[2 * size :] = proj_grad


def observe_kernel(*refs):
    *part_refs, obs_ref, seen_ref, parts, sems = refs
    tall, size, width = seen_ref.shape
    pairs, high, lanes = obs_ref.shape
    members = high - 8
    part = lanes
    groups = width // part
    copies = []
    for d, ref in enumerate(part_refs):
        copies.append(pltpu.make_async_copy(ref, parts.at[d], sems.at[d]))
        copies[-1].start()
    for copy in copies:
        copy.wait()
    whole = parts[...].sum(0)
    own_grad, own_proj, proj_grad = whole[:size], whole[size : 2 * size], whole[2 * size :]
    lane = lax.broadcasted_iota(jnp.int32, (size, lanes), 1)
    sub = lax.broadcasted_iota(jnp.int32, (part, lanes), 0)
    block = lanes // 2 // groups
    for t in range(pairs):
        scaled = obs_ref[t, :members]
        innovation, obs_scale, inv_sd, index = (
            obs_ref[t, members + i : members + i + 1] for i in range(4)
        )
        obs_grad = (dot(own_grad, scaled) + own_proj * innovation) * obs_scale
        obs_grad = obs_grad - dot(proj_grad, scaled)[:1] * inv_sd / members
        apart = jnp.concatenate(
            [jnp.where(lane // block == i, obs_grad, 0.0) for i in range(2 * groups)], axis=0
        )
        hit = (sub == index.astype(jnp.int32)).astype(jnp.float32)
        put = dot(apart, hit, ((1,), (1,)))
        for h in range(2):
            for j in range(groups):
                at = (h * groups + j) * size
                seen_ref[t + h * pairs, :, j * part : (j + 1) * part] = put[at : at + size]


def cross_kernel(state_ref, cot_ref, out_ref):
    groups, sites, size, part = state_ref.shape
    members = groups * size
    total = jnp.zeros((members, members), jnp.float32)
    for at in range(0, sites, 2):
        pick = lambda ref: jnp.concatenate(
            [ref[:, at + i].reshape(members, part) for i in range(2)], axis=1
        )
        total += dot(pick(state_ref), pick(cot_ref), ((1,), (1,)))
    out_ref[...] = total


def mix_kernel(mixing_ref, cot_ref, out_ref, mixed_ref, sems):
    groups, sites, size, part = cot_ref.shape
    members = groups * size
    mixing = mixing_ref[...]
    copies = []
    pieces = sems.shape[0]
    for at in range(0, sites, 2):
        both = jnp.concatenate(
            [cot_ref[:, at + i].reshape(members, part) for i in range(2)], axis=1
        )
        mixed = dot(mixing, both)
        for i in range(2):
            mixed_ref[:, at + i] = mixed[:, i * part : (i + 1) * part].reshape(groups, size, part)
        if (at + 2) % (sites // pieces) == 0:
            done = pl.ds(at + 2 - sites // pieces, sites // pieces)
            copies.append(
                pltpu.make_async_copy(
                    mixed_ref.at[:, done], out_ref.at[:, done], sems.at[len(copies)]
                )
            )
            copies[-1].start()
    for copy in copies:
        copy.wait()


def per_device(initial_state, depth_field, obs_index, obs_value, obs_var, cotangent):
    groups = lax.axis_size("ens")
    ens_place = lax.axis_index("ens")
    space_place = lax.axis_index("space")
    fields, own_rows, own_members, width = initial_state.shape
    members = own_members * groups
    block_cols = width // groups
    tall = own_rows + 2 * HALO
    band = own_rows * lax.axis_size("space")
    sites = fields * own_rows
    half = own_rows // 2

    packed = jnp.concatenate([obs_index.T.astype(jnp.float32), obs_value.T, obs_var.T])
    packed = jnp.pad(packed, ((0, 0), (0, block_cols - packed.shape[1])))
    params = gathered(packed, "ens")
    edge = (sum(n for _, n in STATE_EDGE) + 1, own_members, width)
    blocks = (groups, sites * own_members, block_cols)
    tail, head, cot_out = kernel_call(
        prepare_kernel,
        [edge, edge, blocks],
        [initial_state, depth_field, cotangent.reshape(-1, width)],
        [edge, edge, (sites * own_members, width), blocks],
        copies=4 * fields + 4,
        far_outs=(0, 1, 2),
        far_ins=(0, 1, 2),
        name="prepare",
    )
    above, below = from_above(tail), from_below(head)
    cot_out, params = lax.optimization_barrier((cot_out, params))
    cot = exchanged(cot_out).reshape(groups, sites, own_members, block_cols)
    per_block = obs_index.shape[1]
    observations = per_block * groups
    params = params[:, :, :own_rows].reshape(groups, 3, per_block, 2, half)
    params = params.transpose(1, 4, 3, 0, 2).reshape(3, half, 2 * observations)

    row_number = space_place * own_rows - HALO + jnp.arange(tall)
    inside = ((row_number >= 0) & (row_number < band)).astype(jnp.float32)
    shape = (own_rows, own_members, width)
    padded = (tall, own_members, width)
    spread, observed, east1, north1, east2, north2 = kernel_call(
        forward_kernel,
        [(groups, sites, own_members, block_cols), (half, own_members, 2 * observations)]
        + [shape] * 4,
        [inside, initial_state, depth_field, above, below, params[0]],
        [padded] * 4 + [shape, shape, (tall, width), (groups, sites, own_members, block_cols)],
        copies=5,
        far_outs=(0, 2, 3, 4, 5),
        flops=10**8,
        name="forward",
    )
    observed = [observed] + [turned(observed, d) for d in range(1, groups)]
    place = ens_place.astype(jnp.int32)[None]
    scaled, extra, gram = kernel_call(
        gram_kernel,
        [(half, members, 2 * observations), (half, 8, 2 * observations), (members + 8, members)],
        [place, params] + observed,
        [(groups,) + observed[0].shape],
        copies=groups,
        far_ins=tuple(range(2, 2 + groups)),
        flops=4 * 2 * 6 * members**3,
        name="gram",
    )
    spread, gram = lax.optimization_barrier((spread, gram))
    forecast = exchanged(spread)
    gram = summed(gram, "space")
    inverse, mixing, mean_weights = kernel_call(
        factor_kernel,
        [(members, members), (members, members), (8, members)],
        [gram],
        flops=10**9,
        name="factor",
    )
    scaled, extra, _ = lax.optimization_barrier((scaled, extra, gram))
    obs_pack = jnp.concatenate([scaled, extra], axis=1)
    left, right = obs_pack[..., :observations], obs_pack[..., observations:]
    obs_tall = jnp.concatenate(
        [
            jnp.concatenate([from_above(right), right], axis=-1),
            jnp.concatenate([left, from_below(left)], axis=-1),
        ]
    )

    (own_cross,) = kernel_call(
        cross_kernel, [(members, members)], [forecast, cot], flops=10**10, name="cross"
    )
    mixing, obs_tall = lax.optimization_barrier((mixing, obs_tall))
    (mixed,) = kernel_call(
        mix_kernel,
        [cot.shape],
        [mixing, cot],
        [cot.shape],
        copies=fields,
        far_outs=(0,),
        flops=10**10,
        name="mix",
    )
    mixed, own_cross = lax.optimization_barrier((mixed, own_cross))
    back = exchanged(mixed)

    parts = kernel_call(
        pullback_kernel,
        [(2 * own_members + 8, members)] * groups,
        [place, summed(own_cross, "space"), inverse, mean_weights],
        [(members, members)] * 2,
        flops=10**9,
        name="pullback",
    )
    parts = [parts[0]] + [turned(parts[d], d) for d in range(1, groups)]
    (seen,) = kernel_call(
        observe_kernel,
        [padded],
        parts + [obs_tall],
        [(groups,) + parts[0].shape],
        copies=groups,
        far_ins=tuple(range(groups)),
        flops=10**9,
        name="observe",
    )
    back, parts = lax.optimization_barrier((back, parts))

    by_field = back.reshape(groups, fields, own_rows, own_members, block_cols)

    def adjoint_edge(take):
        parts = [
            by_field[:, f, take(n)].reshape(groups, -1, block_cols) for f, n in ADJOINT_EDGE
        ]
        return jnp.concatenate(parts, axis=1)

    adjoint_above = from_above(adjoint_edge(lambda n: slice(own_rows - n, own_rows)))
    adjoint_below = from_below(adjoint_edge(lambda n: slice(0, n)))
    depth_tall = jnp.concatenate([above[-1, half:own_rows], depth_field, below[-1, :half]])
    depth_grad, state_grad = kernel_call(
        backward_kernel,
        [(own_rows, width), (fields,) + shape],
        [
            inside, back, adjoint_above, adjoint_below, seen, depth_tall,
            east1, north1, east2, north2,
        ],
        [padded] * 5,
        flops=10**8,
        name="backward",
    )
    depth_grad = jnp.sum(gathered(depth_grad, "ens"), axis=0)
    return (state_grad, depth_grad)


def solution(mesh):
    in_specs = (
        P(None, "space", "ens", None),
        P("space", None),
        P("space", "ens"),
        P("space", "ens"),
        P("space", "ens"),
        P(None, "space", "ens", None),
    )
    out_specs = (P(None, "space", "ens", None), P("space", None))
    return jax.shard_map(
        per_device, mesh=mesh, in_specs=in_specs, out_specs=out_specs, check_vma=False
    )
```

```python
import functools
import math

import jax
import jax.numpy as jnp
from jax import lax
from jax.experimental import pallas as pl
from jax.experimental.pallas import tpu as pltpu
from jax.sharding import PartitionSpec as P

WAVE_COEF = 0.3
SPIN_COEF = 0.1
HALO = 4
HIGHEST = lax.Precision.HIGHEST
STATE_EDGE = ((0, 4), (1, 3), (2, 3))
ADJOINT_EDGE = ((0, 4), (2, 3), (1, 2))
VMEM = pl.BlockSpec(memory_space=pltpu.VMEM)
HBM = pl.BlockSpec(memory_space=pltpu.HBM)
SMEM = pl.BlockSpec(memory_space=pltpu.SMEM)


def kernel_call(body, outs, ins, scratch=(), copies=0, far_outs=(), far_ins=(), flops=0, name=None):
    moved = sum(math.prod(o) for o in outs) * 4 + sum(i.size for i in ins) * 4
    near = lambda i, a: SMEM if a.ndim == 1 else HBM if i in far_ins else VMEM
    made = lambda i, o: (pltpu.HBM if i in far_outs else jax.ShapeDtypeStruct)(o, jnp.float32)
    ins = [
        pltpu.with_memory_space_constraint(a, pltpu.HBM) if i in far_ins else a
        for i, a in enumerate(ins)
    ]
    return pl.pallas_call(
        body,
        out_shape=[made(i, o) for i, o in enumerate(outs)],
        in_specs=[near(i, a) for i, a in enumerate(ins)],
        out_specs=[HBM if i in far_outs else VMEM for i in range(len(outs))],
        scratch_shapes=[pltpu.VMEM(s, jnp.float32) for s in scratch]
        + ([pltpu.SemaphoreType.DMA((copies,))] if copies else []),
        compiler_params=pltpu.CompilerParams(vmem_limit_bytes=20 * 2**20),
        cost_estimate=pl.CostEstimate(flops=flops, bytes_accessed=moved, transcendentals=0),
        name=name,
    )(*ins)


def exchanged(blocks):
    return lax.all_to_all(blocks, "ens", 0, 0, tiled=False)


def gathered(block, axis):
    count = lax.axis_size(axis)
    copies = jnp.broadcast_to(block[None], (count,) + block.shape)
    return lax.all_to_all(copies, axis, 0, 0, tiled=False)


def turned(block, distance):
    count = lax.axis_size("ens")
    return lax.ppermute(block, "ens", [(i, (i + distance) % count) for i in range(count)])


def summed(block):
    count = lax.axis_size("space")

    def other(distance):
        return lax.ppermute(block, "space", [(i, i ^ distance) for i in range(count)])

    distance = 1
    while distance < count:
        if distance > 1 and 2 * distance < count:
            near, far, both = other(distance), other(2 * distance), other(3 * distance)
            block = (block + near) + (far + both)
            distance *= 4
        else:
            block = block + other(distance)
            distance *= 2
    return block


def from_above(rows_sent):
    count = lax.axis_size("space")
    return lax.ppermute(rows_sent, "space", [(i, i + 1) for i in range(count - 1)])


def from_below(rows_sent):
    count = lax.axis_size("space")
    return lax.ppermute(rows_sent, "space", [(i + 1, i) for i in range(count - 1)])


def cols(field):
    width = field.shape[1]
    return pltpu.roll(field, width - 1, 1) - pltpu.roll(field, 1, 1)


def dot(a, b, dims=((1,), (0,))):
    return lax.dot_general(
        a, b, (dims, ((), ())), precision=HIGHEST, preferred_element_type=jnp.float32
    )


def prepare_kernel(
    state_ref, depth_ref, cot_ref, tail_ref, head_ref, out_ref, tail, head, cot, spread, sems
):
    own = state_ref.shape[1]
    groups, sites, part = spread.shape
    copies = []

    def send(source, target):
        copies.append(pltpu.make_async_copy(source, target, sems.at[len(copies)]))
        copies[-1].start()

    fields = len(STATE_EDGE)
    piece = sites // fields
    at = 0
    for f, n in STATE_EDGE:
        send(state_ref.at[f, pl.ds(own - n, n)], tail.at[pl.ds(at, n)])
        send(state_ref.at[f, pl.ds(0, n)], head.at[pl.ds(at, n)])
        at += n
    for edge in (tail, head):
        send(depth_ref, edge.at[at, pl.ds(0, own)])
    for f in range(fields):
        send(cot_ref.at[pl.ds(f * piece, piece)], cot.at[pl.ds(f * piece, piece)])
    for copy in copies[: 2 * fields + 2]:
        copy.wait()
    tail[at, own:] = tail[at, :own]
    head[at, own:] = head[at, :own]
    send(tail, tail_ref)
    send(head, head_ref)
    for f in range(fields):
        copies[2 * fields + 2 + f].wait()
        for j in range(groups):
            spread[j, f * piece : (f + 1) * piece] = cot[
                f * piece : (f + 1) * piece, j * part : (j + 1) * part
            ]
        send(spread.at[:, pl.ds(f * piece, piece)], out_ref.at[:, pl.ds(f * piece, piece)])
    for copy in copies[3 * fields + 2 :]:
        copy.wait()


def padded_rows(edges, size, own_row, above, below):
    start = {}
    at = 0
    for f, n in edges:
        start[f] = (at, n)
        at += n * size

    def row(f, p, own_rows):
        first, n = start[f]
        if p < HALO:
            return above(first + (p - (HALO - n)) * size)
        if p < HALO + own_rows:
            return own_row(f, p - HALO)
        return below(first + (p - HALO - own_rows) * size)

    return row, at


def forward_kernel(
    inside_ref, state_ref, depth_ref, above_ref, below_ref, index_ref,
    out_ref, observed_ref, east1_ref, north1_ref, east2_ref, north2_ref,
    e1, n1, h1, n2, h2, e2, depth, spread, sems,
):
    own, size, width = east1_ref.shape
    groups = spread.shape[0]
    part = width // groups
    low, high = HALO, HALO + own
    row, at = padded_rows(
        STATE_EDGE,
        1,
        lambda f, r: state_ref[f, r],
        lambda i: above_ref[i],
        lambda i: below_ref[i],
    )
    row = functools.partial(row, own_rows=own)
    depth[:HALO] = above_ref[at, own - HALO : own]
    depth[low:high] = depth_ref[...]
    depth[high:] = below_ref[at, :HALO]

    def d(p):
        return depth[p : p + 1]

    for p in range(low - 3, high + 3):
        n1[p] = row(2, p) - WAVE_COEF * (row(0, p + 1) - row(0, p - 1)) - SPIN_COEF * row(1, p)
    for p in range(low - 2, high + 2):
        new_east = row(1, p) - WAVE_COEF * cols(row(0, p)) + SPIN_COEF * row(2, p)
        e1[p] = new_east
        flow = cols(d(p) * new_east) + (d(p + 1) * n1[p + 1] - d(p - 1) * n1[p - 1])
        h1[p] = (row(0, p) - WAVE_COEF * flow) * inside_ref[p]
    copies = []

    def send(source, target):
        copies.append(pltpu.make_async_copy(source, target, sems.at[len(copies)]))
        copies[-1].start()

    send(e1.at[pl.ds(low, own)], east1_ref)
    send(n1.at[pl.ds(low, own)], north1_ref)
    for p in range(low - 1, high + 1):
        n2[p] = n1[p] - WAVE_COEF * (h1[p + 1] - h1[p - 1]) - SPIN_COEF * e1[p]
    for p in range(low, high):
        r = p - low
        new_east = e1[p] - WAVE_COEF * cols(h1[p]) + SPIN_COEF * n1[p]
        flow = cols(d(p) * new_east) + (d(p + 1) * n2[p + 1] - d(p - 1) * n2[p - 1])
        new_height = h1[p] - WAVE_COEF * flow
        new_north = n2[p]
        h2[r] = new_height
        e2[r] = new_east
        for f, field in enumerate((new_height, new_east, new_north)):
            for j in range(groups):
                spread[j, f * own + r] = field[:, j * part : (j + 1) * part]
    send(spread, out_ref)
    send(e2, east2_ref)
    send(n2.at[pl.ds(low, own)], north2_ref)
    pairs, lanes = index_ref.shape
    many = 2 * groups * size
    sub = lax.broadcasted_iota(jnp.int32, (part, lanes), 0)
    source = lax.broadcasted_iota(jnp.int32, (many, lanes), 0) // size
    target = lax.broadcasted_iota(jnp.int32, (many, lanes), 1) // (lanes // 2 // groups)
    for q in range(pairs):
        index = index_ref[q : q + 1].astype(jnp.int32)
        hit = (sub == index).astype(jnp.float32)
        stacked = jnp.concatenate(
            [h2[q + h * pairs, :, j * part : (j + 1) * part] for h in range(2) for j in range(groups)],
            axis=0,
        )
        seen = jnp.where(source == target, dot(stacked, hit), 0.0)
        observed_ref[q] = seen.reshape(2 * groups, size, lanes).sum(0)
    for copy in copies:
        copy.wait()


def backward_kernel(
    inside_ref, back_ref, above_ref, below_ref, seen_ref, depth_ref,
    east1_ref, north1_ref, east2_ref, north2_ref,
    depth_grad_ref, height_ref, east_ref, north_ref,
    h2, h1, e1, n1, nt,
):
    own, size, width = east1_ref.shape
    groups = back_ref.shape[0]
    low, high = HALO, HALO + own
    wide = lambda ref, at: jnp.concatenate([ref[j, at] for j in range(groups)], axis=1)
    row, _ = padded_rows(
        ADJOINT_EDGE,
        size,
        lambda f, r: wide(back_ref, f * own + r),
        lambda i: wide(above_ref, slice(i, i + size)),
        lambda i: wide(below_ref, slice(i, i + size)),
    )
    row = functools.partial(row, own_rows=own)

    def d(p):
        return depth_ref[p : p + 1]

    for p in range(0, high + HALO):
        h2[p] = row(0, p) + seen_ref[p]
    for p in range(low - 3, high + 3):
        along = WAVE_COEF * (h2[p + 1] - h2[p - 1])
        nt[p] = row(2, p) + d(p) * along
    for p in range(low - 2, high + 2):
        across = WAVE_COEF * cols(h2[p])
        total = row(1, p) + d(p) * across
        h1[p] = (h2[p] + WAVE_COEF * (cols(total) + (nt[p + 1] - nt[p - 1]))) * inside_ref[p]
        if low - 1 <= p < high + 1:
            n1[p] = nt[p] + SPIN_COEF * total
        if low <= p < high:
            r = p - low
            e1[p] = total - SPIN_COEF * nt[p]
            along = WAVE_COEF * (h2[p + 1] - h2[p - 1])
            depth_grad_ref[r : r + 1] = jnp.sum(
                east2_ref[r] * across + north2_ref[r] * along, axis=0, keepdims=True
            )
    for p in range(low - 1, high + 1):
        along = WAVE_COEF * (h1[p + 1] - h1[p - 1])
        nt[p] = n1[p] + d(p) * along
    height_ref[...] = h1[low - 1 : high + 1]
    for p in range(low, high):
        r = p - low
        across = WAVE_COEF * cols(h1[p])
        along = WAVE_COEF * (h1[p + 1] - h1[p - 1])
        east_ref[r] = e1[p] + d(p) * across
        depth_grad_ref[r : r + 1] += jnp.sum(
            east1_ref[r] * across + north1_ref[r] * along, axis=0, keepdims=True
        )
    north_ref[...] = nt[low - 1 : high + 1]


def finish_kernel(height_ref, east_ref, north_ref, state_grad_ref):
    own = east_ref.shape[0]
    for r in range(own):
        total, north = east_ref[r], north_ref[r + 1]
        state_grad_ref[0, r] = height_ref[r + 1] + WAVE_COEF * (
            cols(total) + (north_ref[r + 2] - north_ref[r])
        )
        state_grad_ref[1, r] = total - SPIN_COEF * north
        state_grad_ref[2, r] = north + SPIN_COEF * total


def gram_kernel(place_ref, params_ref, *refs):
    *observed_refs, scaled_ref, extra_ref, gram_ref, observed_ref, sems = refs
    groups, pairs, size, lanes = observed_ref.shape
    copies = []
    for d, ref in enumerate(observed_refs):
        there = observed_ref.at[lax.rem(place_ref[0] + groups - d, groups)]
        copies.append(pltpu.make_async_copy(ref, there, sems.at[d]))
        copies[-1].start()
    for copy in copies:
        copy.wait()
    members = groups * size
    gram = jnp.zeros((members, members), jnp.float32)
    proj = jnp.zeros((8, members), jnp.float32)
    for q in range(pairs):
        seen = observed_ref[:, q].reshape(members, lanes)
        mean = jnp.mean(seen, axis=0, keepdims=True)
        value, var = params_ref[1, q : q + 1], params_ref[2, q : q + 1]
        inv_sd = 1.0 / jnp.sqrt(var)
        obs_scale = 1.0 / jnp.sqrt(var * (members - 1))
        scaled = (seen - mean) * obs_scale
        innovation = (value - mean) * inv_sd
        scaled_ref[q] = scaled
        extra_ref[q] = jnp.concatenate(
            [innovation, obs_scale, inv_sd, params_ref[0, q : q + 1]]
            + [jnp.zeros((4, lanes), jnp.float32)],
            axis=0,
        )
        gram += dot(scaled, scaled, ((1,), (1,)))
        lead = jnp.concatenate([innovation, jnp.zeros((7, lanes), jnp.float32)], axis=0)
        proj += dot(lead, scaled, ((1,), (1,)))
    gram_ref[:members] = gram
    gram_ref[members:] = proj


def factor_kernel(gram_ref, inverse_ref, mixing_ref, mean_ref):
    members = inverse_ref.shape[0]
    step = 8
    blocks = members // step
    lane = lax.broadcasted_iota(jnp.int32, (step, members), 1)
    sub = lax.broadcasted_iota(jnp.int32, (step, members), 0)
    row_lane = lane[:1]
    body = [
        gram_ref[i * step : (i + 1) * step] + (lane == sub + i * step).astype(jnp.float32)
        for i in range(blocks)
    ]
    for k in range(0, members, 2):
        i0, s = divmod(k, step)
        row0, row1 = body[i0][s : s + 1], body[i0][s + 1 : s + 2]
        a, b, c = row0[:, k : k + 1], row0[:, k + 1 : k + 2], row1[:, k + 1 : k + 2]
        over_a = 1.0 / a
        over_c = a * (1.0 / (a * c - b * b))
        ratio = b * over_a
        first, second = row_lane == k, row_lane == k + 1
        row0 = jnp.where(first, 1.0, jnp.where(second, 0.0, row0))
        row1 = jnp.where(second, 1.0, jnp.where(first, 0.0, row1)) - ratio * row0
        inverse_ref[k : k + 1] = jnp.where(row_lane <= k, row0 * jnp.sqrt(over_a), 0.0)
        inverse_ref[k + 1 : k + 2] = jnp.where(row_lane <= k + 1, row1 * jnp.sqrt(over_c), 0.0)
        if k + 2 == members:
            break
        turned1 = row1 * over_c
        turned0 = row0 * over_a - ratio * turned1
        used = (lane == k) | (lane == k + 1)
        for i in range(i0, blocks):
            if i == i0 and s + 2 == step:
                continue
            factor0 = jnp.broadcast_to(body[i][:, k : k + 1], (step, members))
            factor1 = jnp.broadcast_to(body[i][:, k + 1 : k + 2], (step, members))
            update = jnp.where(used, 0.0, body[i]) - factor0 * turned0 - factor1 * turned1
            body[i] = jnp.where(sub > s + 1, update, body[i]) if i == i0 else update
    inverse = inverse_ref[...]
    proj = gram_ref[members:]
    mean = dot(dot(proj, inverse, ((1,), (1,))), inverse)
    mean_ref[...] = mean
    root = math.sqrt(members - 1)
    turned = inverse + mean[:1] / root
    turned = turned - jnp.mean(turned, axis=1, keepdims=True) + 1.0 / members
    mixing_ref[...] = turned.T


def pullback_kernel(place_ref, cross_ref, inverse_ref, mean_ref, *refs):
    *parts, grad, column = refs
    members = inverse_ref.shape[0]
    groups = len(parts)
    size = members // groups
    inverse = inverse_ref[...]
    cross = cross_ref[...]
    cross = cross - jnp.mean(cross, axis=0, keepdims=True)
    first = lax.broadcasted_iota(jnp.int32, (8, members), 0) == 0
    ones = jnp.where(first, 1.0, 0.0)
    mean_grad = dot(ones, cross, ((1,), (1,))) / math.sqrt(members - 1)
    proj_grad = dot(dot(mean_grad, inverse, ((1,), (1,))), inverse)
    product = dot(inverse, cross)
    row = lax.broadcasted_iota(jnp.int32, (members, members), 0)
    col = lax.broadcasted_iota(jnp.int32, (members, members), 1)
    upper = jnp.where(row < col, product, 0.0)
    mirrored = jnp.where(row == col, product, 0.0) + upper + upper.T
    inner_grad = dot(inverse.T, dot(mirrored, inverse))
    every = jnp.broadcast_to(proj_grad[:1], (members, members)).T
    outer = every * mean_ref[:1]
    gram_grad = -(inner_grad + outer + outer.T)
    grad[...] = gram_grad - jnp.mean(gram_grad, axis=0, keepdims=True)
    column[...] = every - jnp.mean(every, axis=0, keepdims=True)
    for d, part in enumerate(parts):
        there = lax.rem(place_ref[0] + d, groups)
        rows_there = pl.ds(pl.multiple_of(there * size, size), size)
        part[:size] = grad[rows_there]
        part[size : 2 * size] = column[rows_there]
        part[2 * size :] = proj_grad


def observe_kernel(*refs):
    *part_refs, obs_ref, seen_ref, parts, sems = refs
    tall, size, width = seen_ref.shape
    pairs, high, lanes = obs_ref.shape
    members = high - 8
    part = lanes
    groups = width // part
    copies = []
    for d, ref in enumerate(part_refs):
        copies.append(pltpu.make_async_copy(ref, parts.at[d], sems.at[d]))
        copies[-1].start()
    for copy in copies:
        copy.wait()
    whole = parts[...].sum(0)
    own_grad, own_proj, proj_grad = whole[:size], whole[size : 2 * size], whole[2 * size :]
    lane = lax.broadcasted_iota(jnp.int32, (size, lanes), 1)
    sub = lax.broadcasted_iota(jnp.int32, (part, lanes), 0)
    block = lanes // 2 // groups
    for t in range(pairs):
        scaled = obs_ref[t, :members]
        innovation, obs_scale, inv_sd, index = (
            obs_ref[t, members + i : members + i + 1] for i in range(4)
        )
        obs_grad = (dot(own_grad, scaled) + own_proj * innovation) * obs_scale
        obs_grad = obs_grad - dot(proj_grad, scaled)[:1] * inv_sd / members
        apart = jnp.concatenate(
            [jnp.where(lane // block == i, obs_grad, 0.0) for i in range(2 * groups)], axis=0
        )
        hit = (sub == index.astype(jnp.int32)).astype(jnp.float32)
        put = dot(apart, hit, ((1,), (1,)))
        for h in range(2):
            for j in range(groups):
                at = (h * groups + j) * size
                seen_ref[t + h * pairs, :, j * part : (j + 1) * part] = put[at : at + size]


def cross_kernel(state_ref, cot_ref, out_ref):
    groups, sites, size, part = state_ref.shape
    members = groups * size
    total = jnp.zeros((members, members), jnp.float32)
    for at in range(0, sites, 2):
        pick = lambda ref: jnp.concatenate(
            [ref[:, at + i].reshape(members, part) for i in range(2)], axis=1
        )
        total += dot(pick(state_ref), pick(cot_ref), ((1,), (1,)))
    out_ref[...] = total


def mix_kernel(mixing_ref, cot_ref, out_ref, mixed_ref, sems):
    groups, sites, size, part = cot_ref.shape
    members = groups * size
    mixing = mixing_ref[...]
    copies = []
    pieces = sems.shape[0]
    for at in range(0, sites, 2):
        both = jnp.concatenate(
            [cot_ref[:, at + i].reshape(members, part) for i in range(2)], axis=1
        )
        mixed = dot(mixing, both)
        for i in range(2):
            mixed_ref[:, at + i] = mixed[:, i * part : (i + 1) * part].reshape(groups, size, part)
        if (at + 2) % (sites // pieces) == 0:
            done = pl.ds(at + 2 - sites // pieces, sites // pieces)
            copies.append(
                pltpu.make_async_copy(
                    mixed_ref.at[:, done], out_ref.at[:, done], sems.at[len(copies)]
                )
            )
            copies[-1].start()
    for copy in copies:
        copy.wait()


def per_device(initial_state, depth_field, obs_index, obs_value, obs_var, cotangent):
    groups = lax.axis_size("ens")
    ens_place = lax.axis_index("ens")
    space_place = lax.axis_index("space")
    fields, own_rows, own_members, width = initial_state.shape
    members = own_members * groups
    block_cols = width // groups
    tall = own_rows + 2 * HALO
    band = own_rows * lax.axis_size("space")
    sites = fields * own_rows
    half = own_rows // 2

    edge = (sum(n for _, n in STATE_EDGE) + 1, own_members, width)
    blocks = (groups, sites * own_members, block_cols)
    tail, head, cot_out = kernel_call(
        prepare_kernel,
        [edge, edge, blocks],
        [initial_state, depth_field, cotangent.reshape(-1, width)],
        [edge, edge, (sites * own_members, width), blocks],
        copies=4 * fields + 4,
        far_outs=(0, 1, 2),
        far_ins=(0, 1, 2),
        name="prepare",
    )
    packed = jnp.concatenate([obs_index.T.astype(jnp.float32), obs_value.T, obs_var.T])
    packed = jnp.pad(packed, ((0, 0), (0, block_cols - packed.shape[1])))
    params = gathered(packed, "ens")
    above, below = from_above(tail), from_below(head)
    cot_out, params = lax.optimization_barrier((cot_out, params))
    cot = exchanged(cot_out).reshape(groups, sites, own_members, block_cols)
    per_block = obs_index.shape[1]
    observations = per_block * groups
    params = params[:, :, :own_rows].reshape(groups, 3, per_block, 2, half)
    params = params.transpose(1, 4, 3, 0, 2).reshape(3, half, 2 * observations)

    row_number = space_place * own_rows - HALO + jnp.arange(tall)
    inside = ((row_number >= 0) & (row_number < band)).astype(jnp.float32)
    shape = (own_rows, own_members, width)
    padded = (tall, own_members, width)
    spread, observed, east1, north1, east2, north2 = kernel_call(
        forward_kernel,
        [(groups, sites, own_members, block_cols), (half, own_members, 2 * observations)]
        + [shape] * 4,
        [inside, initial_state, depth_field, above, below, params[0]],
        [padded] * 4 + [shape, shape, (tall, width), (groups, sites, own_members, block_cols)],
        copies=5,
        far_outs=(0, 2, 3, 4, 5),
        flops=10**8,
        name="forward",
    )
    observed = [observed] + [turned(observed, d) for d in range(1, groups)]
    spread, observed = lax.optimization_barrier((spread, observed))
    forecast = exchanged(spread)
    place = ens_place.astype(jnp.int32)[None]
    scaled, extra, gram = kernel_call(
        gram_kernel,
        [(half, members, 2 * observations), (half, 8, 2 * observations), (members + 8, members)],
        [place, params] + observed,
        [(groups,) + observed[0].shape],
        copies=groups,
        far_ins=tuple(range(2, 2 + groups)),
        flops=4 * 2 * 6 * members**3,
        name="gram",
    )
    gram = summed(gram)
    inverse, mixing, mean_weights = kernel_call(
        factor_kernel,
        [(members, members), (members, members), (8, members)],
        [gram],
        flops=10**9,
        name="factor",
    )
    scaled, extra, _ = lax.optimization_barrier((scaled, extra, gram))
    obs_pack = jnp.concatenate([scaled, extra], axis=1)
    left, right = obs_pack[..., :observations], obs_pack[..., observations:]
    obs_tall = jnp.concatenate(
        [
            jnp.concatenate([from_above(right), right], axis=-1),
            jnp.concatenate([left, from_below(left)], axis=-1),
        ]
    )

    (own_cross,) = kernel_call(
        cross_kernel, [(members, members)], [forecast, cot], flops=10**10, name="cross"
    )
    (mixed,) = kernel_call(
        mix_kernel,
        [cot.shape],
        [mixing, cot],
        [cot.shape],
        copies=fields,
        far_outs=(0,),
        flops=10**10,
        name="mix",
    )
    back = exchanged(mixed)
    cross, obs_tall = lax.optimization_barrier((summed(own_cross), obs_tall))

    parts = kernel_call(
        pullback_kernel,
        [(2 * own_members + 8, members)] * groups,
        [place, cross, inverse, mean_weights],
        [(members, members)] * 2,
        flops=10**9,
        name="pullback",
    )
    parts = [parts[0]] + [turned(parts[d], d) for d in range(1, groups)]
    back, parts = lax.optimization_barrier((back, parts))
    (seen,) = kernel_call(
        observe_kernel,
        [padded],
        parts + [obs_tall],
        [(groups,) + parts[0].shape],
        copies=groups,
        far_ins=tuple(range(groups)),
        flops=10**9,
        name="observe",
    )

    by_field = back.reshape(groups, fields, own_rows, own_members, block_cols)

    def adjoint_edge(take):
        parts = [
            by_field[:, f, take(n)].reshape(groups, -1, block_cols) for f, n in ADJOINT_EDGE
        ]
        return jnp.concatenate(parts, axis=1)

    adjoint_above = from_above(adjoint_edge(lambda n: slice(own_rows - n, own_rows)))
    adjoint_below = from_below(adjoint_edge(lambda n: slice(0, n)))
    depth_tall = jnp.concatenate([above[-1, half:own_rows], depth_field, below[-1, :half]])
    wider = (own_rows + 2, own_members, width)
    depth_grad, *remaining = kernel_call(
        backward_kernel,
        [(own_rows, width), wider, shape, wider],
        [
            inside, back, adjoint_above, adjoint_below, seen, depth_tall,
            east1, north1, east2, north2,
        ],
        [padded] * 5,
        flops=10**8,
        name="backward",
    )
    (state_grad,) = kernel_call(
        finish_kernel, [(fields,) + shape], remaining, flops=10**7, name="finish"
    )
    depth_grad = jnp.sum(gathered(depth_grad, "ens"), axis=0)
    return (state_grad, depth_grad)


def solution(mesh):
    in_specs = (
        P(None, "space", "ens", None),
        P("space", None),
        P("space", "ens"),
        P("space", "ens"),
        P("space", "ens"),
        P(None, "space", "ens", None),
    )
    out_specs = (P(None, "space", "ens", None), P("space", None))
    return jax.shard_map(
        per_device, mesh=mesh, in_specs=in_specs, out_specs=out_specs, check_vma=False
    )
```

```python
import functools
import math

import jax
import jax.numpy as jnp
from jax import lax
from jax.experimental import pallas as pl
from jax.experimental.pallas import tpu as pltpu
from jax.sharding import PartitionSpec as P

WAVE_COEF = 0.3
SPIN_COEF = 0.1
HALO = 4
HIGHEST = lax.Precision.HIGHEST
STATE_EDGE = ((0, 4), (1, 3), (2, 3))
ADJOINT_EDGE = ((0, 4), (2, 3), (1, 2))
VMEM = pl.BlockSpec(memory_space=pltpu.VMEM)
HBM = pl.BlockSpec(memory_space=pltpu.HBM)
SMEM = pl.BlockSpec(memory_space=pltpu.SMEM)


def kernel_call(body, outs, ins, scratch=(), copies=0, far_outs=(), far_ins=(), flops=0, name=None):
    moved = sum(math.prod(o) for o in outs) * 4 + sum(i.size for i in ins) * 4
    near = lambda i, a: SMEM if a.ndim == 1 else HBM if i in far_ins else VMEM
    made = lambda i, o: (pltpu.HBM if i in far_outs else jax.ShapeDtypeStruct)(o, jnp.float32)
    ins = [
        pltpu.with_memory_space_constraint(a, pltpu.HBM) if i in far_ins else a
        for i, a in enumerate(ins)
    ]
    return pl.pallas_call(
        body,
        out_shape=[made(i, o) for i, o in enumerate(outs)],
        in_specs=[near(i, a) for i, a in enumerate(ins)],
        out_specs=[HBM if i in far_outs else VMEM for i in range(len(outs))],
        scratch_shapes=[pltpu.VMEM(s, jnp.float32) for s in scratch]
        + ([pltpu.SemaphoreType.DMA((copies,))] if copies else []),
        compiler_params=pltpu.CompilerParams(vmem_limit_bytes=20 * 2**20),
        cost_estimate=pl.CostEstimate(flops=flops, bytes_accessed=moved, transcendentals=0),
        name=name,
    )(*ins)


def exchanged(blocks):
    return lax.all_to_all(blocks, "ens", 0, 0, tiled=False)


def gathered(block, axis):
    count = lax.axis_size(axis)
    copies = jnp.broadcast_to(block[None], (count,) + block.shape)
    return lax.all_to_all(copies, axis, 0, 0, tiled=False)


def turned(block, distance):
    count = lax.axis_size("ens")
    return lax.ppermute(block, "ens", [(i, (i + distance) % count) for i in range(count)])


def crossed(block, distance):
    count = lax.axis_size("ens")
    return lax.ppermute(block, "ens", [(i, i ^ distance) for i in range(count)])


def summed(block):
    count = lax.axis_size("space")

    def other(distance):
        return lax.ppermute(block, "space", [(i, i ^ distance) for i in range(count)])

    distance = 1
    while distance < count:
        if distance > 1 and 2 * distance < count:
            near, far, both = other(distance), other(2 * distance), other(3 * distance)
            block = (block + near) + (far + both)
            distance *= 4
        else:
            block = block + other(distance)
            distance *= 2
    return block


def from_above(rows_sent):
    count = lax.axis_size("space")
    return lax.ppermute(rows_sent, "space", [(i, i + 1) for i in range(count - 1)])


def from_below(rows_sent):
    count = lax.axis_size("space")
    return lax.ppermute(rows_sent, "space", [(i + 1, i) for i in range(count - 1)])


def cols(field):
    width = field.shape[1]
    return pltpu.roll(field, width - 1, 1) - pltpu.roll(field, 1, 1)


def dot(a, b, dims=((1,), (0,))):
    return lax.dot_general(
        a, b, (dims, ((), ())), precision=HIGHEST, preferred_element_type=jnp.float32
    )


def prepare_kernel(
    state_ref, depth_ref, cot_ref, tail_ref, head_ref, out_ref, tail, head, cot, spread, sems
):
    own = state_ref.shape[1]
    groups, sites, part = spread.shape
    copies = []

    def send(source, target):
        copies.append(pltpu.make_async_copy(source, target, sems.at[len(copies)]))
        copies[-1].start()

    fields = len(STATE_EDGE)
    piece = sites // fields
    at = 0
    for f, n in STATE_EDGE:
        send(state_ref.at[f, pl.ds(own - n, n)], tail.at[pl.ds(at, n)])
        send(state_ref.at[f, pl.ds(0, n)], head.at[pl.ds(at, n)])
        at += n
    for edge in (tail, head):
        send(depth_ref, edge.at[at, pl.ds(0, own)])
    for f in range(fields):
        send(cot_ref.at[pl.ds(f * piece, piece)], cot.at[pl.ds(f * piece, piece)])
    for copy in copies[: 2 * fields + 2]:
        copy.wait()
    tail[at, own:] = tail[at, :own]
    head[at, own:] = head[at, :own]
    send(tail, tail_ref)
    send(head, head_ref)
    for f in range(fields):
        copies[2 * fields + 2 + f].wait()
        for j in range(groups):
            spread[j, f * piece : (f + 1) * piece] = cot[
                f * piece : (f + 1) * piece, j * part : (j + 1) * part
            ]
        send(spread.at[:, pl.ds(f * piece, piece)], out_ref.at[:, pl.ds(f * piece, piece)])
    for copy in copies[3 * fields + 2 :]:
        copy.wait()


def padded_rows(edges, size, own_row, above, below):
    start = {}
    at = 0
    for f, n in edges:
        start[f] = (at, n)
        at += n * size

    def row(f, p, own_rows):
        first, n = start[f]
        if p < HALO:
            return above(first + (p - (HALO - n)) * size)
        if p < HALO + own_rows:
            return own_row(f, p - HALO)
        return below(first + (p - HALO - own_rows) * size)

    return row, at


def forward_kernel(
    inside_ref, state_ref, depth_ref, above_ref, below_ref, index_ref,
    out_ref, observed_ref, east1_ref, north1_ref, east2_ref, north2_ref,
    e1, n1, h1, n2, h2, e2, depth, spread, sems,
):
    own, size, width = east1_ref.shape
    groups = spread.shape[0]
    part = width // groups
    low, high = HALO, HALO + own
    row, at = padded_rows(
        STATE_EDGE,
        1,
        lambda f, r: state_ref[f, r],
        lambda i: above_ref[i],
        lambda i: below_ref[i],
    )
    row = functools.partial(row, own_rows=own)
    depth[:HALO] = above_ref[at, own - HALO : own]
    depth[low:high] = depth_ref[...]
    depth[high:] = below_ref[at, :HALO]

    def d(p):
        return depth[p : p + 1]

    for p in range(low - 3, high + 3):
        n1[p] = row(2, p) - WAVE_COEF * (row(0, p + 1) - row(0, p - 1)) - SPIN_COEF * row(1, p)
    for p in range(low - 2, high + 2):
        new_east = row(1, p) - WAVE_COEF * cols(row(0, p)) + SPIN_COEF * row(2, p)
        e1[p] = new_east
        flow = cols(d(p) * new_east) + (d(p + 1) * n1[p + 1] - d(p - 1) * n1[p - 1])
        h1[p] = (row(0, p) - WAVE_COEF * flow) * inside_ref[p]
    copies = []

    def send(source, target):
        copies.append(pltpu.make_async_copy(source, target, sems.at[len(copies)]))
        copies[-1].start()

    send(e1.at[pl.ds(low, own)], east1_ref)
    send(n1.at[pl.ds(low, own)], north1_ref)
    for p in range(low - 1, high + 1):
        n2[p] = n1[p] - WAVE_COEF * (h1[p + 1] - h1[p - 1]) - SPIN_COEF * e1[p]
    for p in range(low, high):
        r = p - low
        new_east = e1[p] - WAVE_COEF * cols(h1[p]) + SPIN_COEF * n1[p]
        flow = cols(d(p) * new_east) + (d(p + 1) * n2[p + 1] - d(p - 1) * n2[p - 1])
        new_height = h1[p] - WAVE_COEF * flow
        new_north = n2[p]
        h2[r] = new_height
        e2[r] = new_east
        for f, field in enumerate((new_height, new_east, new_north)):
            for j in range(groups):
                spread[j, f * own + r] = field[:, j * part : (j + 1) * part]
    send(spread, out_ref)
    send(e2, east2_ref)
    send(n2.at[pl.ds(low, own)], north2_ref)
    pairs, lanes = index_ref.shape
    many = 2 * groups * size
    sub = lax.broadcasted_iota(jnp.int32, (part, lanes), 0)
    source = lax.broadcasted_iota(jnp.int32, (many, lanes), 0) // size
    target = lax.broadcasted_iota(jnp.int32, (many, lanes), 1) // (lanes // 2 // groups)
    for q in range(pairs):
        index = index_ref[q : q + 1].astype(jnp.int32)
        hit = (sub == index).astype(jnp.float32)
        stacked = jnp.concatenate(
            [h2[q + h * pairs, :, j * part : (j + 1) * part] for h in range(2) for j in range(groups)],
            axis=0,
        )
        seen = jnp.where(source == target, dot(stacked, hit), 0.0)
        observed_ref[q] = seen.reshape(2 * groups, size, lanes).sum(0)
    for copy in copies:
        copy.wait()


def backward_kernel(
    inside_ref, back_ref, above_ref, below_ref, seen_ref, depth_ref,
    east1_ref, north1_ref, east2_ref, north2_ref,
    depth_grad_ref, height_ref, east_ref, north_ref,
    h2, h1, e1, n1, nt,
):
    own, size, width = east1_ref.shape
    groups = back_ref.shape[0]
    low, high = HALO, HALO + own
    wide = lambda ref, at: jnp.concatenate([ref[j, at] for j in range(groups)], axis=1)
    row, _ = padded_rows(
        ADJOINT_EDGE,
        size,
        lambda f, r: wide(back_ref, f * own + r),
        lambda i: wide(above_ref, slice(i, i + size)),
        lambda i: wide(below_ref, slice(i, i + size)),
    )
    row = functools.partial(row, own_rows=own)

    def d(p):
        return depth_ref[p : p + 1]

    for p in range(0, high + HALO):
        h2[p] = row(0, p) + seen_ref[p]
    for p in range(low - 3, high + 3):
        along = WAVE_COEF * (h2[p + 1] - h2[p - 1])
        nt[p] = row(2, p) + d(p) * along
    for p in range(low - 2, high + 2):
        across = WAVE_COEF * cols(h2[p])
        total = row(1, p) + d(p) * across
        h1[p] = (h2[p] + WAVE_COEF * (cols(total) + (nt[p + 1] - nt[p - 1]))) * inside_ref[p]
        if low - 1 <= p < high + 1:
            n1[p] = nt[p] + SPIN_COEF * total
        if low <= p < high:
            r = p - low
            e1[p] = total - SPIN_COEF * nt[p]
            along = WAVE_COEF * (h2[p + 1] - h2[p - 1])
            depth_grad_ref[r : r + 1] = jnp.sum(
                east2_ref[r] * across + north2_ref[r] * along, axis=0, keepdims=True
            )
    for p in range(low - 1, high + 1):
        along = WAVE_COEF * (h1[p + 1] - h1[p - 1])
        nt[p] = n1[p] + d(p) * along
    height_ref[...] = h1[low - 1 : high + 1]
    for p in range(low, high):
        r = p - low
        across = WAVE_COEF * cols(h1[p])
        along = WAVE_COEF * (h1[p + 1] - h1[p - 1])
        east_ref[r] = e1[p] + d(p) * across
        depth_grad_ref[r : r + 1] += jnp.sum(
            east1_ref[r] * across + north1_ref[r] * along, axis=0, keepdims=True
        )
    north_ref[...] = nt[low - 1 : high + 1]


def finish_kernel(height_ref, east_ref, north_ref, state_grad_ref):
    own = east_ref.shape[0]
    for r in range(own):
        total, north = east_ref[r], north_ref[r + 1]
        state_grad_ref[0, r] = height_ref[r + 1] + WAVE_COEF * (
            cols(total) + (north_ref[r + 2] - north_ref[r])
        )
        state_grad_ref[1, r] = total - SPIN_COEF * north
        state_grad_ref[2, r] = north + SPIN_COEF * total


def gram_kernel(place_ref, params_ref, *refs):
    *observed_refs, scaled_ref, extra_ref, gram_ref, observed_ref, sems = refs
    groups, pairs, size, lanes = observed_ref.shape
    copies = []
    for d, ref in enumerate(observed_refs):
        there = observed_ref.at[lax.rem(place_ref[0] + groups - d, groups)]
        copies.append(pltpu.make_async_copy(ref, there, sems.at[d]))
        copies[-1].start()
    for copy in copies:
        copy.wait()
    members = groups * size
    gram = jnp.zeros((members, members), jnp.float32)
    proj = jnp.zeros((8, members), jnp.float32)
    for q in range(pairs):
        seen = observed_ref[:, q].reshape(members, lanes)
        mean = jnp.mean(seen, axis=0, keepdims=True)
        value, var = params_ref[1, q : q + 1], params_ref[2, q : q + 1]
        inv_sd = 1.0 / jnp.sqrt(var)
        obs_scale = 1.0 / jnp.sqrt(var * (members - 1))
        scaled = (seen - mean) * obs_scale
        innovation = (value - mean) * inv_sd
        scaled_ref[q] = scaled
        extra_ref[q] = jnp.concatenate(
            [innovation, obs_scale, inv_sd, params_ref[0, q : q + 1]]
            + [jnp.zeros((4, lanes), jnp.float32)],
            axis=0,
        )
        gram += dot(scaled, scaled, ((1,), (1,)))
        lead = jnp.concatenate([innovation, jnp.zeros((7, lanes), jnp.float32)], axis=0)
        proj += dot(lead, scaled, ((1,), (1,)))
    gram_ref[:members] = gram
    gram_ref[members:] = proj


def factor_kernel(gram_ref, inverse_ref, mixing_ref, mean_ref):
    members = inverse_ref.shape[0]
    step = 8
    blocks = members // step
    lane = lax.broadcasted_iota(jnp.int32, (step, members), 1)
    sub = lax.broadcasted_iota(jnp.int32, (step, members), 0)
    row_lane = lane[:1]
    body = [
        gram_ref[i * step : (i + 1) * step] + (lane == sub + i * step).astype(jnp.float32)
        for i in range(blocks)
    ]
    for k in range(0, members, 2):
        i0, s = divmod(k, step)
        row0, row1 = body[i0][s : s + 1], body[i0][s + 1 : s + 2]
        a, b, c = row0[:, k : k + 1], row0[:, k + 1 : k + 2], row1[:, k + 1 : k + 2]
        over_a = 1.0 / a
        over_c = a * (1.0 / (a * c - b * b))
        ratio = b * over_a
        first, second = row_lane == k, row_lane == k + 1
        row0 = jnp.where(first, 1.0, jnp.where(second, 0.0, row0))
        row1 = jnp.where(second, 1.0, jnp.where(first, 0.0, row1)) - ratio * row0
        inverse_ref[k : k + 1] = jnp.where(row_lane <= k, row0 * jnp.sqrt(over_a), 0.0)
        inverse_ref[k + 1 : k + 2] = jnp.where(row_lane <= k + 1, row1 * jnp.sqrt(over_c), 0.0)
        if k + 2 == members:
            break
        turned1 = row1 * over_c
        turned0 = row0 * over_a - ratio * turned1
        used = (lane == k) | (lane == k + 1)
        for i in range(i0, blocks):
            if i == i0 and s + 2 == step:
                continue
            factor0 = jnp.broadcast_to(body[i][:, k : k + 1], (step, members))
            factor1 = jnp.broadcast_to(body[i][:, k + 1 : k + 2], (step, members))
            update = jnp.where(used, 0.0, body[i]) - factor0 * turned0 - factor1 * turned1
            body[i] = jnp.where(sub > s + 1, update, body[i]) if i == i0 else update
    inverse = inverse_ref[...]
    proj = gram_ref[members:]
    mean = dot(dot(proj, inverse, ((1,), (1,))), inverse)
    mean_ref[...] = mean
    root = math.sqrt(members - 1)
    turned = inverse + mean[:1] / root
    turned = turned - jnp.mean(turned, axis=1, keepdims=True) + 1.0 / members
    mixing_ref[...] = turned.T


def pullback_kernel(place_ref, cross_ref, inverse_ref, mean_ref, *refs):
    *parts, grad, column = refs
    members = inverse_ref.shape[0]
    near = len(parts)
    groups = 2 * near
    size = members // groups
    inverse = inverse_ref[...]
    cross = cross_ref[...]
    cross = cross - jnp.mean(cross, axis=0, keepdims=True)
    first = lax.broadcasted_iota(jnp.int32, (8, members), 0) == 0
    ones = jnp.where(first, 1.0, 0.0)
    mean_grad = dot(ones, cross, ((1,), (1,))) / math.sqrt(members - 1)
    proj_grad = dot(dot(mean_grad, inverse, ((1,), (1,))), inverse)
    product = dot(inverse, cross)
    row = lax.broadcasted_iota(jnp.int32, (members, members), 0)
    col = lax.broadcasted_iota(jnp.int32, (members, members), 1)
    upper = jnp.where(row < col, product, 0.0)
    mirrored = jnp.where(row == col, product, 0.0) + upper + upper.T
    inner_grad = dot(inverse.T, dot(mirrored, inverse))
    every = jnp.broadcast_to(proj_grad[:1], (members, members)).T
    outer = every * mean_ref[:1]
    gram_grad = -(inner_grad + outer + outer.T)
    grad[...] = gram_grad - jnp.mean(gram_grad, axis=0, keepdims=True)
    column[...] = every - jnp.mean(every, axis=0, keepdims=True)
    for j, part in enumerate(parts):
        for h in range(2):
            there = place_ref[0] ^ (j + h * near)
            rows_there = pl.ds(pl.multiple_of(there * size, size), size)
            part[h, :size] = grad[rows_there]
            part[h, size : 2 * size] = column[rows_there]
            part[h, 2 * size :] = proj_grad


def observe_kernel(*refs):
    near_ref, far_ref, obs_ref, seen_ref = refs
    tall, size, width = seen_ref.shape
    pairs, high, lanes = obs_ref.shape
    members = high - 8
    part = lanes
    groups = width // part
    whole = near_ref[...] + far_ref[...]
    own_grad, own_proj, proj_grad = whole[:size], whole[size : 2 * size], whole[2 * size :]
    lane = lax.broadcasted_iota(jnp.int32, (size, lanes), 1)
    sub = lax.broadcasted_iota(jnp.int32, (part, lanes), 0)
    block = lanes // 2 // groups
    for t in range(pairs):
        scaled = obs_ref[t, :members]
        innovation, obs_scale, inv_sd, index = (
            obs_ref[t, members + i : members + i + 1] for i in range(4)
        )
        obs_grad = (dot(own_grad, scaled) + own_proj * innovation) * obs_scale
        obs_grad = obs_grad - dot(proj_grad, scaled)[:1] * inv_sd / members
        apart = jnp.concatenate(
            [jnp.where(lane // block == i, obs_grad, 0.0) for i in range(2 * groups)], axis=0
        )
        hit = (sub == index.astype(jnp.int32)).astype(jnp.float32)
        put = dot(apart, hit, ((1,), (1,)))
        for h in range(2):
            for j in range(groups):
                at = (h * groups + j) * size
                seen_ref[t + h * pairs, :, j * part : (j + 1) * part] = put[at : at + size]


def cross_kernel(state_ref, cot_ref, out_ref, state, sems):
    groups, sites, size, part = state.shape
    members = groups * size
    pieces = sems.shape[0]
    piece = sites // pieces
    copies = []
    for i in range(pieces):
        now = pl.ds(i * piece, piece)
        copies.append(pltpu.make_async_copy(state_ref.at[:, now], state.at[:, now], sems.at[i]))
        copies[-1].start()
    total = jnp.zeros((members, members), jnp.float32)
    for at in range(0, sites, 2):
        if at % piece == 0:
            copies[at // piece].wait()
        pick = lambda ref: jnp.concatenate(
            [ref[:, at + i].reshape(members, part) for i in range(2)], axis=1
        )
        total += dot(pick(state), pick(cot_ref), ((1,), (1,)))
    out_ref[...] = total


def mix_kernel(mixing_ref, cot_ref, out_ref, mixed_ref, sems):
    groups, sites, size, part = cot_ref.shape
    members = groups * size
    mixing = mixing_ref[...]
    copies = []
    pieces = sems.shape[0]
    for at in range(0, sites, 2):
        both = jnp.concatenate(
            [cot_ref[:, at + i].reshape(members, part) for i in range(2)], axis=1
        )
        mixed = dot(mixing, both)
        for i in range(2):
            mixed_ref[:, at + i] = mixed[:, i * part : (i + 1) * part].reshape(groups, size, part)
        if (at + 2) % (sites // pieces) == 0:
            done = pl.ds(at + 2 - sites // pieces, sites // pieces)
            copies.append(
                pltpu.make_async_copy(
                    mixed_ref.at[:, done], out_ref.at[:, done], sems.at[len(copies)]
                )
            )
            copies[-1].start()
    for copy in copies:
        copy.wait()


def per_device(initial_state, depth_field, obs_index, obs_value, obs_var, cotangent):
    groups = lax.axis_size("ens")
    ens_place = lax.axis_index("ens")
    space_place = lax.axis_index("space")
    fields, own_rows, own_members, width = initial_state.shape
    members = own_members * groups
    block_cols = width // groups
    tall = own_rows + 2 * HALO
    band = own_rows * lax.axis_size("space")
    sites = fields * own_rows
    half = own_rows // 2

    edge = (sum(n for _, n in STATE_EDGE) + 1, own_members, width)
    blocks = (groups, sites * own_members, block_cols)
    tail, head, cot_out = kernel_call(
        prepare_kernel,
        [edge, edge, blocks],
        [initial_state, depth_field, cotangent.reshape(-1, width)],
        [edge, edge, (sites * own_members, width), blocks],
        copies=4 * fields + 4,
        far_outs=(0, 1, 2),
        far_ins=(0, 1, 2),
        name="prepare",
    )
    packed = jnp.concatenate([obs_index.T.astype(jnp.float32), obs_value.T, obs_var.T])
    packed = jnp.pad(packed, ((0, 0), (0, block_cols - packed.shape[1])))
    params = gathered(packed, "ens")
    above, below = from_above(tail), from_below(head)
    cot_out, params = lax.optimization_barrier((cot_out, params))
    cot = exchanged(cot_out).reshape(groups, sites, own_members, block_cols)
    per_block = obs_index.shape[1]
    observations = per_block * groups
    params = params[:, :, :own_rows].reshape(groups, 3, per_block, 2, half)
    params = params.transpose(1, 4, 3, 0, 2).reshape(3, half, 2 * observations)

    row_number = space_place * own_rows - HALO + jnp.arange(tall)
    inside = ((row_number >= 0) & (row_number < band)).astype(jnp.float32)
    shape = (own_rows, own_members, width)
    padded = (tall, own_members, width)
    spread, observed, east1, north1, east2, north2 = kernel_call(
        forward_kernel,
        [(groups, sites, own_members, block_cols), (half, own_members, 2 * observations)]
        + [shape] * 4,
        [inside, initial_state, depth_field, above, below, params[0]],
        [padded] * 4 + [shape, shape, (tall, width), (groups, sites, own_members, block_cols)],
        copies=5,
        far_outs=(0, 2, 3, 4, 5),
        flops=10**8,
        name="forward",
    )
    observed = [observed] + [turned(observed, d) for d in range(1, groups)]
    spread, observed = lax.optimization_barrier((spread, observed))
    forecast = exchanged(spread)
    place = ens_place.astype(jnp.int32)[None]
    scaled, extra, gram = kernel_call(
        gram_kernel,
        [(half, members, 2 * observations), (half, 8, 2 * observations), (members + 8, members)],
        [place, params] + observed,
        [(groups,) + observed[0].shape],
        copies=groups,
        far_ins=tuple(range(2, 2 + groups)),
        flops=4 * 2 * 6 * members**3,
        name="gram",
    )
    gram = summed(gram)
    inverse, mixing, mean_weights = kernel_call(
        factor_kernel,
        [(members, members), (members, members), (8, members)],
        [gram],
        flops=10**9,
        name="factor",
    )
    scaled, extra, _ = lax.optimization_barrier((scaled, extra, gram))
    obs_pack = jnp.concatenate([scaled, extra], axis=1)
    left, right = obs_pack[..., :observations], obs_pack[..., observations:]
    obs_tall = jnp.concatenate(
        [
            jnp.concatenate([from_above(right), right], axis=-1),
            jnp.concatenate([left, from_below(left)], axis=-1),
        ]
    )

    (own_cross,) = kernel_call(
        cross_kernel,
        [(members, members)],
        [forecast, cot],
        [cot.shape],
        copies=fields,
        far_ins=(0,),
        flops=10**10,
        name="cross",
    )
    (mixed,) = kernel_call(
        mix_kernel,
        [cot.shape],
        [mixing, cot],
        [cot.shape],
        copies=fields,
        far_outs=(0,),
        flops=10**10,
        name="mix",
    )
    back = exchanged(mixed)
    cross, obs_tall = lax.optimization_barrier((summed(own_cross), obs_tall))

    near = groups // 2
    parts = kernel_call(
        pullback_kernel,
        [(2, 2 * own_members + 8, members)] * near,
        [place, cross, inverse, mean_weights],
        [(members, members)] * 2,
        flops=10**9,
        name="pullback",
    )
    parts = [parts[0]] + [crossed(parts[j], j) for j in range(1, near)]
    back, parts = lax.optimization_barrier((back, parts))
    whole = sum(parts[1:], parts[0])

    by_field = back.reshape(groups, fields, own_rows, own_members, block_cols)

    def adjoint_edge(take):
        parts = [
            by_field[:, f, take(n)].reshape(groups, -1, block_cols) for f, n in ADJOINT_EDGE
        ]
        return jnp.concatenate(parts, axis=1)

    adjoint_tail = adjoint_edge(lambda n: slice(own_rows - n, own_rows))
    adjoint_head = adjoint_edge(lambda n: slice(0, n))
    adjoint_above, adjoint_below = from_above(adjoint_tail), from_below(adjoint_head)
    whole, _, _ = lax.optimization_barrier((whole, adjoint_tail, adjoint_head))
    (seen,) = kernel_call(
        observe_kernel,
        [padded],
        [whole[0], crossed(whole[1], near), obs_tall],
        flops=10**9,
        name="observe",
    )
    depth_tall = jnp.concatenate([above[-1, half:own_rows], depth_field, below[-1, :half]])
    wider = (own_rows + 2, own_members, width)
    depth_grad, *remaining = kernel_call(
        backward_kernel,
        [(own_rows, width), wider, shape, wider],
        [
            inside, back, adjoint_above, adjoint_below, seen, depth_tall,
            east1, north1, east2, north2,
        ],
        [padded] * 5,
        flops=10**8,
        name="backward",
    )
    (state_grad,) = kernel_call(
        finish_kernel, [(fields,) + shape], remaining, flops=10**7, name="finish"
    )
    depth_grad = jnp.sum(gathered(depth_grad, "ens"), axis=0)
    return (state_grad, depth_grad)


def solution(mesh):
    in_specs = (
        P(None, "space", "ens", None),
        P("space", None),
        P("space", "ens"),
        P("space", "ens"),
        P("space", "ens"),
        P(None, "space", "ens", None),
    )
    out_specs = (P(None, "space", "ens", None), P("space", None))
    return jax.shard_map(
        per_device, mesh=mesh, in_specs=in_specs, out_specs=out_specs, check_vma=False
    )
```

```python
import functools
import math

import jax
import jax.numpy as jnp
from jax import lax
from jax.experimental import pallas as pl
from jax.experimental.pallas import tpu as pltpu
from jax.sharding import PartitionSpec as P

WAVE_COEF = 0.3
SPIN_COEF = 0.1
HALO = 4
HIGHEST = lax.Precision.HIGHEST
STATE_EDGE = ((0, 4), (1, 3), (2, 3))
ADJOINT_EDGE = ((0, 4), (2, 3), (1, 2))
VMEM = pl.BlockSpec(memory_space=pltpu.VMEM)
HBM = pl.BlockSpec(memory_space=pltpu.HBM)
SMEM = pl.BlockSpec(memory_space=pltpu.SMEM)


def kernel_call(body, outs, ins, scratch=(), copies=0, far_outs=(), far_ins=(), flops=0, name=None):
    moved = sum(math.prod(o) for o in outs) * 4 + sum(i.size for i in ins) * 4
    near = lambda i, a: SMEM if a.ndim == 1 else HBM if i in far_ins else VMEM
    made = lambda i, o: (pltpu.HBM if i in far_outs else jax.ShapeDtypeStruct)(o, jnp.float32)
    ins = [
        pltpu.with_memory_space_constraint(a, pltpu.HBM) if i in far_ins else a
        for i, a in enumerate(ins)
    ]
    return pl.pallas_call(
        body,
        out_shape=[made(i, o) for i, o in enumerate(outs)],
        in_specs=[near(i, a) for i, a in enumerate(ins)],
        out_specs=[HBM if i in far_outs else VMEM for i in range(len(outs))],
        scratch_shapes=[pltpu.VMEM(s, jnp.float32) for s in scratch]
        + ([pltpu.SemaphoreType.DMA((copies,))] if copies else []),
        compiler_params=pltpu.CompilerParams(vmem_limit_bytes=20 * 2**20),
        cost_estimate=pl.CostEstimate(flops=flops, bytes_accessed=moved, transcendentals=0),
        name=name,
    )(*ins)


def exchanged(blocks):
    return lax.all_to_all(blocks, "ens", 0, 0, tiled=False)


def gathered(block, axis):
    count = lax.axis_size(axis)
    copies = jnp.broadcast_to(block[None], (count,) + block.shape)
    return lax.all_to_all(copies, axis, 0, 0, tiled=False)


def turned(block, distance):
    count = lax.axis_size("ens")
    return lax.ppermute(block, "ens", [(i, (i + distance) % count) for i in range(count)])


def crossed(block, distance):
    count = lax.axis_size("ens")
    return lax.ppermute(block, "ens", [(i, i ^ distance) for i in range(count)])


def summed(block):
    count = lax.axis_size("space")

    def other(distance):
        return lax.ppermute(block, "space", [(i, i ^ distance) for i in range(count)])

    distance = 1
    while distance < count:
        if distance > 1 and 2 * distance < count:
            near, far, both = other(distance), other(2 * distance), other(3 * distance)
            block = (block + near) + (far + both)
            distance *= 4
        else:
            block = block + other(distance)
            distance *= 2
    return block


def from_above(rows_sent):
    count = lax.axis_size("space")
    return lax.ppermute(rows_sent, "space", [(i, i + 1) for i in range(count - 1)])


def from_below(rows_sent):
    count = lax.axis_size("space")
    return lax.ppermute(rows_sent, "space", [(i + 1, i) for i in range(count - 1)])


def cols(field):
    width = field.shape[1]
    return pltpu.roll(field, width - 1, 1) - pltpu.roll(field, 1, 1)


def dot(a, b, dims=((1,), (0,))):
    return lax.dot_general(
        a, b, (dims, ((), ())), precision=HIGHEST, preferred_element_type=jnp.float32
    )


def prepare_kernel(
    state_ref, depth_ref, cot_ref, tail_ref, head_ref, out_ref, tail, head, cot, spread, sems
):
    own = state_ref.shape[1]
    groups, sites, part = spread.shape
    copies = []

    def send(source, target):
        copies.append(pltpu.make_async_copy(source, target, sems.at[len(copies)]))
        copies[-1].start()

    fields = len(STATE_EDGE)
    piece = sites // fields
    at = 0
    for f, n in STATE_EDGE:
        send(state_ref.at[f, pl.ds(own - n, n)], tail.at[pl.ds(at, n)])
        send(state_ref.at[f, pl.ds(0, n)], head.at[pl.ds(at, n)])
        at += n
    for edge in (tail, head):
        send(depth_ref, edge.at[at, pl.ds(0, own)])
    for f in range(fields):
        send(cot_ref.at[pl.ds(f * piece, piece)], cot.at[pl.ds(f * piece, piece)])
    for copy in copies[: 2 * fields + 2]:
        copy.wait()
    tail[at, own:] = tail[at, :own]
    head[at, own:] = head[at, :own]
    send(tail, tail_ref)
    send(head, head_ref)
    for f in range(fields):
        copies[2 * fields + 2 + f].wait()
        for j in range(groups):
            spread[j, f * piece : (f + 1) * piece] = cot[
                f * piece : (f + 1) * piece, j * part : (j + 1) * part
            ]
        send(spread.at[:, pl.ds(f * piece, piece)], out_ref.at[:, pl.ds(f * piece, piece)])
    for copy in copies[3 * fields + 2 :]:
        copy.wait()


def padded_rows(edges, size, own_row, above, below):
    start = {}
    at = 0
    for f, n in edges:
        start[f] = (at, n)
        at += n * size

    def row(f, p, own_rows):
        first, n = start[f]
        if p < HALO:
            return above(first + (p - (HALO - n)) * size)
        if p < HALO + own_rows:
            return own_row(f, p - HALO)
        return below(first + (p - HALO - own_rows) * size)

    return row, at


def forward_kernel(
    inside_ref, state_ref, depth_ref, above_ref, below_ref, index_ref,
    out_ref, observed_ref, east1_ref, north1_ref, east2_ref, north2_ref,
    e1, n1, h1, n2, h2, e2, depth, spread, sems,
):
    own, size, width = east1_ref.shape
    groups = spread.shape[0]
    part = width // groups
    low, high = HALO, HALO + own
    row, at = padded_rows(
        STATE_EDGE,
        1,
        lambda f, r: state_ref[f, r],
        lambda i: above_ref[i],
        lambda i: below_ref[i],
    )
    row = functools.partial(row, own_rows=own)
    depth[:HALO] = above_ref[at, own - HALO : own]
    depth[low:high] = depth_ref[...]
    depth[high:] = below_ref[at, :HALO]

    def d(p):
        return depth[p : p + 1]

    for p in range(low - 3, high + 3):
        n1[p] = row(2, p) - WAVE_COEF * (row(0, p + 1) - row(0, p - 1)) - SPIN_COEF * row(1, p)
    for p in range(low - 2, high + 2):
        new_east = row(1, p) - WAVE_COEF * cols(row(0, p)) + SPIN_COEF * row(2, p)
        e1[p] = new_east
        flow = cols(d(p) * new_east) + (d(p + 1) * n1[p + 1] - d(p - 1) * n1[p - 1])
        h1[p] = (row(0, p) - WAVE_COEF * flow) * inside_ref[p]
    copies = []

    def send(source, target):
        copies.append(pltpu.make_async_copy(source, target, sems.at[len(copies)]))
        copies[-1].start()

    send(e1.at[pl.ds(low, own)], east1_ref)
    send(n1.at[pl.ds(low, own)], north1_ref)
    for p in range(low - 1, high + 1):
        n2[p] = n1[p] - WAVE_COEF * (h1[p + 1] - h1[p - 1]) - SPIN_COEF * e1[p]
    for p in range(low, high):
        r = p - low
        new_east = e1[p] - WAVE_COEF * cols(h1[p]) + SPIN_COEF * n1[p]
        flow = cols(d(p) * new_east) + (d(p + 1) * n2[p + 1] - d(p - 1) * n2[p - 1])
        new_height = h1[p] - WAVE_COEF * flow
        new_north = n2[p]
        h2[r] = new_height
        e2[r] = new_east
        for f, field in enumerate((new_height, new_east, new_north)):
            for j in range(groups):
                spread[j, f * own + r] = field[:, j * part : (j + 1) * part]
    send(spread, out_ref)
    send(e2, east2_ref)
    send(n2.at[pl.ds(low, own)], north2_ref)
    pairs, lanes = index_ref.shape
    many = 2 * groups * size
    sub = lax.broadcasted_iota(jnp.int32, (part, lanes), 0)
    source = lax.broadcasted_iota(jnp.int32, (many, lanes), 0) // size
    target = lax.broadcasted_iota(jnp.int32, (many, lanes), 1) // (lanes // 2 // groups)
    for q in range(pairs):
        index = index_ref[q : q + 1].astype(jnp.int32)
        hit = (sub == index).astype(jnp.float32)
        stacked = jnp.concatenate(
            [h2[q + h * pairs, :, j * part : (j + 1) * part] for h in range(2) for j in range(groups)],
            axis=0,
        )
        seen = jnp.where(source == target, dot(stacked, hit), 0.0)
        observed_ref[q] = seen.reshape(2 * groups, size, lanes).sum(0)
    for copy in copies:
        copy.wait()


def backward_kernel(
    inside_ref, back_ref, above_ref, below_ref, seen_ref, depth_ref,
    east1_ref, north1_ref, east2_ref, north2_ref,
    depth_grad_ref, height_ref, east_ref, north_ref,
    h2, h1, e1, n1, nt,
):
    own, size, width = east1_ref.shape
    groups = back_ref.shape[0]
    low, high = HALO, HALO + own
    wide = lambda ref, at: jnp.concatenate([ref[j, at] for j in range(groups)], axis=1)
    row, _ = padded_rows(
        ADJOINT_EDGE,
        size,
        lambda f, r: wide(back_ref, f * own + r),
        lambda i: wide(above_ref, slice(i, i + size)),
        lambda i: wide(below_ref, slice(i, i + size)),
    )
    row = functools.partial(row, own_rows=own)

    def d(p):
        return depth_ref[p : p + 1]

    for p in range(0, high + HALO):
        h2[p] = row(0, p) + seen_ref[p]
    for p in range(low - 3, high + 3):
        along = WAVE_COEF * (h2[p + 1] - h2[p - 1])
        nt[p] = row(2, p) + d(p) * along
    for p in range(low - 2, high + 2):
        across = WAVE_COEF * cols(h2[p])
        total = row(1, p) + d(p) * across
        h1[p] = (h2[p] + WAVE_COEF * (cols(total) + (nt[p + 1] - nt[p - 1]))) * inside_ref[p]
        if low - 1 <= p < high + 1:
            n1[p] = nt[p] + SPIN_COEF * total
        if low <= p < high:
            r = p - low
            e1[p] = total - SPIN_COEF * nt[p]
            along = WAVE_COEF * (h2[p + 1] - h2[p - 1])
            depth_grad_ref[r : r + 1] = jnp.sum(
                east2_ref[r] * across + north2_ref[r] * along, axis=0, keepdims=True
            )
    for p in range(low - 1, high + 1):
        along = WAVE_COEF * (h1[p + 1] - h1[p - 1])
        nt[p] = n1[p] + d(p) * along
    height_ref[...] = h1[low - 1 : high + 1]
    for p in range(low, high):
        r = p - low
        across = WAVE_COEF * cols(h1[p])
        along = WAVE_COEF * (h1[p + 1] - h1[p - 1])
        east_ref[r] = e1[p] + d(p) * across
        depth_grad_ref[r : r + 1] += jnp.sum(
            east1_ref[r] * across + north1_ref[r] * along, axis=0, keepdims=True
        )
    north_ref[...] = nt[low - 1 : high + 1]


def finish_kernel(height_ref, east_ref, north_ref, state_grad_ref):
    own = east_ref.shape[0]
    for r in range(own):
        total, north = east_ref[r], north_ref[r + 1]
        state_grad_ref[0, r] = height_ref[r + 1] + WAVE_COEF * (
            cols(total) + (north_ref[r + 2] - north_ref[r])
        )
        state_grad_ref[1, r] = total - SPIN_COEF * north
        state_grad_ref[2, r] = north + SPIN_COEF * total


def gram_kernel(place_ref, params_ref, *refs):
    *observed_refs, scaled_ref, extra_ref, gram_ref, observed_ref, sems = refs
    groups, pairs, size, lanes = observed_ref.shape
    copies = []
    for d, ref in enumerate(observed_refs):
        there = observed_ref.at[lax.rem(place_ref[0] + groups - d, groups)]
        copies.append(pltpu.make_async_copy(ref, there, sems.at[d]))
        copies[-1].start()
    for copy in copies:
        copy.wait()
    members = groups * size
    gram = jnp.zeros((members, members), jnp.float32)
    proj = jnp.zeros((8, members), jnp.float32)
    for q in range(pairs):
        seen = observed_ref[:, q].reshape(members, lanes)
        mean = jnp.mean(seen, axis=0, keepdims=True)
        value, var = params_ref[1, q : q + 1], params_ref[2, q : q + 1]
        inv_sd = 1.0 / jnp.sqrt(var)
        obs_scale = 1.0 / jnp.sqrt(var * (members - 1))
        scaled = (seen - mean) * obs_scale
        innovation = (value - mean) * inv_sd
        scaled_ref[q] = scaled
        extra_ref[q] = jnp.concatenate(
            [innovation, obs_scale, inv_sd, params_ref[0, q : q + 1]]
            + [jnp.zeros((4, lanes), jnp.float32)],
            axis=0,
        )
        gram += dot(scaled, scaled, ((1,), (1,)))
        lead = jnp.concatenate([innovation, jnp.zeros((7, lanes), jnp.float32)], axis=0)
        proj += dot(lead, scaled, ((1,), (1,)))
    gram_ref[:members] = gram
    gram_ref[members:] = proj


def factor_kernel(gram_ref, inverse_ref, mixing_ref, mean_ref):
    members = inverse_ref.shape[0]
    step = 8
    blocks = members // step
    lane = lax.broadcasted_iota(jnp.int32, (step, members), 1)
    sub = lax.broadcasted_iota(jnp.int32, (step, members), 0)
    row_lane = lane[:1]
    body = [
        gram_ref[i * step : (i + 1) * step] + (lane == sub + i * step).astype(jnp.float32)
        for i in range(blocks)
    ]
    for k in range(0, members, 2):
        i0, s = divmod(k, step)
        row0, row1 = body[i0][s : s + 1], body[i0][s + 1 : s + 2]
        a, b, c = row0[:, k : k + 1], row0[:, k + 1 : k + 2], row1[:, k + 1 : k + 2]
        over_a = 1.0 / a
        over_c = a * (1.0 / (a * c - b * b))
        ratio = b * over_a
        first, second = row_lane == k, row_lane == k + 1
        row0 = jnp.where(first, 1.0, jnp.where(second, 0.0, row0))
        row1 = jnp.where(second, 1.0, jnp.where(first, 0.0, row1)) - ratio * row0
        inverse_ref[k : k + 1] = jnp.where(row_lane <= k, row0 * jnp.sqrt(over_a), 0.0)
        inverse_ref[k + 1 : k + 2] = jnp.where(row_lane <= k + 1, row1 * jnp.sqrt(over_c), 0.0)
        if k + 2 == members:
            break
        turned1 = row1 * over_c
        turned0 = row0 * over_a - ratio * turned1
        used = (lane == k) | (lane == k + 1)
        for i in range(i0, blocks):
            if i == i0 and s + 2 == step:
                continue
            factor0 = jnp.broadcast_to(body[i][:, k : k + 1], (step, members))
            factor1 = jnp.broadcast_to(body[i][:, k + 1 : k + 2], (step, members))
            update = jnp.where(used, 0.0, body[i]) - factor0 * turned0 - factor1 * turned1
            body[i] = jnp.where(sub > s + 1, update, body[i]) if i == i0 else update
    inverse = inverse_ref[...]
    proj = gram_ref[members:]
    mean = dot(dot(proj, inverse, ((1,), (1,))), inverse)
    mean_ref[...] = mean
    root = math.sqrt(members - 1)
    turned = inverse + mean[:1] / root
    turned = turned - jnp.mean(turned, axis=1, keepdims=True) + 1.0 / members
    mixing_ref[...] = turned.T


def pullback_kernel(place_ref, cross_ref, inverse_ref, mean_ref, *refs):
    *parts, grad, column = refs
    members = inverse_ref.shape[0]
    near = len(parts)
    groups = 2 * near
    size = members // groups
    inverse = inverse_ref[...]
    cross = cross_ref[...]
    cross = cross - jnp.mean(cross, axis=0, keepdims=True)
    first = lax.broadcasted_iota(jnp.int32, (8, members), 0) == 0
    ones = jnp.where(first, 1.0, 0.0)
    mean_grad = dot(ones, cross, ((1,), (1,))) / math.sqrt(members - 1)
    proj_grad = dot(dot(mean_grad, inverse, ((1,), (1,))), inverse)
    product = dot(inverse, cross)
    row = lax.broadcasted_iota(jnp.int32, (members, members), 0)
    col = lax.broadcasted_iota(jnp.int32, (members, members), 1)
    upper = jnp.where(row < col, product, 0.0)
    mirrored = jnp.where(row == col, product, 0.0) + upper + upper.T
    inner_grad = dot(inverse.T, dot(mirrored, inverse))
    every = jnp.broadcast_to(proj_grad[:1], (members, members)).T
    outer = every * mean_ref[:1]
    gram_grad = -(inner_grad + outer + outer.T)
    grad[...] = gram_grad - jnp.mean(gram_grad, axis=0, keepdims=True)
    column[...] = every - jnp.mean(every, axis=0, keepdims=True)
    for j, part in enumerate(parts):
        for h in range(2):
            there = place_ref[0] ^ (j + h * near)
            rows_there = pl.ds(pl.multiple_of(there * size, size), size)
            part[h, :size] = grad[rows_there]
            part[h, size : 2 * size] = column[rows_there]
            part[h, 2 * size :] = proj_grad


def observe_kernel(*refs):
    near_ref, far_ref, obs_ref, seen_ref = refs
    tall, size, width = seen_ref.shape
    pairs, high, lanes = obs_ref.shape
    members = high - 8
    part = lanes
    groups = width // part
    whole = near_ref[...] + far_ref[...]
    own_grad, own_proj, proj_grad = whole[:size], whole[size : 2 * size], whole[2 * size :]
    lane = lax.broadcasted_iota(jnp.int32, (size, lanes), 1)
    sub = lax.broadcasted_iota(jnp.int32, (part, lanes), 0)
    block = lanes // 2 // groups
    for t in range(pairs):
        scaled = obs_ref[t, :members]
        innovation, obs_scale, inv_sd, index = (
            obs_ref[t, members + i : members + i + 1] for i in range(4)
        )
        obs_grad = (dot(own_grad, scaled) + own_proj * innovation) * obs_scale
        obs_grad = obs_grad - dot(proj_grad, scaled)[:1] * inv_sd / members
        apart = jnp.concatenate(
            [jnp.where(lane // block == i, obs_grad, 0.0) for i in range(2 * groups)], axis=0
        )
        hit = (sub == index.astype(jnp.int32)).astype(jnp.float32)
        put = dot(apart, hit, ((1,), (1,)))
        for h in range(2):
            for j in range(groups):
                at = (h * groups + j) * size
                seen_ref[t + h * pairs, :, j * part : (j + 1) * part] = put[at : at + size]


def cross_kernel(state_ref, cot_ref, out_ref, state, sems):
    groups, sites, size, part = state.shape
    members = groups * size
    pieces = sems.shape[0]
    piece = sites // pieces
    copies = []
    for i in range(pieces):
        now = pl.ds(i * piece, piece)
        copies.append(pltpu.make_async_copy(state_ref.at[:, now], state.at[:, now], sems.at[i]))
        copies[-1].start()
    total = jnp.zeros((members, members), jnp.float32)
    for at in range(0, sites, 2):
        if at % piece == 0:
            copies[at // piece].wait()
        pick = lambda ref: jnp.concatenate(
            [ref[:, at + i].reshape(members, part) for i in range(2)], axis=1
        )
        total += dot(pick(state), pick(cot_ref), ((1,), (1,)))
    out_ref[...] = total


def mix_kernel(mixing_ref, cot_ref, out_ref, mixed_ref, sems):
    groups, sites, size, part = cot_ref.shape
    members = groups * size
    mixing = mixing_ref[...]
    copies = []
    pieces = sems.shape[0]
    for at in range(0, sites, 2):
        both = jnp.concatenate(
            [cot_ref[:, at + i].reshape(members, part) for i in range(2)], axis=1
        )
        mixed = dot(mixing, both)
        for i in range(2):
            mixed_ref[:, at + i] = mixed[:, i * part : (i + 1) * part].reshape(groups, size, part)
        if (at + 2) % (sites // pieces) == 0:
            done = pl.ds(at + 2 - sites // pieces, sites // pieces)
            copies.append(
                pltpu.make_async_copy(
                    mixed_ref.at[:, done], out_ref.at[:, done], sems.at[len(copies)]
                )
            )
            copies[-1].start()
    for copy in copies:
        copy.wait()


def per_device(initial_state, depth_field, obs_index, obs_value, obs_var, cotangent):
    groups = lax.axis_size("ens")
    ens_place = lax.axis_index("ens")
    space_place = lax.axis_index("space")
    fields, own_rows, own_members, width = initial_state.shape
    members = own_members * groups
    block_cols = width // groups
    tall = own_rows + 2 * HALO
    band = own_rows * lax.axis_size("space")
    sites = fields * own_rows
    half = own_rows // 2

    edge = (sum(n for _, n in STATE_EDGE) + 1, own_members, width)
    blocks = (groups, sites * own_members, block_cols)
    tail, head, cot_out = kernel_call(
        prepare_kernel,
        [edge, edge, blocks],
        [initial_state, depth_field, cotangent.reshape(-1, width)],
        [edge, edge, (sites * own_members, width), blocks],
        copies=4 * fields + 4,
        far_outs=(0, 1, 2),
        far_ins=(0, 1, 2),
        name="prepare",
    )
    packed = jnp.concatenate([obs_index.T.astype(jnp.float32), obs_value.T, obs_var.T])
    packed = jnp.pad(packed, ((0, 0), (0, block_cols - packed.shape[1])))
    params = gathered(packed, "ens")
    above, below = from_above(tail), from_below(head)
    cot_out, params = lax.optimization_barrier((cot_out, params))
    cot = exchanged(cot_out).reshape(groups, sites, own_members, block_cols)
    per_block = obs_index.shape[1]
    observations = per_block * groups
    params = params[:, :, :own_rows].reshape(groups, 3, per_block, 2, half)
    params = params.transpose(1, 4, 3, 0, 2).reshape(3, half, 2 * observations)

    row_number = space_place * own_rows - HALO + jnp.arange(tall)
    inside = ((row_number >= 0) & (row_number < band)).astype(jnp.float32)
    shape = (own_rows, own_members, width)
    padded = (tall, own_members, width)
    spread, observed, east1, north1, east2, north2 = kernel_call(
        forward_kernel,
        [(groups, sites, own_members, block_cols), (half, own_members, 2 * observations)]
        + [shape] * 4,
        [inside, initial_state, depth_field, above, below, params[0]],
        [padded] * 4 + [shape, shape, (tall, width), (groups, sites, own_members, block_cols)],
        copies=5,
        far_outs=(0, 2, 3, 4, 5),
        flops=10**8,
        name="forward",
    )
    observed = [observed] + [turned(observed, d) for d in range(1, groups)]
    spread, observed = lax.optimization_barrier((spread, observed))
    forecast = exchanged(spread)
    place = ens_place.astype(jnp.int32)[None]
    scaled, extra, gram = kernel_call(
        gram_kernel,
        [(half, members, 2 * observations), (half, 8, 2 * observations), (members + 8, members)],
        [place, params] + observed,
        [(groups,) + observed[0].shape],
        copies=groups,
        far_ins=tuple(range(2, 2 + groups)),
        flops=4 * 2 * 6 * members**3,
        name="gram",
    )
    gram = summed(gram)
    inverse, mixing, mean_weights = kernel_call(
        factor_kernel,
        [(members, members), (members, members), (8, members)],
        [gram],
        flops=10**9,
        name="factor",
    )
    scaled, extra, _ = lax.optimization_barrier((scaled, extra, gram))
    obs_pack = jnp.concatenate([scaled, extra], axis=1)
    left, right = obs_pack[..., :observations], obs_pack[..., observations:]
    obs_tall = jnp.concatenate(
        [
            jnp.concatenate([from_above(right), right], axis=-1),
            jnp.concatenate([left, from_below(left)], axis=-1),
        ]
    )

    (own_cross,) = kernel_call(
        cross_kernel,
        [(members, members)],
        [forecast, cot],
        [cot.shape],
        copies=fields,
        far_ins=(0,),
        flops=10**10,
        name="cross",
    )
    (mixed,) = kernel_call(
        mix_kernel,
        [cot.shape],
        [mixing, cot],
        [cot.shape],
        copies=fields,
        far_outs=(0,),
        flops=10**10,
        name="mix",
    )
    back = exchanged(mixed)
    cross, obs_tall = lax.optimization_barrier((summed(own_cross), obs_tall))

    near = groups // 2
    parts = kernel_call(
        pullback_kernel,
        [(2, 2 * own_members + 8, members)] * near,
        [place, cross, inverse, mean_weights],
        [(members, members)] * 2,
        flops=10**9,
        name="pullback",
    )
    parts = [parts[0]] + [crossed(parts[j], j) for j in range(1, near)]
    back, parts[1] = lax.optimization_barrier((back, parts[1]))
    whole = sum(parts[1:], parts[0])

    by_field = back.reshape(groups, fields, own_rows, own_members, block_cols)

    def adjoint_edge(take):
        parts = [
            by_field[:, f, take(n)].reshape(groups, -1, block_cols) for f, n in ADJOINT_EDGE
        ]
        return jnp.concatenate(parts, axis=1)

    adjoint_tail = adjoint_edge(lambda n: slice(own_rows - n, own_rows))
    adjoint_head = adjoint_edge(lambda n: slice(0, n))
    adjoint_above, adjoint_below = from_above(adjoint_tail), from_below(adjoint_head)
    whole, _, _ = lax.optimization_barrier((whole, adjoint_tail, adjoint_head))
    (seen,) = kernel_call(
        observe_kernel,
        [padded],
        [whole[0], crossed(whole[1], near), obs_tall],
        flops=10**9,
        name="observe",
    )
    depth_tall = jnp.concatenate([above[-1, half:own_rows], depth_field, below[-1, :half]])
    wider = (own_rows + 2, own_members, width)
    depth_grad, *remaining = kernel_call(
        backward_kernel,
        [(own_rows, width), wider, shape, wider],
        [
            inside, back, adjoint_above, adjoint_below, seen, depth_tall,
            east1, north1, east2, north2,
        ],
        [padded] * 5,
        flops=10**8,
        name="backward",
    )
    (state_grad,) = kernel_call(
        finish_kernel, [(fields,) + shape], remaining, flops=10**7, name="finish"
    )
    depth_grad = jnp.sum(gathered(depth_grad, "ens"), axis=0)
    return (state_grad, depth_grad)


def solution(mesh):
    in_specs = (
        P(None, "space", "ens", None),
        P("space", None),
        P("space", "ens"),
        P("space", "ens"),
        P("space", "ens"),
        P(None, "space", "ens", None),
    )
    out_specs = (P(None, "space", "ens", None), P("space", None))
    return jax.shard_map(
        per_device, mesh=mesh, in_specs=in_specs, out_specs=out_specs, check_vma=False
    )
```

```python
import functools
import math

import jax
import jax.numpy as jnp
from jax import lax
from jax.experimental import pallas as pl
from jax.experimental.pallas import tpu as pltpu
from jax.sharding import PartitionSpec as P

WAVE_COEF = 0.3
SPIN_COEF = 0.1
HALO = 4
HIGHEST = lax.Precision.HIGHEST
STATE_EDGE = ((0, 4), (1, 3), (2, 3))
VMEM = pl.BlockSpec(memory_space=pltpu.VMEM)
HBM = pl.BlockSpec(memory_space=pltpu.HBM)
SMEM = pl.BlockSpec(memory_space=pltpu.SMEM)


def kernel_call(body, outs, ins, scratch=(), copies=0, far_outs=(), far_ins=(), flops=0, name=None):
    moved = sum(math.prod(o) for o in outs) * 4 + sum(i.size for i in ins) * 4
    near = lambda i, a: SMEM if a.ndim == 1 else HBM if i in far_ins else VMEM
    made = lambda i, o: (pltpu.HBM if i in far_outs else jax.ShapeDtypeStruct)(o, jnp.float32)
    ins = [
        pltpu.with_memory_space_constraint(a, pltpu.HBM) if i in far_ins else a
        for i, a in enumerate(ins)
    ]
    return pl.pallas_call(
        body,
        out_shape=[made(i, o) for i, o in enumerate(outs)],
        in_specs=[near(i, a) for i, a in enumerate(ins)],
        out_specs=[HBM if i in far_outs else VMEM for i in range(len(outs))],
        scratch_shapes=[pltpu.VMEM(s, jnp.float32) for s in scratch]
        + ([pltpu.SemaphoreType.DMA((copies,))] if copies else []),
        compiler_params=pltpu.CompilerParams(vmem_limit_bytes=20 * 2**20),
        cost_estimate=pl.CostEstimate(flops=flops, bytes_accessed=moved, transcendentals=0),
        name=name,
    )(*ins)


def exchanged(blocks):
    return lax.all_to_all(blocks, "ens", 0, 0, tiled=False)


def gathered(block, axis):
    count = lax.axis_size(axis)
    copies = jnp.broadcast_to(block[None], (count,) + block.shape)
    return lax.all_to_all(copies, axis, 0, 0, tiled=False)


def turned(block, distance):
    count = lax.axis_size("ens")
    return lax.ppermute(block, "ens", [(i, (i + distance) % count) for i in range(count)])


def crossed(block, distance):
    count = lax.axis_size("ens")
    return lax.ppermute(block, "ens", [(i, i ^ distance) for i in range(count)])


def summed(block):
    count = lax.axis_size("space")

    def other(distance):
        return lax.ppermute(block, "space", [(i, i ^ distance) for i in range(count)])

    distance = 1
    while distance < count:
        if distance > 1 and 2 * distance < count:
            near, far, both = other(distance), other(2 * distance), other(3 * distance)
            block = (block + near) + (far + both)
            distance *= 4
        else:
            block = block + other(distance)
            distance *= 2
    return block


def from_above(rows_sent):
    count = lax.axis_size("space")
    return lax.ppermute(rows_sent, "space", [(i, i + 1) for i in range(count - 1)])


def from_below(rows_sent):
    count = lax.axis_size("space")
    return lax.ppermute(rows_sent, "space", [(i + 1, i) for i in range(count - 1)])


def cols(field):
    width = field.shape[1]
    return pltpu.roll(field, width - 1, 1) - pltpu.roll(field, 1, 1)


def dot(a, b, dims=((1,), (0,)), precision=HIGHEST):
    return lax.dot_general(
        a, b, (dims, ((), ())), precision=precision, preferred_element_type=jnp.float32
    )


def prepare_kernel(
    state_ref, depth_ref, cot_ref, tail_ref, head_ref, out_ref, tail, head, cot, spread, sems
):
    own = state_ref.shape[1]
    groups, sites, part = spread.shape
    copies = []

    def send(source, target):
        copies.append(pltpu.make_async_copy(source, target, sems.at[len(copies)]))
        copies[-1].start()

    fields = len(STATE_EDGE)
    piece = sites // fields
    at = 0
    for f, n in STATE_EDGE:
        send(state_ref.at[f, pl.ds(own - n, n)], tail.at[pl.ds(at, n)])
        send(state_ref.at[f, pl.ds(0, n)], head.at[pl.ds(at, n)])
        at += n
    for edge in (tail, head):
        send(depth_ref, edge.at[at, pl.ds(0, own)])
    for f in range(fields):
        send(cot_ref.at[pl.ds(f * piece, piece)], cot.at[pl.ds(f * piece, piece)])
    for copy in copies[: 2 * fields + 2]:
        copy.wait()
    tail[at, own:] = tail[at, :own]
    head[at, own:] = head[at, :own]
    send(tail, tail_ref)
    send(head, head_ref)
    for f in range(fields):
        copies[2 * fields + 2 + f].wait()
        for j in range(groups):
            spread[j, f * piece : (f + 1) * piece] = cot[
                f * piece : (f + 1) * piece, j * part : (j + 1) * part
            ]
        send(spread.at[:, pl.ds(f * piece, piece)], out_ref.at[:, pl.ds(f * piece, piece)])
    for copy in copies[3 * fields + 2 :]:
        copy.wait()


def padded_rows(edges, size, own_row, above, below):
    start = {}
    at = 0
    for f, n in edges:
        start[f] = (at, n)
        at += n * size

    def row(f, p, own_rows):
        first, n = start[f]
        if p < HALO:
            return above(first + (p - (HALO - n)) * size)
        if p < HALO + own_rows:
            return own_row(f, p - HALO)
        return below(first + (p - HALO - own_rows) * size)

    return row, at


def forward_kernel(
    inside_ref, state_ref, depth_ref, above_ref, below_ref, index_ref,
    out_ref, observed_ref, east1_ref, north1_ref, east2_ref, north2_ref,
    e1, n1, h1, n2, h2, e2, depth, spread, sems,
):
    own, size, width = east1_ref.shape
    groups = spread.shape[0]
    part = width // groups
    low, high = HALO, HALO + own
    row, at = padded_rows(
        STATE_EDGE,
        1,
        lambda f, r: state_ref[f, r],
        lambda i: above_ref[i],
        lambda i: below_ref[i],
    )
    row = functools.partial(row, own_rows=own)
    depth[:HALO] = above_ref[at, own - HALO : own]
    depth[low:high] = depth_ref[...]
    depth[high:] = below_ref[at, :HALO]

    def d(p):
        return depth[p : p + 1]

    for p in range(low - 3, high + 3):
        n1[p] = row(2, p) - WAVE_COEF * (row(0, p + 1) - row(0, p - 1)) - SPIN_COEF * row(1, p)
    for p in range(low - 2, high + 2):
        new_east = row(1, p) - WAVE_COEF * cols(row(0, p)) + SPIN_COEF * row(2, p)
        e1[p] = new_east
        flow = cols(d(p) * new_east) + (d(p + 1) * n1[p + 1] - d(p - 1) * n1[p - 1])
        h1[p] = (row(0, p) - WAVE_COEF * flow) * inside_ref[p]
    copies = []

    def send(source, target):
        copies.append(pltpu.make_async_copy(source, target, sems.at[len(copies)]))
        copies[-1].start()

    send(e1.at[pl.ds(low, own)], east1_ref)
    send(n1.at[pl.ds(low, own)], north1_ref)
    for p in range(low - 1, high + 1):
        n2[p] = n1[p] - WAVE_COEF * (h1[p + 1] - h1[p - 1]) - SPIN_COEF * e1[p]
    for p in range(low, high):
        r = p - low
        new_east = e1[p] - WAVE_COEF * cols(h1[p]) + SPIN_COEF * n1[p]
        flow = cols(d(p) * new_east) + (d(p + 1) * n2[p + 1] - d(p - 1) * n2[p - 1])
        new_height = h1[p] - WAVE_COEF * flow
        new_north = n2[p]
        h2[r] = new_height
        e2[r] = new_east
        for f, field in enumerate((new_height, new_east, new_north)):
            for j in range(groups):
                spread[j, f * own + r] = field[:, j * part : (j + 1) * part]
    send(spread, out_ref)
    send(e2, east2_ref)
    send(n2.at[pl.ds(low, own)], north2_ref)
    pairs, lanes = index_ref.shape
    many = 2 * groups * size
    sub = lax.broadcasted_iota(jnp.int32, (part, lanes), 0)
    source = lax.broadcasted_iota(jnp.int32, (many, lanes), 0) // size
    target = lax.broadcasted_iota(jnp.int32, (many, lanes), 1) // (lanes // 2 // groups)
    for q in range(pairs):
        index = index_ref[q : q + 1].astype(jnp.int32)
        hit = (sub == index).astype(jnp.float32)
        stacked = jnp.concatenate(
            [h2[q + h * pairs, :, j * part : (j + 1) * part] for h in range(2) for j in range(groups)],
            axis=0,
        )
        seen = jnp.where(source == target, dot(stacked, hit), 0.0)
        observed_ref[q] = seen.reshape(2 * groups, size, lanes).sum(0)
    for copy in copies:
        copy.wait()


def boundary(sign, h, e, n, d):
    def north(i):
        return n(i) + sign * WAVE_COEF * d(i) * (h(i - 1) - h(i + 1))

    def east(i):
        return e(i) + WAVE_COEF * d(i) * cols(h(i))

    near = east(1)
    later = h(1) + WAVE_COEF * (cols(near) - sign * north(2))
    beyond = h(2) + WAVE_COEF * (cols(east(2)) - sign * north(3))
    first = n(1) - sign * WAVE_COEF * d(1) * h(2)
    second = SPIN_COEF * near - sign * WAVE_COEF * d(1) * beyond
    return h(1), later, first, second


def edges_kernel(back_ref, depth_ref, tail_ref, head_ref):
    own = depth_ref.shape[0]
    groups = back_ref.shape[0]

    def field(f, at):
        return lambda i: jnp.concatenate(
            [back_ref[j, f * own + at(i)] for j in range(groups)], axis=1
        )

    for sign, out_ref, at in (
        (1.0, tail_ref, lambda i: own - i),
        (-1.0, head_ref, lambda i: i - 1),
    ):
        depth = lambda i: depth_ref[at(i) : at(i) + 1]
        found = boundary(sign, field(0, at), field(1, at), field(2, at), depth)
        for q, row in enumerate(found):
            out_ref[q] = row


def backward_kernel(
    inside_ref, back_ref, above_ref, below_ref, seen_ref, depth_ref,
    east1_ref, north1_ref, east2_ref, north2_ref,
    depth_grad_ref, height_ref, east_ref, north_ref,
    h2, h1, e1, n1, nt,
):
    own, size, width = east1_ref.shape
    groups = back_ref.shape[0]
    low, high = HALO, HALO + own
    none = jnp.zeros((size, width), jnp.float32)

    def row(f, p):
        at = f * own + p - low
        return jnp.concatenate([back_ref[j, at] for j in range(groups)], axis=1)

    def d(p):
        return depth_ref[p : p + 1]

    for p in range(low, high):
        h2[p] = row(0, p) + seen_ref[p]
    sides = (
        (1.0, above_ref, low, lambda i: low - i),
        (-1.0, below_ref, high - 1, lambda i: high - 1 + i),
    )
    for sign, sent_ref, edge, at in sides:
        seen = boundary(
            sign, lambda i: seen_ref[at(i)], lambda i: none, lambda i: none, lambda i: d(at(i))
        )
        out = at(1)
        h2[out] = sent_ref[0] + seen[0]
        h1[out] = sent_ref[1] + seen[1]
        nt[out] = sent_ref[2] + seen[2] + sign * WAVE_COEF * d(out) * h2[edge]
        n1[out] = sent_ref[3] + seen[3] + nt[out] * (1.0 - WAVE_COEF * WAVE_COEF * d(out))
    for p in range(low, high):
        nt[p] = row(2, p) + d(p) * WAVE_COEF * (h2[p + 1] - h2[p - 1])
    for p in range(low, high):
        r = p - low
        across = WAVE_COEF * cols(h2[p])
        along = WAVE_COEF * (h2[p + 1] - h2[p - 1])
        total = row(1, p) + d(p) * across
        h1[p] = h2[p] + WAVE_COEF * (cols(total) + (nt[p + 1] - nt[p - 1]))
        n1[p] = nt[p] + SPIN_COEF * total
        e1[p] = total - SPIN_COEF * nt[p]
        depth_grad_ref[r : r + 1] = jnp.sum(
            east2_ref[r] * across + north2_ref[r] * along, axis=0, keepdims=True
        )
    for sign, _, edge, at in sides:
        out = at(1)
        h1[out] = (h1[out] + sign * WAVE_COEF * nt[edge]) * inside_ref[out]
        nt[out] = n1[out] + sign * WAVE_COEF * d(out) * h1[edge]
    for p in range(low, high):
        nt[p] = n1[p] + d(p) * WAVE_COEF * (h1[p + 1] - h1[p - 1])
    height_ref[...] = h1[low - 1 : high + 1]
    for p in range(low, high):
        r = p - low
        across = WAVE_COEF * cols(h1[p])
        along = WAVE_COEF * (h1[p + 1] - h1[p - 1])
        east_ref[r] = e1[p] + d(p) * across
        depth_grad_ref[r : r + 1] += jnp.sum(
            east1_ref[r] * across + north1_ref[r] * along, axis=0, keepdims=True
        )
    north_ref[...] = nt[low - 1 : high + 1]


def finish_kernel(height_ref, east_ref, north_ref, state_grad_ref):
    own = east_ref.shape[0]
    for r in range(own):
        total, north = east_ref[r], north_ref[r + 1]
        state_grad_ref[0, r] = height_ref[r + 1] + WAVE_COEF * (
            cols(total) + (north_ref[r + 2] - north_ref[r])
        )
        state_grad_ref[1, r] = total - SPIN_COEF * north
        state_grad_ref[2, r] = north + SPIN_COEF * total


def gram_kernel(place_ref, params_ref, *refs):
    *observed_refs, scaled_ref, extra_ref, gram_ref, observed_ref, sems = refs
    groups, pairs, size, lanes = observed_ref.shape
    copies = []
    for d, ref in enumerate(observed_refs):
        there = observed_ref.at[lax.rem(place_ref[0] + groups - d, groups)]
        copies.append(pltpu.make_async_copy(ref, there, sems.at[d]))
        copies[-1].start()
    for copy in copies:
        copy.wait()
    members = groups * size
    gram = jnp.zeros((members, members), jnp.float32)
    proj = jnp.zeros((8, members), jnp.float32)
    for q in range(pairs):
        seen = observed_ref[:, q].reshape(members, lanes)
        mean = jnp.mean(seen, axis=0, keepdims=True)
        value, var = params_ref[1, q : q + 1], params_ref[2, q : q + 1]
        inv_sd = 1.0 / jnp.sqrt(var)
        obs_scale = 1.0 / jnp.sqrt(var * (members - 1))
        scaled = (seen - mean) * obs_scale
        innovation = (value - mean) * inv_sd
        scaled_ref[q] = scaled
        extra_ref[q] = jnp.concatenate(
            [innovation, obs_scale, inv_sd, params_ref[0, q : q + 1]]
            + [jnp.zeros((4, lanes), jnp.float32)],
            axis=0,
        )
        gram += dot(scaled, scaled, ((1,), (1,)))
        lead = jnp.concatenate([innovation, jnp.zeros((7, lanes), jnp.float32)], axis=0)
        proj += dot(lead, scaled, ((1,), (1,)))
    gram_ref[:members] = gram
    gram_ref[members:] = proj


def factor_kernel(gram_ref, inverse_ref, mixing_ref, mean_ref):
    members = inverse_ref.shape[0]
    step = 8
    blocks = members // step
    lane = lax.broadcasted_iota(jnp.int32, (step, members), 1)
    sub = lax.broadcasted_iota(jnp.int32, (step, members), 0)
    row_lane = lane[:1]
    body = [
        gram_ref[i * step : (i + 1) * step] + (lane == sub + i * step).astype(jnp.float32)
        for i in range(blocks)
    ]
    for k in range(0, members, 2):
        i0, s = divmod(k, step)
        row0, row1 = body[i0][s : s + 1], body[i0][s + 1 : s + 2]
        a, b, c = row0[:, k : k + 1], row0[:, k + 1 : k + 2], row1[:, k + 1 : k + 2]
        over_a = 1.0 / a
        over_c = a * (1.0 / (a * c - b * b))
        ratio = b * over_a
        first, second = row_lane == k, row_lane == k + 1
        row0 = jnp.where(first, 1.0, jnp.where(second, 0.0, row0))
        row1 = jnp.where(second, 1.0, jnp.where(first, 0.0, row1)) - ratio * row0
        inverse_ref[k : k + 1] = jnp.where(row_lane <= k, row0 * jnp.sqrt(over_a), 0.0)
        inverse_ref[k + 1 : k + 2] = jnp.where(row_lane <= k + 1, row1 * jnp.sqrt(over_c), 0.0)
        if k + 2 == members:
            break
        turned1 = row1 * over_c
        turned0 = row0 * over_a - ratio * turned1
        used = (lane == k) | (lane == k + 1)
        for i in range(i0, blocks):
            if i == i0 and s + 2 == step:
                continue
            factor0 = jnp.broadcast_to(body[i][:, k : k + 1], (step, members))
            factor1 = jnp.broadcast_to(body[i][:, k + 1 : k + 2], (step, members))
            update = jnp.where(used, 0.0, body[i]) - factor0 * turned0 - factor1 * turned1
            body[i] = jnp.where(sub > s + 1, update, body[i]) if i == i0 else update
    inverse = inverse_ref[...]
    proj = gram_ref[members:]
    mean = dot(dot(proj, inverse, ((1,), (1,))), inverse)
    mean_ref[...] = mean
    root = math.sqrt(members - 1)
    turned = inverse + mean[:1] / root
    turned = turned - jnp.mean(turned, axis=1, keepdims=True) + 1.0 / members
    mixing_ref[...] = turned.T


def pullback_kernel(place_ref, cross_ref, inverse_ref, mean_ref, *refs):
    *parts, grad, column = refs
    members = inverse_ref.shape[0]
    near = len(parts)
    groups = 2 * near
    size = members // groups
    inverse = inverse_ref[...]
    cross = cross_ref[...]
    cross = cross - jnp.mean(cross, axis=0, keepdims=True)
    first = lax.broadcasted_iota(jnp.int32, (8, members), 0) == 0
    ones = jnp.where(first, 1.0, 0.0)
    mean_grad = dot(ones, cross, ((1,), (1,))) / math.sqrt(members - 1)
    proj_grad = dot(dot(mean_grad, inverse, ((1,), (1,))), inverse)
    product = dot(inverse, cross)
    row = lax.broadcasted_iota(jnp.int32, (members, members), 0)
    col = lax.broadcasted_iota(jnp.int32, (members, members), 1)
    upper = jnp.where(row < col, product, 0.0)
    mirrored = jnp.where(row == col, product, 0.0) + upper + upper.T
    inner_grad = dot(inverse.T, dot(mirrored, inverse))
    every = jnp.broadcast_to(proj_grad[:1], (members, members)).T
    outer = every * mean_ref[:1]
    gram_grad = -(inner_grad + outer + outer.T)
    grad[...] = gram_grad - jnp.mean(gram_grad, axis=0, keepdims=True)
    column[...] = every - jnp.mean(every, axis=0, keepdims=True)
    for j, part in enumerate(parts):
        for h in range(2):
            there = place_ref[0] ^ (j + h * near)
            rows_there = pl.ds(pl.multiple_of(there * size, size), size)
            part[h, :size] = grad[rows_there]
            part[h, size : 2 * size] = column[rows_there]
            part[h, 2 * size :] = proj_grad


def observe_kernel(*refs):
    near_ref, far_ref, obs_ref, seen_ref = refs
    tall, size, width = seen_ref.shape
    pairs, high, lanes = obs_ref.shape
    members = high - 8
    part = lanes
    groups = width // part
    whole = near_ref[...] + far_ref[...]
    own_grad, own_proj, proj_grad = whole[:size], whole[size : 2 * size], whole[2 * size :]
    lane = lax.broadcasted_iota(jnp.int32, (size, lanes), 1)
    sub = lax.broadcasted_iota(jnp.int32, (part, lanes), 0)
    block = lanes // 2 // groups
    for t in range(pairs):
        scaled = obs_ref[t, :members]
        innovation, obs_scale, inv_sd, index = (
            obs_ref[t, members + i : members + i + 1] for i in range(4)
        )
        obs_grad = (dot(own_grad, scaled) + own_proj * innovation) * obs_scale
        obs_grad = obs_grad - dot(proj_grad, scaled)[:1] * inv_sd / members
        apart = jnp.concatenate(
            [jnp.where(lane // block == i, obs_grad, 0.0) for i in range(2 * groups)], axis=0
        )
        hit = (sub == index.astype(jnp.int32)).astype(jnp.float32)
        put = dot(apart, hit, ((1,), (1,)), lax.Precision.HIGH)
        for h in range(2):
            for j in range(groups):
                at = (h * groups + j) * size
                seen_ref[t + h * pairs, :, j * part : (j + 1) * part] = put[at : at + size]


def cross_kernel(state_ref, cot_ref, out_ref, state, sems):
    groups, sites, size, part = state.shape
    members = groups * size
    pieces = sems.shape[0]
    piece = sites // pieces
    copies = []
    for i in range(pieces):
        now = pl.ds(i * piece, piece)
        copies.append(pltpu.make_async_copy(state_ref.at[:, now], state.at[:, now], sems.at[i]))
        copies[-1].start()
    total = jnp.zeros((members, members), jnp.float32)
    for at in range(0, sites, 2):
        if at % piece == 0:
            copies[at // piece].wait()
        pick = lambda ref: jnp.concatenate(
            [ref[:, at + i].reshape(members, part) for i in range(2)], axis=1
        )
        total += dot(pick(state), pick(cot_ref), ((1,), (1,)))
    out_ref[...] = total


def mix_kernel(mixing_ref, cot_ref, out_ref, mixed_ref, sems):
    groups, sites, size, part = cot_ref.shape
    members = groups * size
    mixing = mixing_ref[...]
    copies = []
    pieces = sems.shape[0]
    for at in range(0, sites, 2):
        both = jnp.concatenate(
            [cot_ref[:, at + i].reshape(members, part) for i in range(2)], axis=1
        )
        mixed = dot(mixing, both)
        for i in range(2):
            mixed_ref[:, at + i] = mixed[:, i * part : (i + 1) * part].reshape(groups, size, part)
        if (at + 2) % (sites // pieces) == 0:
            done = pl.ds(at + 2 - sites // pieces, sites // pieces)
            copies.append(
                pltpu.make_async_copy(
                    mixed_ref.at[:, done], out_ref.at[:, done], sems.at[len(copies)]
                )
            )
            copies[-1].start()
    for copy in copies:
        copy.wait()


def per_device(initial_state, depth_field, obs_index, obs_value, obs_var, cotangent):
    groups = lax.axis_size("ens")
    ens_place = lax.axis_index("ens")
    space_place = lax.axis_index("space")
    fields, own_rows, own_members, width = initial_state.shape
    members = own_members * groups
    block_cols = width // groups
    tall = own_rows + 2 * HALO
    band = own_rows * lax.axis_size("space")
    sites = fields * own_rows
    half = own_rows // 2

    edge = (sum(n for _, n in STATE_EDGE) + 1, own_members, width)
    blocks = (groups, sites * own_members, block_cols)
    tail, head, cot_out = kernel_call(
        prepare_kernel,
        [edge, edge, blocks],
        [initial_state, depth_field, cotangent.reshape(-1, width)],
        [edge, edge, (sites * own_members, width), blocks],
        copies=4 * fields + 4,
        far_outs=(0, 1, 2),
        far_ins=(0, 1, 2),
        name="prepare",
    )
    packed = jnp.concatenate([obs_index.T.astype(jnp.float32), obs_value.T, obs_var.T])
    packed = jnp.pad(packed, ((0, 0), (0, block_cols - packed.shape[1])))
    params = gathered(packed, "ens")
    above, below = from_above(tail), from_below(head)
    cot_out, params = lax.optimization_barrier((cot_out, params))
    cot = exchanged(cot_out).reshape(groups, sites, own_members, block_cols)
    per_block = obs_index.shape[1]
    observations = per_block * groups
    params = params[:, :, :own_rows].reshape(groups, 3, per_block, 2, half)
    params = params.transpose(1, 4, 3, 0, 2).reshape(3, half, 2 * observations)

    row_number = space_place * own_rows - HALO + jnp.arange(tall)
    inside = ((row_number >= 0) & (row_number < band)).astype(jnp.float32)
    shape = (own_rows, own_members, width)
    padded = (tall, own_members, width)
    spread, observed, east1, north1, east2, north2 = kernel_call(
        forward_kernel,
        [(groups, sites, own_members, block_cols), (half, own_members, 2 * observations)]
        + [shape] * 4,
        [inside, initial_state, depth_field, above, below, params[0]],
        [padded] * 4 + [shape, shape, (tall, width), (groups, sites, own_members, block_cols)],
        copies=5,
        far_outs=(0, 2, 3, 4, 5),
        flops=10**8,
        name="forward",
    )
    observed = [observed] + [turned(observed, d) for d in range(1, groups)]
    spread, observed = lax.optimization_barrier((spread, observed))
    forecast = exchanged(spread)
    place = ens_place.astype(jnp.int32)[None]
    scaled, extra, gram = kernel_call(
        gram_kernel,
        [(half, members, 2 * observations), (half, 8, 2 * observations), (members + 8, members)],
        [place, params] + observed,
        [(groups,) + observed[0].shape],
        copies=groups,
        far_ins=tuple(range(2, 2 + groups)),
        flops=4 * 2 * 6 * members**3,
        name="gram",
    )
    gram = summed(gram)
    inverse, mixing, mean_weights = kernel_call(
        factor_kernel,
        [(members, members), (members, members), (8, members)],
        [gram],
        flops=10**9,
        name="factor",
    )
    scaled, extra, _ = lax.optimization_barrier((scaled, extra, gram))
    obs_pack = jnp.concatenate([scaled, extra], axis=1)
    left, right = obs_pack[..., :observations], obs_pack[..., observations:]
    obs_tall = jnp.concatenate(
        [
            jnp.concatenate([from_above(right), right], axis=-1),
            jnp.concatenate([left, from_below(left)], axis=-1),
        ]
    )

    (own_cross,) = kernel_call(
        cross_kernel,
        [(members, members)],
        [forecast, cot],
        [cot.shape],
        copies=fields,
        far_ins=(0,),
        flops=10**10,
        name="cross",
    )
    (mixed,) = kernel_call(
        mix_kernel,
        [cot.shape],
        [mixing, cot],
        [cot.shape],
        copies=fields,
        far_outs=(0,),
        flops=10**10,
        name="mix",
    )
    back = exchanged(mixed)
    cross, obs_tall = lax.optimization_barrier((summed(own_cross), obs_tall))

    near = groups // 2
    parts = kernel_call(
        pullback_kernel,
        [(2, 2 * own_members + 8, members)] * near,
        [place, cross, inverse, mean_weights],
        [(members, members)] * 2,
        flops=10**9,
        name="pullback",
    )
    parts = [parts[0]] + [crossed(parts[j], j) for j in range(1, near)]
    back, parts[1] = lax.optimization_barrier((back, parts[1]))
    whole = sum(parts[1:], parts[0])

    adjoint_tail, adjoint_head = kernel_call(
        edges_kernel,
        [(4, own_members, width)] * 2,
        [back, depth_field],
        flops=10**7,
        name="edges",
    )
    adjoint_above, adjoint_below = from_above(adjoint_tail), from_below(adjoint_head)
    whole, _, _ = lax.optimization_barrier((whole, adjoint_tail, adjoint_head))
    (seen,) = kernel_call(
        observe_kernel,
        [padded],
        [whole[0], crossed(whole[1], near), obs_tall],
        flops=10**11,
        name="observe",
    )
    depth_tall = jnp.concatenate([above[-1, half:own_rows], depth_field, below[-1, :half]])
    wider = (own_rows + 2, own_members, width)
    depth_grad, *remaining = kernel_call(
        backward_kernel,
        [(own_rows, width), wider, shape, wider],
        [
            inside, back, adjoint_above, adjoint_below, seen, depth_tall,
            east1, north1, east2, north2,
        ],
        [padded] * 5,
        flops=10**8,
        name="backward",
    )
    (state_grad,) = kernel_call(
        finish_kernel, [(fields,) + shape], remaining, flops=10**7, name="finish"
    )
    depth_grad = jnp.sum(gathered(depth_grad, "ens"), axis=0)
    return (state_grad, depth_grad)


def solution(mesh):
    in_specs = (
        P(None, "space", "ens", None),
        P("space", None),
        P("space", "ens"),
        P("space", "ens"),
        P("space", "ens"),
        P(None, "space", "ens", None),
    )
    out_specs = (P(None, "space", "ens", None), P("space", None))
    return jax.shard_map(
        per_device, mesh=mesh, in_specs=in_specs, out_specs=out_specs, check_vma=False
    )
```

```python
import functools
import math

import jax
import jax.numpy as jnp
from jax import lax
from jax.experimental import pallas as pl
from jax.experimental.pallas import tpu as pltpu
from jax.sharding import PartitionSpec as P

WAVE_COEF = 0.3
SPIN_COEF = 0.1
HALO = 4
HIGHEST = lax.Precision.HIGHEST
STATE_EDGE = ((0, 4), (1, 3), (2, 3))
VMEM = pl.BlockSpec(memory_space=pltpu.VMEM)
HBM = pl.BlockSpec(memory_space=pltpu.HBM)
SMEM = pl.BlockSpec(memory_space=pltpu.SMEM)


def kernel_call(body, outs, ins, scratch=(), copies=0, far_outs=(), far_ins=(), flops=0, name=None):
    moved = sum(math.prod(o) for o in outs) * 4 + sum(i.size for i in ins) * 4
    near = lambda i, a: SMEM if a.ndim == 1 else HBM if i in far_ins else VMEM
    made = lambda i, o: (pltpu.HBM if i in far_outs else jax.ShapeDtypeStruct)(o, jnp.float32)
    ins = [
        pltpu.with_memory_space_constraint(a, pltpu.HBM) if i in far_ins else a
        for i, a in enumerate(ins)
    ]
    return pl.pallas_call(
        body,
        out_shape=[made(i, o) for i, o in enumerate(outs)],
        in_specs=[near(i, a) for i, a in enumerate(ins)],
        out_specs=[HBM if i in far_outs else VMEM for i in range(len(outs))],
        scratch_shapes=[pltpu.VMEM(s, jnp.float32) for s in scratch]
        + ([pltpu.SemaphoreType.DMA((copies,))] if copies else []),
        compiler_params=pltpu.CompilerParams(vmem_limit_bytes=20 * 2**20),
        cost_estimate=pl.CostEstimate(flops=flops, bytes_accessed=moved, transcendentals=0),
        name=name,
    )(*ins)


def exchanged(blocks):
    return lax.all_to_all(blocks, "ens", 0, 0, tiled=False)


def gathered(block, axis):
    count = lax.axis_size(axis)
    copies = jnp.broadcast_to(block[None], (count,) + block.shape)
    return lax.all_to_all(copies, axis, 0, 0, tiled=False)


def turned(block, distance):
    count = lax.axis_size("ens")
    return lax.ppermute(block, "ens", [(i, (i + distance) % count) for i in range(count)])


def crossed(block, distance):
    count = lax.axis_size("ens")
    return lax.ppermute(block, "ens", [(i, i ^ distance) for i in range(count)])


def summed(block):
    count = lax.axis_size("space")

    def other(distance):
        return lax.ppermute(block, "space", [(i, i ^ distance) for i in range(count)])

    distance = 1
    while distance < count:
        if distance > 1 and 2 * distance < count:
            near, far, both = other(distance), other(2 * distance), other(3 * distance)
            block = (block + near) + (far + both)
            distance *= 4
        else:
            block = block + other(distance)
            distance *= 2
    return block


def from_above(rows_sent):
    count = lax.axis_size("space")
    return lax.ppermute(rows_sent, "space", [(i, i + 1) for i in range(count - 1)])


def from_below(rows_sent):
    count = lax.axis_size("space")
    return lax.ppermute(rows_sent, "space", [(i + 1, i) for i in range(count - 1)])


def cols(field):
    width = field.shape[1]
    return pltpu.roll(field, width - 1, 1) - pltpu.roll(field, 1, 1)


def dot(a, b, dims=((1,), (0,)), precision=HIGHEST):
    return lax.dot_general(
        a, b, (dims, ((), ())), precision=precision, preferred_element_type=jnp.float32
    )


def prepare_kernel(
    state_ref, depth_ref, cot_ref, tail_ref, head_ref, out_ref, tail, head, cot, spread, sems
):
    own = state_ref.shape[1]
    groups, sites, part = spread.shape
    copies = []

    def send(source, target):
        copies.append(pltpu.make_async_copy(source, target, sems.at[len(copies)]))
        copies[-1].start()

    fields = len(STATE_EDGE)
    piece = sites // fields
    at = 0
    for f, n in STATE_EDGE:
        send(state_ref.at[f, pl.ds(own - n, n)], tail.at[pl.ds(at, n)])
        send(state_ref.at[f, pl.ds(0, n)], head.at[pl.ds(at, n)])
        at += n
    for edge in (tail, head):
        send(depth_ref, edge.at[at, pl.ds(0, own)])
    for f in range(fields):
        send(cot_ref.at[pl.ds(f * piece, piece)], cot.at[pl.ds(f * piece, piece)])
    for copy in copies[: 2 * fields + 2]:
        copy.wait()
    tail[at, own:] = tail[at, :own]
    head[at, own:] = head[at, :own]
    send(tail, tail_ref)
    send(head, head_ref)
    for f in range(fields):
        copies[2 * fields + 2 + f].wait()
        for j in range(groups):
            spread[j, f * piece : (f + 1) * piece] = cot[
                f * piece : (f + 1) * piece, j * part : (j + 1) * part
            ]
        send(spread.at[:, pl.ds(f * piece, piece)], out_ref.at[:, pl.ds(f * piece, piece)])
    for copy in copies[3 * fields + 2 :]:
        copy.wait()


def padded_rows(edges, size, own_row, above, below):
    start = {}
    at = 0
    for f, n in edges:
        start[f] = (at, n)
        at += n * size

    def row(f, p, own_rows):
        first, n = start[f]
        if p < HALO:
            return above(first + (p - (HALO - n)) * size)
        if p < HALO + own_rows:
            return own_row(f, p - HALO)
        return below(first + (p - HALO - own_rows) * size)

    return row, at


def forward_kernel(
    inside_ref, state_ref, depth_ref, above_ref, below_ref, index_ref,
    out_ref, observed_ref, east1_ref, north1_ref, east2_ref, north2_ref,
    e1, n1, h1, n2, h2, e2, depth, spread, sems,
):
    own, size, width = east1_ref.shape
    groups = spread.shape[0]
    part = width // groups
    low, high = HALO, HALO + own
    row, at = padded_rows(
        STATE_EDGE,
        1,
        lambda f, r: state_ref[f, r],
        lambda i: above_ref[i],
        lambda i: below_ref[i],
    )
    row = functools.partial(row, own_rows=own)
    depth[:HALO] = above_ref[at, own - HALO : own]
    depth[low:high] = depth_ref[...]
    depth[high:] = below_ref[at, :HALO]

    def d(p):
        return depth[p : p + 1]

    for p in range(low - 3, high + 3):
        n1[p] = row(2, p) - WAVE_COEF * (row(0, p + 1) - row(0, p - 1)) - SPIN_COEF * row(1, p)
    for p in range(low - 2, high + 2):
        new_east = row(1, p) - WAVE_COEF * cols(row(0, p)) + SPIN_COEF * row(2, p)
        e1[p] = new_east
        flow = cols(d(p) * new_east) + (d(p + 1) * n1[p + 1] - d(p - 1) * n1[p - 1])
        h1[p] = (row(0, p) - WAVE_COEF * flow) * inside_ref[p]
    copies = []

    def send(source, target):
        copies.append(pltpu.make_async_copy(source, target, sems.at[len(copies)]))
        copies[-1].start()

    send(e1.at[pl.ds(low, own)], east1_ref)
    send(n1.at[pl.ds(low, own)], north1_ref)
    for p in range(low - 1, high + 1):
        n2[p] = n1[p] - WAVE_COEF * (h1[p + 1] - h1[p - 1]) - SPIN_COEF * e1[p]
    for p in range(low, high):
        r = p - low
        new_east = e1[p] - WAVE_COEF * cols(h1[p]) + SPIN_COEF * n1[p]
        flow = cols(d(p) * new_east) + (d(p + 1) * n2[p + 1] - d(p - 1) * n2[p - 1])
        new_height = h1[p] - WAVE_COEF * flow
        new_north = n2[p]
        h2[r] = new_height
        e2[r] = new_east
        for f, field in enumerate((new_height, new_east, new_north)):
            for j in range(groups):
                spread[j, f * own + r] = field[:, j * part : (j + 1) * part]
    send(spread, out_ref)
    send(e2, east2_ref)
    send(n2.at[pl.ds(low, own)], north2_ref)
    pairs, lanes = index_ref.shape
    many = 2 * groups * size
    sub = lax.broadcasted_iota(jnp.int32, (part, lanes), 0)
    source = lax.broadcasted_iota(jnp.int32, (many, lanes), 0) // size
    target = lax.broadcasted_iota(jnp.int32, (many, lanes), 1) // (lanes // 2 // groups)
    for q in range(pairs):
        index = index_ref[q : q + 1].astype(jnp.int32)
        hit = (sub == index).astype(jnp.float32)
        stacked = jnp.concatenate(
            [h2[q + h * pairs, :, j * part : (j + 1) * part] for h in range(2) for j in range(groups)],
            axis=0,
        )
        seen = jnp.where(source == target, dot(stacked, hit), 0.0)
        observed_ref[q] = seen.reshape(2 * groups, size, lanes).sum(0)
    for copy in copies:
        copy.wait()


def boundary(sign, h, e, n, d):
    def north(i):
        return n(i) + sign * WAVE_COEF * d(i) * (h(i - 1) - h(i + 1))

    def east(i):
        return e(i) + WAVE_COEF * d(i) * cols(h(i))

    near = east(1)
    later = h(1) + WAVE_COEF * (cols(near) - sign * north(2))
    beyond = h(2) + WAVE_COEF * (cols(east(2)) - sign * north(3))
    first = n(1) - sign * WAVE_COEF * d(1) * h(2)
    second = SPIN_COEF * near - sign * WAVE_COEF * d(1) * beyond
    return h(1), later, first, second


def edges_kernel(back_ref, depth_ref, tail_ref, head_ref):
    own = depth_ref.shape[0]
    groups = back_ref.shape[0]

    def field(f, at):
        return lambda i: jnp.concatenate(
            [back_ref[j, f * own + at(i)] for j in range(groups)], axis=1
        )

    for sign, out_ref, at in (
        (1.0, tail_ref, lambda i: own - i),
        (-1.0, head_ref, lambda i: i - 1),
    ):
        depth = lambda i: depth_ref[at(i) : at(i) + 1]
        found = boundary(sign, field(0, at), field(1, at), field(2, at), depth)
        for q, row in enumerate(found):
            out_ref[q] = row


def backward_kernel(
    inside_ref, back_ref, above_ref, below_ref, seen_ref, depth_ref,
    east1_ref, north1_ref, east2_ref, north2_ref,
    depth_grad_ref, height_ref, east_ref, north_ref,
    h2, h1, e1, n1, nt,
):
    own, size, width = east1_ref.shape
    groups = back_ref.shape[0]
    low, high = HALO, HALO + own
    none = jnp.zeros((size, width), jnp.float32)

    def row(f, p):
        at = f * own + p - low
        return jnp.concatenate([back_ref[j, at] for j in range(groups)], axis=1)

    def d(p):
        return depth_ref[p : p + 1]

    for p in range(low, high):
        h2[p] = row(0, p) + seen_ref[p]
    sides = (
        (1.0, above_ref, low, lambda i: low - i),
        (-1.0, below_ref, high - 1, lambda i: high - 1 + i),
    )
    for sign, sent_ref, edge, at in sides:
        seen = boundary(
            sign, lambda i: seen_ref[at(i)], lambda i: none, lambda i: none, lambda i: d(at(i))
        )
        out = at(1)
        h2[out] = sent_ref[0] + seen[0]
        h1[out] = sent_ref[1] + seen[1]
        nt[out] = sent_ref[2] + seen[2] + sign * WAVE_COEF * d(out) * h2[edge]
        n1[out] = sent_ref[3] + seen[3] + nt[out] * (1.0 - WAVE_COEF * WAVE_COEF * d(out))
    for p in range(low, high):
        nt[p] = row(2, p) + d(p) * WAVE_COEF * (h2[p + 1] - h2[p - 1])
    for p in range(low, high):
        r = p - low
        across = WAVE_COEF * cols(h2[p])
        along = WAVE_COEF * (h2[p + 1] - h2[p - 1])
        total = row(1, p) + d(p) * across
        h1[p] = h2[p] + WAVE_COEF * (cols(total) + (nt[p + 1] - nt[p - 1]))
        n1[p] = nt[p] + SPIN_COEF * total
        e1[p] = total - SPIN_COEF * nt[p]
        depth_grad_ref[r : r + 1] = jnp.sum(
            east2_ref[r] * across + north2_ref[r] * along, axis=0, keepdims=True
        )
    for sign, _, edge, at in sides:
        out = at(1)
        h1[out] = (h1[out] + sign * WAVE_COEF * nt[edge]) * inside_ref[out]
        nt[out] = n1[out] + sign * WAVE_COEF * d(out) * h1[edge]
    for p in range(low, high):
        nt[p] = n1[p] + d(p) * WAVE_COEF * (h1[p + 1] - h1[p - 1])
    height_ref[...] = h1[low - 1 : high + 1]
    for p in range(low, high):
        r = p - low
        across = WAVE_COEF * cols(h1[p])
        along = WAVE_COEF * (h1[p + 1] - h1[p - 1])
        east_ref[r] = e1[p] + d(p) * across
        depth_grad_ref[r : r + 1] += jnp.sum(
            east1_ref[r] * across + north1_ref[r] * along, axis=0, keepdims=True
        )
    north_ref[...] = nt[low - 1 : high + 1]


def finish_kernel(height_ref, east_ref, north_ref, state_grad_ref):
    own = east_ref.shape[0]
    for r in range(own):
        total, north = east_ref[r], north_ref[r + 1]
        state_grad_ref[0, r] = height_ref[r + 1] + WAVE_COEF * (
            cols(total) + (north_ref[r + 2] - north_ref[r])
        )
        state_grad_ref[1, r] = total - SPIN_COEF * north
        state_grad_ref[2, r] = north + SPIN_COEF * total


def gram_kernel(place_ref, params_ref, *refs):
    *observed_refs, scaled_ref, extra_ref, gram_ref, observed_ref, sems = refs
    groups, pairs, size, lanes = observed_ref.shape
    copies = []
    for d, ref in enumerate(observed_refs):
        there = observed_ref.at[lax.rem(place_ref[0] + groups - d, groups)]
        copies.append(pltpu.make_async_copy(ref, there, sems.at[d]))
        copies[-1].start()
    for copy in copies:
        copy.wait()
    members = groups * size
    gram = jnp.zeros((members, members), jnp.float32)
    proj = jnp.zeros((8, members), jnp.float32)
    for q in range(pairs):
        seen = observed_ref[:, q].reshape(members, lanes)
        mean = jnp.mean(seen, axis=0, keepdims=True)
        value, var = params_ref[1, q : q + 1], params_ref[2, q : q + 1]
        inv_sd = 1.0 / jnp.sqrt(var)
        obs_scale = 1.0 / jnp.sqrt(var * (members - 1))
        scaled = (seen - mean) * obs_scale
        innovation = (value - mean) * inv_sd
        scaled_ref[q] = scaled
        extra_ref[q] = jnp.concatenate(
            [innovation, obs_scale, inv_sd, params_ref[0, q : q + 1]]
            + [jnp.zeros((4, lanes), jnp.float32)],
            axis=0,
        )
        gram += dot(scaled, scaled, ((1,), (1,)))
        lead = jnp.concatenate([innovation, jnp.zeros((7, lanes), jnp.float32)], axis=0)
        proj += dot(lead, scaled, ((1,), (1,)))
    gram_ref[:members] = gram
    gram_ref[members:] = proj


def factor_kernel(gram_ref, inverse_ref, mixing_ref, mean_ref):
    members = inverse_ref.shape[0]
    step = 8
    blocks = members // step
    lane = lax.broadcasted_iota(jnp.int32, (step, members), 1)
    sub = lax.broadcasted_iota(jnp.int32, (step, members), 0)
    row_lane = lane[:1]
    body = [
        gram_ref[i * step : (i + 1) * step] + (lane == sub + i * step).astype(jnp.float32)
        for i in range(blocks)
    ]
    for k in range(0, members, 2):
        i0, s = divmod(k, step)
        row0, row1 = body[i0][s : s + 1], body[i0][s + 1 : s + 2]
        a, b, c = row0[:, k : k + 1], row0[:, k + 1 : k + 2], row1[:, k + 1 : k + 2]
        over_a = 1.0 / a
        over_c = a * (1.0 / (a * c - b * b))
        ratio = b * over_a
        first, second = row_lane == k, row_lane == k + 1
        row0 = jnp.where(first, 1.0, jnp.where(second, 0.0, row0))
        row1 = jnp.where(second, 1.0, jnp.where(first, 0.0, row1)) - ratio * row0
        inverse_ref[k : k + 1] = jnp.where(row_lane <= k, row0 * jnp.sqrt(over_a), 0.0)
        inverse_ref[k + 1 : k + 2] = jnp.where(row_lane <= k + 1, row1 * jnp.sqrt(over_c), 0.0)
        if k + 2 == members:
            break
        turned1 = row1 * over_c
        turned0 = row0 * over_a - ratio * turned1
        used = (lane == k) | (lane == k + 1)
        for i in range(i0, blocks):
            if i == i0 and s + 2 == step:
                continue
            factor0 = jnp.broadcast_to(body[i][:, k : k + 1], (step, members))
            factor1 = jnp.broadcast_to(body[i][:, k + 1 : k + 2], (step, members))
            update = jnp.where(used, 0.0, body[i]) - factor0 * turned0 - factor1 * turned1
            body[i] = jnp.where(sub > s + 1, update, body[i]) if i == i0 else update
    inverse = inverse_ref[...]
    proj = gram_ref[members:]
    mean = dot(dot(proj, inverse, ((1,), (1,))), inverse)
    mean_ref[...] = mean
    root = math.sqrt(members - 1)
    turned = inverse + mean[:1] / root
    turned = turned - jnp.mean(turned, axis=1, keepdims=True) + 1.0 / members
    mixing_ref[...] = turned.T


def pullback_kernel(place_ref, cross_ref, inverse_ref, mean_ref, *refs):
    *parts, grad, column = refs
    members = inverse_ref.shape[0]
    near = len(parts)
    groups = 2 * near
    size = members // groups
    inverse = inverse_ref[...]
    cross = cross_ref[...]
    cross = cross - jnp.mean(cross, axis=0, keepdims=True)
    first = lax.broadcasted_iota(jnp.int32, (8, members), 0) == 0
    ones = jnp.where(first, 1.0, 0.0)
    mean_grad = dot(ones, cross, ((1,), (1,))) / math.sqrt(members - 1)
    proj_grad = dot(dot(mean_grad, inverse, ((1,), (1,))), inverse)
    product = dot(inverse, cross)
    row = lax.broadcasted_iota(jnp.int32, (members, members), 0)
    col = lax.broadcasted_iota(jnp.int32, (members, members), 1)
    upper = jnp.where(row < col, product, 0.0)
    mirrored = jnp.where(row == col, product, 0.0) + upper + upper.T
    inner_grad = dot(inverse.T, dot(mirrored, inverse))
    every = jnp.broadcast_to(proj_grad[:1], (members, members)).T
    outer = every * mean_ref[:1]
    gram_grad = -(inner_grad + outer + outer.T)
    grad[...] = gram_grad - jnp.mean(gram_grad, axis=0, keepdims=True)
    column[...] = every - jnp.mean(every, axis=0, keepdims=True)
    for j, part in enumerate(parts):
        for h in range(2):
            there = place_ref[0] ^ (j + h * near)
            rows_there = pl.ds(pl.multiple_of(there * size, size), size)
            part[h, :size] = grad[rows_there]
            part[h, size : 2 * size] = column[rows_there]
            part[h, 2 * size :] = proj_grad


def observe_kernel(*refs):
    near_ref, far_ref, obs_ref, seen_ref = refs
    tall, size, width = seen_ref.shape
    pairs, high, lanes = obs_ref.shape
    members = high - 8
    part = lanes
    groups = width // part
    whole = near_ref[...] + far_ref[...]
    own_grad, own_proj, proj_grad = whole[:size], whole[size : 2 * size], whole[2 * size :]
    lane = lax.broadcasted_iota(jnp.int32, (size, lanes), 1)
    sub = lax.broadcasted_iota(jnp.int32, (part, lanes), 0)
    block = lanes // 2 // groups
    for t in range(pairs):
        scaled = obs_ref[t, :members]
        innovation, obs_scale, inv_sd, index = (
            obs_ref[t, members + i : members + i + 1] for i in range(4)
        )
        obs_grad = (dot(own_grad, scaled) + own_proj * innovation) * obs_scale
        obs_grad = obs_grad - dot(proj_grad, scaled)[:1] * inv_sd / members
        apart = jnp.concatenate(
            [jnp.where(lane // block == i, obs_grad, 0.0) for i in range(2 * groups)], axis=0
        )
        hit = (sub == index.astype(jnp.int32)).astype(jnp.float32)
        put = dot(apart, hit, ((1,), (1,)), lax.Precision.HIGH)
        for h in range(2):
            for j in range(groups):
                at = (h * groups + j) * size
                seen_ref[t + h * pairs, :, j * part : (j + 1) * part] = put[at : at + size]


def cross_kernel(state_ref, cot_ref, out_ref, state, sems):
    groups, sites, size, part = state.shape
    members = groups * size
    pieces = sems.shape[0]
    piece = sites // pieces
    copies = []
    for i in range(pieces):
        now = pl.ds(i * piece, piece)
        copies.append(pltpu.make_async_copy(state_ref.at[:, now], state.at[:, now], sems.at[i]))
        copies[-1].start()
    total = jnp.zeros((members, members), jnp.float32)
    for at in range(0, sites, 2):
        if at % piece == 0:
            copies[at // piece].wait()
        pick = lambda ref: jnp.concatenate(
            [ref[:, at + i].reshape(members, part) for i in range(2)], axis=1
        )
        total += dot(pick(state), pick(cot_ref), ((1,), (1,)))
    out_ref[...] = total


def mix_kernel(mixing_ref, cot_ref, out_ref, mixed_ref, sems):
    groups, sites, size, part = cot_ref.shape
    members = groups * size
    mixing = mixing_ref[...]
    copies = []
    pieces = sems.shape[0]
    for at in range(0, sites, 2):
        both = jnp.concatenate(
            [cot_ref[:, at + i].reshape(members, part) for i in range(2)], axis=1
        )
        mixed = dot(mixing, both)
        for i in range(2):
            mixed_ref[:, at + i] = mixed[:, i * part : (i + 1) * part].reshape(groups, size, part)
        if (at + 2) % (sites // pieces) == 0:
            done = pl.ds(at + 2 - sites // pieces, sites // pieces)
            copies.append(
                pltpu.make_async_copy(
                    mixed_ref.at[:, done], out_ref.at[:, done], sems.at[len(copies)]
                )
            )
            copies[-1].start()
    for copy in copies:
        copy.wait()


def per_device(initial_state, depth_field, obs_index, obs_value, obs_var, cotangent):
    groups = lax.axis_size("ens")
    ens_place = lax.axis_index("ens")
    space_place = lax.axis_index("space")
    fields, own_rows, own_members, width = initial_state.shape
    members = own_members * groups
    block_cols = width // groups
    tall = own_rows + 2 * HALO
    band = own_rows * lax.axis_size("space")
    sites = fields * own_rows
    half = own_rows // 2

    edge = (sum(n for _, n in STATE_EDGE) + 1, own_members, width)
    blocks = (groups, sites * own_members, block_cols)
    tail, head, cot_out = kernel_call(
        prepare_kernel,
        [edge, edge, blocks],
        [initial_state, depth_field, cotangent.reshape(-1, width)],
        [edge, edge, (sites * own_members, width), blocks],
        copies=4 * fields + 4,
        far_outs=(0, 1, 2),
        far_ins=(0, 1, 2),
        name="prepare",
    )
    packed = [
        jnp.broadcast_to(a.T[None], (groups,) + a.T.shape)
        for a in (obs_index.astype(jnp.float32), obs_value, obs_var)
    ]
    packed = jnp.concatenate(packed, axis=1)
    packed = jnp.pad(packed, ((0, 0), (0, 0), (0, block_cols - packed.shape[2])))
    params = exchanged(packed)
    above, below = from_above(tail), from_below(head)
    cot_out, params = lax.optimization_barrier((cot_out, params))
    cot = exchanged(cot_out).reshape(groups, sites, own_members, block_cols)
    per_block = obs_index.shape[1]
    observations = per_block * groups
    params = params[:, :, :own_rows].reshape(groups, 3, per_block, 2, half)
    params = params.transpose(1, 4, 3, 0, 2).reshape(3, half, 2 * observations)

    row_number = space_place * own_rows - HALO + jnp.arange(tall)
    inside = ((row_number >= 0) & (row_number < band)).astype(jnp.float32)
    shape = (own_rows, own_members, width)
    padded = (tall, own_members, width)
    spread, observed, east1, north1, east2, north2 = kernel_call(
        forward_kernel,
        [(groups, sites, own_members, block_cols), (half, own_members, 2 * observations)]
        + [shape] * 4,
        [inside, initial_state, depth_field, above, below, params[0]],
        [padded] * 4 + [shape, shape, (tall, width), (groups, sites, own_members, block_cols)],
        copies=5,
        far_outs=(0, 2, 3, 4, 5),
        flops=10**8,
        name="forward",
    )
    observed = [observed] + [turned(observed, d) for d in range(1, groups)]
    spread, observed = lax.optimization_barrier((spread, observed))
    forecast = exchanged(spread)
    place = ens_place.astype(jnp.int32)[None]
    scaled, extra, gram = kernel_call(
        gram_kernel,
        [(half, members, 2 * observations), (half, 8, 2 * observations), (members + 8, members)],
        [place, params] + observed,
        [(groups,) + observed[0].shape],
        copies=groups,
        far_ins=tuple(range(2, 2 + groups)),
        flops=4 * 2 * 6 * members**3,
        name="gram",
    )
    gram = summed(gram)
    inverse, mixing, mean_weights = kernel_call(
        factor_kernel,
        [(members, members), (members, members), (8, members)],
        [gram],
        flops=10**9,
        name="factor",
    )
    scaled, extra, _ = lax.optimization_barrier((scaled, extra, gram))
    obs_pack = jnp.concatenate([scaled, extra], axis=1)
    left, right = obs_pack[..., :observations], obs_pack[..., observations:]
    obs_tall = jnp.concatenate(
        [
            jnp.concatenate([from_above(right), right], axis=-1),
            jnp.concatenate([left, from_below(left)], axis=-1),
        ]
    )

    (own_cross,) = kernel_call(
        cross_kernel,
        [(members, members)],
        [forecast, cot],
        [cot.shape],
        copies=fields,
        far_ins=(0,),
        flops=10**10,
        name="cross",
    )
    (mixed,) = kernel_call(
        mix_kernel,
        [cot.shape],
        [mixing, cot],
        [cot.shape],
        copies=fields,
        far_outs=(0,),
        flops=10**10,
        name="mix",
    )
    back = exchanged(mixed)
    cross, obs_tall = lax.optimization_barrier((summed(own_cross), obs_tall))

    near = groups // 2
    parts = kernel_call(
        pullback_kernel,
        [(2, 2 * own_members + 8, members)] * near,
        [place, cross, inverse, mean_weights],
        [(members, members)] * 2,
        flops=10**9,
        name="pullback",
    )
    parts = [parts[0]] + [crossed(parts[j], j) for j in range(1, near)]
    back, parts[1] = lax.optimization_barrier((back, parts[1]))
    whole = sum(parts[1:], parts[0])

    adjoint_tail, adjoint_head = kernel_call(
        edges_kernel,
        [(4, own_members, width)] * 2,
        [back, depth_field],
        flops=10**7,
        name="edges",
    )
    adjoint_above, adjoint_below = from_above(adjoint_tail), from_below(adjoint_head)
    whole, _, _ = lax.optimization_barrier((whole, adjoint_tail, adjoint_head))
    (seen,) = kernel_call(
        observe_kernel,
        [padded],
        [whole[0], crossed(whole[1], near), obs_tall],
        flops=10**11,
        name="observe",
    )
    depth_tall = jnp.concatenate([above[-1, half:own_rows], depth_field, below[-1, :half]])
    wider = (own_rows + 2, own_members, width)
    depth_grad, *remaining = kernel_call(
        backward_kernel,
        [(own_rows, width), wider, shape, wider],
        [
            inside, back, adjoint_above, adjoint_below, seen, depth_tall,
            east1, north1, east2, north2,
        ],
        [padded] * 5,
        flops=10**8,
        name="backward",
    )
    (state_grad,) = kernel_call(
        finish_kernel, [(fields,) + shape], remaining, flops=10**7, name="finish"
    )
    depth_grad = jnp.sum(gathered(depth_grad, "ens"), axis=0)
    return (state_grad, depth_grad)


def solution(mesh):
    in_specs = (
        P(None, "space", "ens", None),
        P("space", None),
        P("space", "ens"),
        P("space", "ens"),
        P("space", "ens"),
        P(None, "space", "ens", None),
    )
    out_specs = (P(None, "space", "ens", None), P("space", None))
    return jax.shard_map(
        per_device, mesh=mesh, in_specs=in_specs, out_specs=out_specs, check_vma=False
    )
```
